32 devices in a mesh: grp: 2 (over y), wide: 8 (over z, x), narrow: 2 (over core).
Axes of the slice: x: 2, y: 2, z: 4, core: 2. Of those that a mesh axis runs over, the one named last changes fastest.
Arguments:
- inputs: bfloat16 [1024, 28672], P(('grp', 'wide'), 'narrow'), parts along dimension 0, may hold values from -6 to 6
- deltas: bfloat16 [1024, 8192], P('grp', 'wide'), parts along dimension 0, may hold values from -0.375 to 0.375
- basis_in: bfloat16 [57344, 14336], P(('grp', 'narrow'), 'wide'), parts along dimension 0, may hold values from -0.03125 to 0.03125
- basis_out: bfloat16 [16384, 4096], P(('grp', 'wide'), 'narrow'), parts along dimension 0, may hold values from -0.0625 to 0.0625
Outputs:
- corrections: float32 [28672, 4096], P(('grp', 'wide'), 'narrow'), parts along dimension 0
The draws below stay inside these ranges and needn't reach their ends.
There are 2 independent parts, one for each index of `grp`. The reference program is written for one: setup_inputs(seed, part) draws one part's arguments, and reference() takes and returns one part's arrays. A program takes and returns all parts, laid end to end along the dimension named above; each array names one. Nothing has to cross between parts.
All inputs are finite; a program needn't handle non-finite values.
Results may differ from the reference program's by a relative error of at most 0.0041.
Values may be sent and summed in bfloat16 or wider, within the bound.
No kernel may reach another device: no remote copies, remote signals or barrier semaphores. Data moves between devices by JAX's collectives and lax.ppermute only.
A program may use at most 192 MiB of HBM per device.

```python
import jax
import jax.numpy as jnp
from jax import lax

DIN = 28672
DOUT = 8192
KA = 14336
KS = 4096
EX = 2
SEQ = 256
ROWS = 512


def level_of(own_key, dims, cuts, low, high):
    def one(position, parts):
        steps = jax.random.uniform(jax.random.fold_in(jax.random.fold_in(own_key, 6), position), (parts,), jnp.float32, low / len(cuts), high / len(cuts))
        return jnp.repeat(jnp.exp(steps), dims[position] // parts).reshape((-1,) + (1,) * (len(dims) - position - 1))

    loudness = one(*cuts[0])
    for cut in cuts[1:]:
        loudness = loudness * one(*cut)
    return loudness


def gaussian(own_key, dims, deviation, limit, pieces=(), held_as=jnp.bfloat16):
    factor_of = level_of(own_key, dims, pieces, -0.22, 0.18) if pieces else 1.0
    entries = jax.random.normal(own_key, dims, jnp.float32) * deviation * factor_of
    return jnp.minimum(jnp.maximum(entries, -limit), limit).astype(held_as)


def setup_inputs(seed: int = 0, part: int = 0) -> dict:
    seeds = jax.random.split(jax.random.key(seed), 5)
    part_splits = jax.random.split(jax.random.fold_in(seeds[4], part), 5)
    inputs = gaussian(part_splits[0], (ROWS, DIN), 1.0, 6.0, ((0, 8), (1, 2)))
    deltas = gaussian(part_splits[1], (ROWS, DOUT), SEQ ** -0.5, 0.375, ((1, 8),))
    basis_in = gaussian(part_splits[2], (DIN, KA), DIN ** -0.5, 0.03125, ((0, 2), (1, 8)))
    basis_out = gaussian(part_splits[3], (DOUT, KS), DOUT ** -0.5, 0.0625, ((0, 8), (1, 2)))
    return {"inputs": inputs, "deltas": deltas, "basis_in": basis_in, "basis_out": basis_out}


def reference(inputs, deltas, basis_in, basis_out):
    rotated_in = jnp.dot(inputs, basis_in, preferred_element_type=jnp.float32).astype(jnp.bfloat16)
    rotated_out = jnp.dot(deltas, basis_out, preferred_element_type=jnp.float32).astype(jnp.bfloat16)
    blocks_in = rotated_in.astype(jnp.float32).reshape(EX, SEQ, KA)
    blocks_out = rotated_out.astype(jnp.float32).reshape(EX, SEQ, KS)

    def accumulate(total, pair):
        left, right = pair
        grad = jnp.dot(left.T, right, precision=lax.Precision.HIGHEST, preferred_element_type=jnp.float32)
        return total + grad * grad, None

    total, unused = lax.scan(accumulate, jnp.zeros((KA, KS), jnp.float32), (blocks_in, blocks_out))
    return total / EX
```

```python
import functools

import jax
import jax.numpy as jnp
from jax import lax
from jax.experimental import pallas as pl
from jax.experimental.pallas import tpu as pltpu
from jax.sharding import PartitionSpec as P

EX = 2
LINE, PAIR = 4, 2
BF16, F32 = jnp.bfloat16, jnp.float32


def dot(a, b):
    return jnp.dot(a, b, preferred_element_type=F32)


def fit_kernel(order_ref, mine_ref, other_ref, out_ref, fit_ref, rot_ref):
    rows, blocks = mine_ref.shape[0], order_ref.shape[0]
    size, seq = rows // blocks, rows // EX
    for slot in range(blocks):
        here = pl.ds(slot * size, size)
        there = pl.ds(pl.multiple_of(order_ref[slot] * size, size), size)
        rot_ref[there, :] = mine_ref[here, :] + other_ref[here, :]
    total = None
    for e in range(EX):
        here = pl.ds(e * seq, seq)
        grad = lax.dot_general(
            rot_ref[here, :].astype(BF16),
            out_ref[here, :],
            (((0,), (0,)), ((), ())),
            preferred_element_type=F32,
        )
        total = grad * grad if total is None else total + grad * grad
    fit_ref[...] = total * (1.0 / EX)


def fit(order, mine, other, rotated_out):
    rows, ka = mine.shape
    ks = rotated_out.shape[1]
    tile = 256 if ka % 256 == 0 else ka
    return pl.pallas_call(
        fit_kernel,
        out_shape=jax.ShapeDtypeStruct((ka, ks), F32),
        grid_spec=pltpu.PrefetchScalarGridSpec(
            num_scalar_prefetch=1,
            grid=(ka // tile,),
            in_specs=[
                pl.BlockSpec((rows, tile), lambda i, o: (0, i)),
                pl.BlockSpec((rows, tile), lambda i, o: (0, i)),
                pl.BlockSpec((rows, ks), lambda i, o: (0, 0)),
            ],
            out_specs=pl.BlockSpec((tile, ks), lambda i, o: (i, 0)),
            scratch_shapes=[pltpu.VMEM((rows, tile), F32)],
        ),
        compiler_params=pltpu.CompilerParams(vmem_limit_bytes=48 << 20),
        cost_estimate=pl.CostEstimate(
            flops=2 * rows * ka * ks,
            bytes_accessed=8 * rows * ka + 2 * rows * ks + 4 * ka * ks,
            transcendentals=0,
        ),
        name="fit",
    )(order, mine, other, rotated_out)


def swap_narrow(a):
    return lax.ppermute(a, "narrow", [(0, 1), (1, 0)])


def general(wide, inputs, deltas, basis_in, basis_out):
    partial_in = dot(lax.all_gather(inputs, "wide", axis=0, tiled=True), basis_in)
    rotated_out = lax.psum(dot(deltas, basis_out), "wide").astype(BF16)
    order = jnp.arange(EX, dtype=jnp.int32)
    return fit(order, partial_in, swap_narrow(partial_in), rotated_out)


def pairs(step, where=lambda z: True):
    out = []
    for z in range(LINE):
        for x in range(PAIR):
            if where(z):
                tz, tx = step(z, x)
                out.append((z * PAIR + x, tz * PAIR + tx))
    return out


def corner(z):
    return z in (0, LINE - 1)


ENDS = pairs(lambda z, x: (z ^ 1, x))
TO_ENDS = pairs(lambda z, x: (z ^ 1, x), lambda z: not corner(z))
MIDDLE = pairs(lambda z, x: (3 - z, x), lambda z: not corner(z))
ACROSS = pairs(lambda z, x: (z, 1 - x))
ACROSS_ENDS = pairs(lambda z, x: (z, 1 - x), corner)


def gather(block, at_end):
    send = lambda a, perm: lax.ppermute(a, "wide", perm)
    pick = lambda a, b: jnp.where(at_end, a, b)
    a1 = send(block, ENDS)
    x1 = send(block, ACROSS)
    m1 = send(block, MIDDLE)
    m2 = send(a1, MIDDLE)
    a2 = send(pick(x1, m1), ENDS)
    x2 = send(pick(a1, m1), ACROSS)
    a3 = send(m2, TO_ENDS)
    x3 = send(pick(a2, m2), ACROSS)
    x4 = send(a3, ACROSS_ENDS)
    return jnp.concatenate(
        [block, a1, pick(a2, m1), pick(a3, m2), x1, pick(x2, a2), pick(x3, x2), pick(x4, x3)], axis=0
    )


def slots(w):
    z, x = w // PAIR, w % PAIR
    flip = jnp.where(z >= 2, 3, 0)
    end = (z == 0) | (z == LINE - 1)
    mine = [jnp.where(end, a, b) ^ flip for a, b in ((0, 1), (1, 0), (2, 2), (3, 3))]
    return jnp.stack([q * PAIR + x for q in mine] + [q * PAIR + 1 - x for q in mine]).astype(jnp.int32)


def scheduled(inputs, deltas, basis_in, basis_out):
    w = lax.axis_index("wide")
    z = w // PAIR
    at_end = (z == 0) | (z == LINE - 1)
    deep = inputs.shape[1]
    chunks = 4
    width = deep // chunks

    partial_out = dot(deltas, basis_out)
    mine_out = lax.psum_scatter(partial_out, "wide", scatter_dimension=0, tiled=True).astype(BF16)
    rotated_out = lax.all_gather(mine_out, "wide", axis=0, tiled=True)

    total = None
    for c in range(chunks):
        here = slice(c * width, (c + 1) * width)
        term = dot(gather(inputs[:, here], at_end), basis_in[here])
        total = term if total is None else total + term
    return fit(slots(w), total, swap_narrow(total), rotated_out)


def solution(mesh):
    wide = mesh.shape["wide"]
    local = scheduled if wide == LINE * PAIR else functools.partial(general, wide)
    return jax.shard_map(
        local,
        mesh=mesh,
        in_specs=(
            P(("grp", "wide"), "narrow"),
            P("grp", "wide"),
            P(("grp", "narrow"), "wide"),
            P(("grp", "wide"), "narrow"),
        ),
        out_specs=P(("grp", "wide"), "narrow"),
        check_vma=False,
    )
```

```python
import functools

import jax
import jax.numpy as jnp
from jax import lax
from jax.experimental import pallas as pl
from jax.experimental.pallas import tpu as pltpu
from jax.sharding import PartitionSpec as P

EX = 2
LINE, PAIR = 4, 2
BF16, F32 = jnp.bfloat16, jnp.float32


def dot(a, b):
    return jnp.dot(a, b, preferred_element_type=F32)


def fit_kernel(order_ref, mine_ref, other_ref, out_ref, fit_ref, rot_ref):
    rows, blocks = mine_ref.shape[0], order_ref.shape[0]
    size, seq = rows // blocks, rows // EX
    for slot in range(blocks):
        here = pl.ds(slot * size, size)
        there = pl.ds(pl.multiple_of(order_ref[slot] * size, size), size)
        rot_ref[there, :] = mine_ref[here, :] + other_ref[here, :]
    total = None
    for e in range(EX):
        here = pl.ds(e * seq, seq)
        grad = lax.dot_general(
            rot_ref[here, :].astype(BF16),
            out_ref[here, :],
            (((0,), (0,)), ((), ())),
            preferred_element_type=F32,
        )
        total = grad * grad if total is None else total + grad * grad
    fit_ref[...] = total * (1.0 / EX)


def fit(order, mine, other, rotated_out):
    rows, ka = mine.shape
    ks = rotated_out.shape[1]
    tile = 256 if ka % 256 == 0 else ka
    return pl.pallas_call(
        fit_kernel,
        out_shape=jax.ShapeDtypeStruct((ka, ks), F32),
        grid_spec=pltpu.PrefetchScalarGridSpec(
            num_scalar_prefetch=1,
            grid=(ka // tile,),
            in_specs=[
                pl.BlockSpec((rows, tile), lambda i, o: (0, i)),
                pl.BlockSpec((rows, tile), lambda i, o: (0, i)),
                pl.BlockSpec((rows, ks), lambda i, o: (0, 0)),
            ],
            out_specs=pl.BlockSpec((tile, ks), lambda i, o: (i, 0)),
            scratch_shapes=[pltpu.VMEM((rows, tile), F32)],
        ),
        compiler_params=pltpu.CompilerParams(vmem_limit_bytes=48 << 20),
        cost_estimate=pl.CostEstimate(
            flops=2 * rows * ka * ks,
            bytes_accessed=8 * rows * ka + 2 * rows * ks + 4 * ka * ks,
            transcendentals=0,
        ),
        name="fit",
    )(order, mine, other, rotated_out)


def swap_narrow(a):
    return lax.ppermute(a, "narrow", [(0, 1), (1, 0)])


def general(wide, inputs, deltas, basis_in, basis_out):
    partial_in = dot(lax.all_gather(inputs, "wide", axis=0, tiled=True), basis_in)
    rotated_out = lax.psum(dot(deltas, basis_out), "wide").astype(BF16)
    order = jnp.arange(EX, dtype=jnp.int32)
    return fit(order, partial_in, swap_narrow(partial_in), rotated_out)


def pairs(step, where=lambda z: True):
    out = []
    for z in range(LINE):
        for x in range(PAIR):
            if where(z):
                tz, tx = step(z, x)
                out.append((z * PAIR + x, tz * PAIR + tx))
    return out


def corner(z):
    return z in (0, LINE - 1)


ENDS = pairs(lambda z, x: (z ^ 1, x))
TO_ENDS = pairs(lambda z, x: (z ^ 1, x), lambda z: not corner(z))
MIDDLE = pairs(lambda z, x: (3 - z, x), lambda z: not corner(z))
ACROSS = pairs(lambda z, x: (z, 1 - x))
ACROSS_ENDS = pairs(lambda z, x: (z, 1 - x), corner)


def send(a, perm):
    return lax.ppermute(a, "wide", perm)


def stage(step, got, at_end):
    pick = lambda a, b: jnp.where(at_end, got[a], got[b])
    if step == 0:
        return {"a1": send(got["own"], ENDS), "x1": send(got["own"], ACROSS), "m1": send(got["own"], MIDDLE)}
    if step == 1:
        return {
            "m2": send(got["a1"], MIDDLE),
            "x2": send(pick("a1", "m1"), ACROSS),
            "a2": send(pick("x1", "m1"), ENDS),
        }
    if step == 2:
        return {"a3": send(got["m2"], TO_ENDS), "x3": send(pick("a2", "m2"), ACROSS)}
    return {"x4": send(got["a3"], ACROSS_ENDS)}


def assemble(got, at_end):
    pick = lambda a, b: jnp.where(at_end, got[a], got[b])
    return jnp.concatenate(
        [got["own"], got["a1"], pick("a2", "m1"), pick("a3", "m2"), got["x1"], pick("x2", "a2"), pick("x3", "x2"),
         pick("x4", "x3")], axis=0
    )


def slots(w):
    z, x = w // PAIR, w % PAIR
    flip = jnp.where(z >= 2, 3, 0)
    end = (z == 0) | (z == LINE - 1)
    mine = [jnp.where(end, a, b) ^ flip for a, b in ((0, 1), (1, 0), (2, 2), (3, 3))]
    return jnp.stack([q * PAIR + x for q in mine] + [q * PAIR + 1 - x for q in mine]).astype(jnp.int32)


def scheduled(inputs, deltas, basis_in, basis_out):
    w = lax.axis_index("wide")
    z = w // PAIR
    at_end = (z == 0) | (z == LINE - 1)
    deep = inputs.shape[1]
    chunks, steps, lag = 8, 4, 2
    width = deep // chunks

    def fence(names, arrays):
        return dict(zip(names, lax.optimization_barrier(tuple(arrays))))

    partial_out = dot(deltas, basis_out)
    sums = lax.psum_scatter(partial_out, "wide", scatter_dimension=0, tiled=True)
    rotated_out = None

    got = [{"own": inputs[:, c * width : (c + 1) * width]} for c in range(chunks)]
    fresh = {}
    total = None
    last = chunks + lag * (steps - 1)
    for slot in range(last + lag):
        names = fresh.get(slot - lag, [])
        if slot < chunks:
            names = names + [(slot, "own")]
        arrays = [got[c][n] for c, n in names]
        if total is not None:
            names, arrays = names + ["total"], arrays + [total]
        if slot == 9:
            names, arrays = names + ["sums"], arrays + [sums]
        if slot == 14:
            names, arrays = names + ["rotated_out"], arrays + [rotated_out]
        for name, value in fence(names, arrays).items():
            if name == "total":
                total = value
            elif name == "sums":
                rotated_out = lax.all_gather(value.astype(BF16), "wide", axis=0, tiled=True)
            elif name == "rotated_out":
                rotated_out = value
            else:
                got[name[0]][name[1]] = value
        fresh[slot] = []
        for step in range(steps):
            c = slot - lag * step
            if 0 <= c < chunks:
                new = stage(step, got[c], at_end)
                got[c].update(new)
                fresh[slot] += [(c, n) for n in new]
        c = slot - lag * steps
        if 0 <= c < chunks:
            term = dot(assemble(got[c], at_end), basis_in[c * width : (c + 1) * width])
            total = term if total is None else total + term
    return fit(slots(w), total, swap_narrow(total), rotated_out)


def solution(mesh):
    wide = mesh.shape["wide"]
    local = scheduled if wide == LINE * PAIR else functools.partial(general, wide)
    return jax.shard_map(
        local,
        mesh=mesh,
        in_specs=(
            P(("grp", "wide"), "narrow"),
            P("grp", "wide"),
            P(("grp", "narrow"), "wide"),
            P(("grp", "wide"), "narrow"),
        ),
        out_specs=P(("grp", "wide"), "narrow"),
        check_vma=False,
    )
```

```python
import jax
import jax.numpy as jnp
from jax import lax
from jax.experimental import pallas as pl
from jax.experimental.pallas import tpu as pltpu
from jax.sharding import Mesh
from jax.sharding import PartitionSpec as P

EX = 2
BF16, F32 = jnp.bfloat16, jnp.float32


def dot(a, b):
    return jnp.dot(a, b, preferred_element_type=F32)


def fit_kernel(order_ref, mine_ref, other_ref, out_ref, fit_ref, rot_ref):
    rows, blocks = mine_ref.shape[0], order_ref.shape[0]
    size, seq = rows // blocks, rows // EX
    for slot in range(blocks):
        here = pl.ds(slot * size, size)
        there = pl.ds(pl.multiple_of(order_ref[slot] * size, size), size)
        rot_ref[there, :] = mine_ref[here, :] + other_ref[here, :]
    total = None
    for e in range(EX):
        here = pl.ds(e * seq, seq)
        grad = lax.dot_general(
            rot_ref[here, :].astype(BF16),
            out_ref[here, :],
            (((0,), (0,)), ((), ())),
            preferred_element_type=F32,
        )
        total = grad * grad if total is None else total + grad * grad
    fit_ref[...] = total * (1.0 / EX)


def fit(order, mine, other, rotated_out):
    rows, ka = mine.shape
    ks = rotated_out.shape[1]
    tile = 256 if ka % 256 == 0 else ka
    return pl.pallas_call(
        fit_kernel,
        out_shape=jax.ShapeDtypeStruct((ka, ks), F32),
        grid_spec=pltpu.PrefetchScalarGridSpec(
            num_scalar_prefetch=1,
            grid=(ka // tile,),
            in_specs=[
                pl.BlockSpec((rows, tile), lambda i, o: (0, i)),
                pl.BlockSpec((rows, tile), lambda i, o: (0, i)),
                pl.BlockSpec((rows, ks), lambda i, o: (0, 0)),
            ],
            out_specs=pl.BlockSpec((tile, ks), lambda i, o: (i, 0)),
            scratch_shapes=[pltpu.VMEM((rows, tile), F32)],
        ),
        compiler_params=pltpu.CompilerParams(vmem_limit_bytes=48 << 20),
        cost_estimate=pl.CostEstimate(
            flops=2 * rows * ka * ks,
            bytes_accessed=8 * rows * ka + 2 * rows * ks + 4 * ka * ks,
            transcendentals=0,
        ),
        name="fit",
    )(order, mine, other, rotated_out)


def swap_narrow(a):
    return lax.ppermute(a, "narrow", [(0, 1), (1, 0)])


def rotate_kernel(*refs):
    mine_ref, other_ref, basis_ref, total_ref, sum_ref = refs if len(refs) == 5 else (*refs[:3], None, refs[3])
    half = mine_ref.shape[0]
    for at, ref in ((0, mine_ref), (half, other_ref)):
        here = pl.ds(at, half)
        term = dot(ref[...], basis_ref[...])
        sum_ref[here, :] = term if total_ref is None else total_ref[here, :] + term


def rotate(total, mine, other, basis, chunk):
    half, width = mine.shape
    ka = basis.shape[1]
    tile = 256 if ka % 256 == 0 else ka
    rows = pl.BlockSpec((half, width), lambda j: (0, 0))
    sums = pl.BlockSpec((2 * half, tile), lambda j: (0, j))
    arrays = [mine, other, basis] + ([] if total is None else [total])
    return pl.pallas_call(
        rotate_kernel,
        out_shape=jax.ShapeDtypeStruct((2 * half, ka), F32),
        grid=(ka // tile,),
        in_specs=[rows, rows, pl.BlockSpec((width, tile), lambda j: (chunk, j)), sums][: len(arrays)],
        out_specs=sums,
        input_output_aliases={} if total is None else {3: 0},
        compiler_params=pltpu.CompilerParams(vmem_limit_bytes=40 << 20),
        cost_estimate=pl.CostEstimate(
            flops=4 * half * width * ka, bytes_accessed=4 * half * width + 2 * width * ka + 16 * half * ka, transcendentals=0
        ),
        name="rotate",
    )(*arrays)


def general(inputs, deltas, basis_in, basis_out):
    wide = ("line", "pair")
    partial_in = dot(lax.all_gather(inputs, wide, axis=0, tiled=True), basis_in)
    rotated_out = lax.psum(dot(deltas, basis_out), wide).astype(BF16)
    order = jnp.arange(EX, dtype=jnp.int32)
    return fit(order, partial_in, swap_narrow(partial_in), rotated_out)


def swap_pair(a):
    return lax.ppermute(a, "pair", [(0, 1), (1, 0)])


def gather_line(a):
    return lax.all_gather(a, "line", axis=0, tiled=True)


CHUNKS = 8
PAIR_FIRST = (0, 1)
ORDER = (2, 3, 0, 4, 1, 5, 6, 7)


def scheduled(inputs, deltas, basis_in, basis_out):
    lines = lax.axis_size("line")
    x = lax.axis_index("pair")
    width = inputs.shape[1] // CHUNKS
    own = [inputs[:, c * width : (c + 1) * width] for c in range(CHUNKS)]

    partial_out = dot(deltas, basis_out)
    ks = partial_out.shape[1] // 2
    keep = lax.dynamic_slice_in_dim(partial_out, x * ks, ks, 1)
    give = lax.dynamic_slice_in_dim(partial_out, (1 - x) * ks, ks, 1)
    crossed = {c: swap_pair(own[c]) for c in PAIR_FIRST}
    sums = keep + swap_pair(give)

    mine, other, total, out = {}, {}, None, None
    for i, c in enumerate(ORDER):
        mine[c] = gather_line(own[c])
        if c in PAIR_FIRST:
            other[c] = gather_line(crossed[c])
        if i == 4:
            sums = lax.psum_scatter(sums, "line", scatter_dimension=0, tiled=True).astype(BF16)
        if i == 6:
            sums = gather_line(sums)
    for i, c in enumerate(ORDER):
        before = ORDER[i - 2] if i >= 2 else None
        held = [mine[c]] + ([other[before]] if i >= 2 else []) + ([total] if i >= 3 else [])
        held = lax.optimization_barrier(tuple(held))
        mine[c] = held[0]
        if i >= 2:
            other[before] = held[1]
        if i >= 3:
            total = held[2]
        if c not in PAIR_FIRST:
            other[c] = swap_pair(mine[c])
        if i >= 2:
            total = rotate(total, mine[before], other[before], basis_in, before)
    sums, total = lax.optimization_barrier((sums, total))
    far = swap_pair(sums)
    for c in ORDER[-2:]:
        total = rotate(total, mine[c], other[c], basis_in, c)
    rotated_out = jnp.where(x == 0, jnp.concatenate([sums, far], 1), jnp.concatenate([far, sums], 1))
    order = jnp.concatenate([2 * jnp.arange(lines) + x, 2 * jnp.arange(lines) + 1 - x]).astype(jnp.int32)
    return fit(order, total, swap_narrow(total), rotated_out)


def solution(mesh):
    grp, wide, narrow = (mesh.shape[name] for name in ("grp", "wide", "narrow"))
    devices = mesh.devices.reshape(grp, wide, narrow)
    columns = len({getattr(d, "coords", (i % 2,))[0] for i, d in enumerate(devices[0, :, 0])})
    grid = Mesh(devices.reshape(grp, wide // columns, columns, narrow), ("grp", "line", "pair", "narrow"))
    wide = ("line", "pair")
    return jax.shard_map(
        scheduled if columns == 2 else general,
        mesh=grid,
        in_specs=(
            P(("grp", *wide), "narrow"),
            P("grp", wide),
            P(("grp", "narrow"), wide),
            P(("grp", *wide), "narrow"),
        ),
        out_specs=P(("grp", *wide), "narrow"),
        check_vma=False,
    )
```

```python
import jax
import jax.numpy as jnp
from jax import lax
from jax.experimental import pallas as pl
from jax.experimental.pallas import tpu as pltpu
from jax.sharding import PartitionSpec as P

EX = 2
LINE, PAIR = 4, 2
DEEP = 1024
BF16, F32 = jnp.bfloat16, jnp.float32


def dot(a, b):
    return jnp.dot(a, b, preferred_element_type=F32)


def fit_kernel(order_ref, flip_ref, *refs):
    *sum_refs, out_ref, fit_ref, rot_ref = refs
    rows, blocks = rot_ref.shape[0], order_ref.shape[0]
    size, seq = rows // blocks, rows // EX

    @pl.when(pl.program_id(1) == 0)
    def _():
        slot = 0
        for mine_ref, other_ref in zip(sum_refs[::2], sum_refs[1::2]):
            for at in range(0, mine_ref.shape[0], size):
                here = pl.ds(at, size)
                there = pl.ds(pl.multiple_of(order_ref[slot] * size, size), size)
                rot_ref[there, :] = mine_ref[here, :] + other_ref[here, :]
                slot += 1

    total = None
    for e in range(EX):
        here = pl.ds(e * seq, seq)
        grad = lax.dot_general(
            rot_ref[here, :].astype(BF16),
            out_ref[here, :],
            (((0,), (0,)), ((), ())),
            preferred_element_type=F32,
        )
        total = grad * grad if total is None else total + grad * grad
    fit_ref[...] = total * (1.0 / EX)


def fit(order, flip, sums, rotated_out):
    rows = sum(mine.shape[0] for mine, _ in sums)
    ka, ks = sums[0][0].shape[1], rotated_out.shape[1]
    tile = 256 if ka % 256 == 0 else ka
    part = ks // 2
    flat = [a for pair in sums for a in pair]
    return pl.pallas_call(
        fit_kernel,
        out_shape=jax.ShapeDtypeStruct((ka, ks), F32),
        grid_spec=pltpu.PrefetchScalarGridSpec(
            num_scalar_prefetch=2,
            grid=(ka // tile, 2),
            in_specs=[pl.BlockSpec((a.shape[0], tile), lambda i, j, o, f: (0, i)) for a in flat]
            + [pl.BlockSpec((rows, part), lambda i, j, o, f: (0, j))],
            out_specs=pl.BlockSpec((tile, part), lambda i, j, o, f: (i, j ^ f[0])),
            scratch_shapes=[pltpu.VMEM((rows, tile), F32)],
        ),
        compiler_params=pltpu.CompilerParams(vmem_limit_bytes=40 << 20),
        cost_estimate=pl.CostEstimate(
            flops=2 * rows * ka * ks, bytes_accessed=8 * rows * ka + 2 * rows * ks + 4 * ka * ks, transcendentals=0
        ),
        name="fit",
    )(order, flip, *flat, rotated_out)


def rotate_kernel(choices, end_ref, *refs):
    blocks = refs[: sum(choices)]
    basis_ref, *before, sum_ref, rows_ref = refs[sum(choices) :]
    size = blocks[0].shape[0]
    at = 0
    for i, choice in enumerate(choices):
        here = pl.ds(i * size, size)
        if choice == 1:
            rows_ref[here, :] = blocks[at][...]
        else:
            rows_ref[here, :] = jnp.where(end_ref[0] == 1, blocks[at][...], blocks[at + 1][...])
        at += choice

    @pl.when(pl.program_id(0) == 0)
    def _():
        sum_ref[...] = before[0][...] if before else jnp.zeros_like(sum_ref)

    sum_ref[...] += dot(rows_ref[...], basis_ref[...])


def rotate(before, end, blocks, basis, first, steps):
    flat = [pair for block in blocks for pair in block]
    size, ka = flat[0][0].shape[0], basis.shape[1]
    rows = size * len(blocks)
    specs = []
    for block in blocks:
        for which, (_, skip) in enumerate(block):
            used = lambda e, which=which, n=len(block): 1 if n == 1 else jnp.where(e[0] == 1, 1 - which, which)
            specs.append(
                pl.BlockSpec((size, DEEP), lambda k, e, used=used, skip=skip: (0, (k + skip) * used(e)))
            )
    whole = pl.BlockSpec((rows, ka), lambda k, e: (0, 0))
    arrays = [a for a, _ in flat] + [basis] + ([] if before is None else [before])
    return pl.pallas_call(
        lambda *refs: rotate_kernel([len(block) for block in blocks], *refs),
        out_shape=jax.ShapeDtypeStruct((rows, ka), F32),
        grid_spec=pltpu.PrefetchScalarGridSpec(
            num_scalar_prefetch=1,
            grid=(steps,),
            in_specs=specs
            + [pl.BlockSpec((DEEP, ka), lambda k, e: (first + k, 0))]
            + ([] if before is None else [whole]),
            out_specs=whole,
            scratch_shapes=[pltpu.VMEM((rows, DEEP), BF16)],
        ),
        compiler_params=pltpu.CompilerParams(vmem_limit_bytes=40 << 20),
        cost_estimate=pl.CostEstimate(
            flops=2 * rows * steps * DEEP * ka, bytes_accessed=2 * steps * DEEP * (rows + ka) + 8 * rows * ka, transcendentals=0
        ),
        name="rotate",
    )(end, *arrays)


def swap_narrow(a):
    return lax.ppermute(a, "narrow", [(0, 1), (1, 0)])


def general(inputs, deltas, basis_in, basis_out):
    partial_in = dot(lax.all_gather(inputs, "wide", axis=0, tiled=True), basis_in)
    rotated_out = lax.psum(dot(deltas, basis_out), "wide").astype(BF16)
    order = jnp.arange(EX, dtype=jnp.int32)
    return fit(order, jnp.zeros((1,), jnp.int32), [(partial_in, swap_narrow(partial_in))], rotated_out)


def pairs(step, where=lambda z: True):
    out = []
    for z in range(LINE):
        for x in range(PAIR):
            if where(z):
                tz, tx = step(z, x)
                out.append((z * PAIR + x, tz * PAIR + tx))
    return out


def corner(z):
    return z in (0, LINE - 1)


def middle(z):
    return not corner(z)


ENDS = pairs(lambda z, x: (z ^ 1, x))
TO_ENDS = pairs(lambda z, x: (z ^ 1, x), middle)
FROM_ENDS = pairs(lambda z, x: (z ^ 1, x), corner)
MIDDLE = pairs(lambda z, x: (3 - z, x), middle)
ACROSS = pairs(lambda z, x: (z, 1 - x))
ACROSS_ENDS = pairs(lambda z, x: (z, 1 - x), corner)
ACROSS_MIDDLE = pairs(lambda z, x: (z, 1 - x), middle)


def send(a, perm):
    return lax.ppermute(a, "wide", perm)


def scheduled(inputs, deltas, basis_in, basis_out):
    w = lax.axis_index("wide")
    z, x = w // PAIR, w % PAIR
    at_end = (z == 0) | (z == LINE - 1)
    end = at_end.astype(jnp.int32).reshape(1)
    half = (z >= 2).astype(jnp.int32)
    steps = inputs.shape[1] // DEEP
    size = [steps - steps // 2, steps // 2]
    late = size[1] - 2
    got = {}

    def fence(*names):
        got.update(zip(names, lax.optimization_barrier(tuple(got[n] for n in names))))

    def pick(a, b):
        return jnp.where(at_end, got[a], got[b])

    for c in range(2):
        got["own", c] = inputs[:, c * size[0] * DEEP : (c * size[0] + size[c]) * DEEP]

    def first(c):
        got["x1", c] = send(got["own", c], ACROSS)
        got["a1", c] = send(got["own", c], ENDS)
        got["m1", c] = send(got["own", c], MIDDLE)

    def second(c):
        got["x2", c] = send(pick(("a1", c), ("m1", c)), ACROSS)
        got["a2", c] = send(got["m1", c], TO_ENDS)
        got["m2", c] = send(got["a1", c], MIDDLE)

    def third(c):
        got["x3", c] = send(pick(("a2", c), ("m2", c)), ACROSS)
        got["a3", c] = send(got["m2", c], TO_ENDS)

    def early(before, c):
        blocks = [[("own", c)], [("a1", c)], [("x1", c)], [("a2", c), ("m1", c)]]
        return rotate(before, end, [[(got[n], 0) for n in b] for b in blocks], basis_in, c * size[0], size[c])

    def tail(before, c, x4, skip, count):
        blocks = [[("a3", c), ("m2", c)], [("x2", c), ("e", c)], [("x3", c), ("x2", c)]]
        blocks = [[(got[n], skip) for n in b] for b in blocks] + [[(got[x4], 0), (got["x3", c], skip)]]
        return rotate(before, end, blocks, basis_in, c * size[0] + skip, count)

    part = basis_out.shape[1] // 4

    def columns(a, h, p):
        return lax.dynamic_slice_in_dim(a, (2 * h + p) * part, part, 1)

    first(0)
    got["out"] = dot(deltas, basis_out)
    got["out16"] = got["out"].astype(BF16)
    fence("out", "out16", ("own", 1))
    got["r1"] = send(got["out16"], FROM_ENDS)
    first(1)
    fence(("x1", 0), ("a1", 0), ("m1", 0))
    second(0)
    fence(("x1", 1), ("a1", 1), ("m1", 1))
    second(1)
    fence(("x2", 0), ("a2", 0), ("m2", 0), "r1")
    third(0)
    here = got["out"] + got["r1"].astype(F32)
    for p in range(2):
        got["keep", p] = columns(here, half, p)
        got["m3", p] = send(columns(here, 1 - half, p), MIDDLE)
    got["early"] = early(None, 0)
    fence(("x2", 1), ("a2", 1), ("m2", 1), ("m3", 0), "early")
    third(1)
    got["keep", 0] += got["m3", 0]
    got["x5", 0] = send(got["keep", 0].astype(BF16), ACROSS_MIDDLE)
    got["early"] = early(got["early"], 1)
    fence(("x3", 0), ("a3", 0), ("m3", 1), "early")
    got["x4", 0] = send(got["a3", 0], ACROSS_ENDS)
    got["e", 0] = send(got["x1", 0], FROM_ENDS)
    got["keep", 1] += got["m3", 1]
    got["x5", 1] = send(got["keep", 1].astype(BF16), ACROSS_MIDDLE)
    got["early2"] = swap_narrow(got["early"])
    fence(("x3", 1), ("a3", 1), ("x5", 0))
    got["x4", 1] = send(got["a3", 1][:, : late * DEEP], ACROSS_ENDS)
    got["x4", 2] = send(got["a3", 1][:, late * DEEP :], ACROSS_ENDS)
    got["e", 1] = send(got["x1", 1], FROM_ENDS)

    def settle(p):
        got["sum", p] = (got["keep", p] + got["x5", p].astype(F32)).astype(BF16)
        got["m4", p] = send(got["sum", p], MIDDLE)
        got["n1", p] = send(got["sum", p], TO_ENDS)

    settle(0)
    fence(("x4", 0), ("e", 0), ("x5", 1), ("m4", 0))
    got["n2", 0] = send(got["m4", 0], TO_ENDS)
    settle(1)
    got["late"] = tail(None, 0, ("x4", 0), 0, size[0])
    fence(("x4", 1), ("e", 1), ("m4", 1), "late", "early2")
    got["n2", 1] = send(got["m4", 1], TO_ENDS)
    got["late"] = tail(got["late"], 1, ("x4", 1), 0, late)
    fence(("x4", 2), "late")
    got["late"] = tail(got["late"], 1, ("x4", 2), late, size[1] - late)
    late2 = swap_narrow(got["late"])
    rotated_out = jnp.concatenate(
        [pick(("n1", 0), ("sum", 0)), pick(("n1", 1), ("sum", 1)), pick(("n2", 0), ("m4", 0)), pick(("n2", 1), ("m4", 1))],
        axis=1,
    )
    turn = jnp.where(z >= 2, 3, 0)
    near = [jnp.where(at_end, a, b) ^ turn for a, b in ((0, 1), (1, 0), (2, 2), (3, 3))]
    mine = [q * PAIR + x for q in near]
    other = [q * PAIR + 1 - x for q in near]
    order = jnp.stack(mine[:2] + [other[0], mine[2], mine[3]] + other[1:]).astype(jnp.int32)
    sums = [(got["early"], got["early2"]), (got["late"], late2)]
    return fit(order, half.reshape(1), sums, rotated_out)


def solution(mesh):
    return jax.shard_map(
        scheduled if mesh.shape["wide"] == LINE * PAIR else general,
        mesh=mesh,
        in_specs=(
            P(("grp", "wide"), "narrow"),
            P("grp", "wide"),
            P(("grp", "narrow"), "wide"),
            P(("grp", "wide"), "narrow"),
        ),
        out_specs=P(("grp", "wide"), "narrow"),
        check_vma=False,
    )
```

```python
import jax
import jax.numpy as jnp
from jax import lax
from jax.experimental import pallas as pl
from jax.experimental.pallas import tpu as pltpu
from jax.sharding import PartitionSpec as P

EX = 2
LINE, PAIR = 4, 2
DEEP = 1024
BF16, F32 = jnp.bfloat16, jnp.float32


def dot(a, b):
    return jnp.dot(a, b, preferred_element_type=F32)


def fit_kernel(sizes, choices, order_ref, end_ref, place_ref, *refs):
    sum_refs, refs = refs[: 2 * len(sizes)], refs[2 * len(sizes) :]
    piece_refs, (fit_ref, out_ref, turned_ref, rot_ref) = refs[:-4], refs[-4:]
    rows, ks = out_ref.shape
    size, seq = rows // order_ref.shape[0], rows // EX

    @pl.when(pl.program_id(0) == 0)
    def _():
        at = 0
        for piece, choice in enumerate(choices):
            width = piece_refs[at].shape[1]
            there = pl.ds(pl.multiple_of(place_ref[piece] * width, width), width)
            if choice == 1:
                out_ref[:, there] = piece_refs[at][...]
            else:
                out_ref[:, there] = jnp.where(end_ref[0] == 1, piece_refs[at][...], piece_refs[at + 1][...])
            at += choice

    slot = 0
    for mine_ref, other_ref in zip(sum_refs[::2], sum_refs[1::2]):
        for at in range(0, mine_ref.shape[0], size):
            here = pl.ds(at, size)
            there = pl.ds(pl.multiple_of(order_ref[slot] * size, size), size)
            rot_ref[there, :] = mine_ref[here, :] + other_ref[here, :]
            slot += 1
    turned_ref[...] = rot_ref[...].T.astype(BF16)
    step = min(512, ks)
    for at in range(0, ks, step):
        total = None
        for e in range(EX):
            here = pl.ds(e * seq, seq)
            grad = dot(turned_ref[:, here], out_ref[here, pl.ds(at, step)])
            total = grad * grad if total is None else total + grad * grad
        fit_ref[:, pl.ds(at, step)] = total * (1.0 / EX)


def fit(order, end, sums, pieces, places):
    rows = sum(mine.shape[0] for mine, _ in sums)
    ka = sums[0][0].shape[1]
    ks = sum(piece[0].shape[1] for piece in pieces)
    tile = 256 if ka % 256 == 0 else ka
    flat = [a for pair in sums for a in pair]
    outs = [a for piece in pieces for a in piece]
    return pl.pallas_call(
        lambda *refs: fit_kernel([pair[0].shape[0] for pair in sums], [len(piece) for piece in pieces], *refs),
        out_shape=jax.ShapeDtypeStruct((ka, ks), F32),
        grid_spec=pltpu.PrefetchScalarGridSpec(
            num_scalar_prefetch=3,
            grid=(ka // tile,),
            in_specs=[pl.BlockSpec((a.shape[0], tile), lambda i, *_: (0, i)) for a in flat]
            + [pl.BlockSpec(a.shape, lambda i, *_: (0, 0)) for a in outs],
            out_specs=pl.BlockSpec((tile, ks), lambda i, *_: (i, 0)),
            scratch_shapes=[
                pltpu.VMEM((rows, ks), BF16),
                pltpu.VMEM((tile, rows), BF16),
                pltpu.VMEM((rows, tile), F32),
            ],
        ),
        compiler_params=pltpu.CompilerParams(vmem_limit_bytes=40 << 20),
        cost_estimate=pl.CostEstimate(
            flops=2 * rows * ka * ks, bytes_accessed=8 * rows * ka + 2 * rows * ks + 4 * ka * ks, transcendentals=0
        ),
        name="fit",
    )(order, end, places, *flat, *outs)


def rotate_kernel(choices, end_ref, *refs):
    blocks = refs[: sum(choices)]
    basis_ref, *before, sum_ref, rows_ref = refs[sum(choices) :]
    size = blocks[0].shape[0]
    at = 0
    for i, choice in enumerate(choices):
        here = pl.ds(i * size, size)
        if choice == 1:
            rows_ref[here, :] = blocks[at][...]
        else:
            rows_ref[here, :] = jnp.where(end_ref[0] == 1, blocks[at][...], blocks[at + 1][...])
        at += choice

    @pl.when(pl.program_id(0) == 0)
    def _():
        sum_ref[...] = before[0][...] if before else jnp.zeros_like(sum_ref)

    sum_ref[...] += dot(rows_ref[...], basis_ref[...])


def rotate(before, end, blocks, basis, first, steps):
    flat = [pair for block in blocks for pair in block]
    size, ka = flat[0][0].shape[0], basis.shape[1]
    rows = size * len(blocks)
    specs = []
    for block in blocks:
        for which, (_, skip) in enumerate(block):
            used = lambda e, which=which, n=len(block): 1 if n == 1 else jnp.where(e[0] == 1, 1 - which, which)
            specs.append(
                pl.BlockSpec((size, DEEP), lambda k, e, used=used, skip=skip: (0, (k + skip) * used(e)))
            )
    whole = pl.BlockSpec((rows, ka), lambda k, e: (0, 0))
    arrays = [a for a, _ in flat] + [basis] + ([] if before is None else [before])
    return pl.pallas_call(
        lambda *refs: rotate_kernel([len(block) for block in blocks], *refs),
        out_shape=jax.ShapeDtypeStruct((rows, ka), F32),
        grid_spec=pltpu.PrefetchScalarGridSpec(
            num_scalar_prefetch=1,
            grid=(steps,),
            in_specs=specs
            + [pl.BlockSpec((DEEP, ka), lambda k, e: (first + k, 0))]
            + ([] if before is None else [whole]),
            out_specs=whole,
            scratch_shapes=[pltpu.VMEM((rows, DEEP), BF16)],
        ),
        compiler_params=pltpu.CompilerParams(vmem_limit_bytes=40 << 20),
        cost_estimate=pl.CostEstimate(
            flops=rows * ka, bytes_accessed=4 * rows * ka, transcendentals=0
        ),
        name="rotate",
    )(end, *arrays)


def swap_narrow(a):
    return lax.ppermute(a, "narrow", [(0, 1), (1, 0)])


def general(inputs, deltas, basis_in, basis_out):
    partial_in = dot(lax.all_gather(inputs, "wide", axis=0, tiled=True), basis_in)
    rotated_out = lax.psum(dot(deltas, basis_out), "wide").astype(BF16)
    order, zero = jnp.arange(EX, dtype=jnp.int32), jnp.zeros((1,), jnp.int32)
    return fit(order, zero, [(partial_in, swap_narrow(partial_in))], [[rotated_out]], zero)


def pairs(step, where=lambda z: True):
    out = []
    for z in range(LINE):
        for x in range(PAIR):
            if where(z):
                tz, tx = step(z, x)
                out.append((z * PAIR + x, tz * PAIR + tx))
    return out


def corner(z):
    return z in (0, LINE - 1)


def middle(z):
    return not corner(z)


ENDS = pairs(lambda z, x: (z ^ 1, x))
TO_ENDS = pairs(lambda z, x: (z ^ 1, x), middle)
FROM_ENDS = pairs(lambda z, x: (z ^ 1, x), corner)
MIDDLE = pairs(lambda z, x: (3 - z, x), middle)
ACROSS = pairs(lambda z, x: (z, 1 - x))
ACROSS_ENDS = pairs(lambda z, x: (z, 1 - x), corner)
ACROSS_MIDDLE = pairs(lambda z, x: (z, 1 - x), middle)


def send(a, perm):
    return lax.ppermute(a, "wide", perm)


def scheduled(inputs, deltas, basis_in, basis_out):
    w = lax.axis_index("wide")
    z, x = w // PAIR, w % PAIR
    at_end = (z == 0) | (z == LINE - 1)
    end = at_end.astype(jnp.int32).reshape(1)
    half = (z >= 2).astype(jnp.int32)
    steps = inputs.shape[1] // DEEP
    some = steps // 2
    cuts = [0, 4 * steps // 14, 8 * steps // 14, 12 * steps // 14, steps]
    part = basis_out.shape[1] // 4
    got = {"own": inputs}

    def fence(*names):
        got.update(zip(names, lax.optimization_barrier(tuple(got[n] for n in names))))

    def pick(a, b):
        return jnp.where(at_end, got[a], got[b])

    def columns(a, h, p):
        return lax.dynamic_slice_in_dim(a, (2 * h + p) * part, part, 1)

    def turn(before, blocks, first, count):
        return rotate(before, end, [[(got[n], first) for n in block] for block in blocks], basis_in, first, count)

    def settle(p):
        got["sum", p] = (got["keep", p] + got["x5", p].astype(F32)).astype(BF16)
        got["m4", p] = send(got["sum", p], MIDDLE)
        got["n1", p] = send(got["sum", p], TO_ENDS)

    got["x1"] = send(got["own"], ACROSS)
    got["a1"] = send(got["own"], ENDS)
    got["m1"] = send(got["own"], MIDDLE)
    got["out"] = dot(deltas, basis_out)
    got["out16"] = got["out"].astype(BF16)
    fence("x1", "a1", "m1", "out", "out16")
    got["x2"] = send(pick("a1", "m1"), ACROSS)
    got["a2"] = send(got["m1"], TO_ENDS)
    got["m2"] = send(got["a1"], MIDDLE)
    got["r1"] = send(got["out16"], FROM_ENDS)
    got["A"] = turn(None, [["own"], ["a1"], ["x1"]], 0, steps)
    fence("x2", "a2", "m2", "r1", "A")
    got["x3"] = send(pick("a2", "m2"), ACROSS)
    got["a3"] = send(got["m2"], TO_ENDS)
    here = got["out"] + got["r1"].astype(F32)
    for p in range(2):
        got["keep", p], got["give", p] = columns(here, half, p), columns(here, 1 - half, p)
    got["m3", 0] = send(got["give", 0], MIDDLE)
    got["e"] = send(got["x1"], FROM_ENDS)
    got["B"] = turn(None, [["a2", "m1"], ["x2"]], 0, some)
    fence(("m3", 0), ("give", 1), "B")
    got["m3", 1] = send(got["give", 1], MIDDLE)
    got["keep", 0] += got["m3", 0]
    got["x5", 0] = send(got["keep", 0].astype(BF16), ACROSS_MIDDLE)
    got["B"] = turn(got["B"], [["a2", "m1"], ["x2"]], some, steps - some)
    fence("x3", "a3", "e", ("x5", 0), "B")
    def x4(piece):
        got["x4", piece] = send(got["a3"][:, cuts[piece] * DEEP : cuts[piece + 1] * DEEP], ACROSS_ENDS)

    def last(piece):
        first = cuts[piece]
        blocks = [[(got["x4", piece], 0), (got["e"], first)]]
        got["D"] = rotate(got.get("D"), end, blocks, basis_in, first, cuts[piece + 1] - first)

    x4(0)
    settle(0)
    got["C"] = turn(None, [["a3", "m2"], ["x3"]], 0, some)
    fence(("x4", 0), ("m3", 1), ("m4", 0), ("n1", 0), "A", "C", "a3")
    x4(1)
    got["keep", 1] += got["m3", 1]
    got["x5", 1] = send(got["keep", 1].astype(BF16), ACROSS_MIDDLE)
    got["n2", 0] = send(got["m4", 0], TO_ENDS)
    got["A2"] = swap_narrow(got["A"])
    got["C"] = turn(got["C"], [["a3", "m2"], ["x3"]], some, steps - some)
    fence(("x4", 1), ("x5", 1), ("n2", 0), "A2", "B", "C", "a3")
    x4(2)
    settle(1)
    got["B2"] = swap_narrow(got["B"])
    last(0)
    last(1)
    fence(("x4", 2), ("m4", 1), ("n1", 1), "B2", "C", "D", "a3")
    x4(3)
    got["n2", 1] = send(got["m4", 1], TO_ENDS)
    got["C2"] = swap_narrow(got["C"])
    last(2)
    fence(("x4", 3), "D")
    last(3)
    got["D2"] = swap_narrow(got["D"])

    flip = jnp.where(z >= 2, 3, 0)
    line = lambda a, b: jnp.where(at_end, a, b) ^ flip
    mine, other = (lambda a, b: line(a, b) * PAIR + x), (lambda a, b: line(a, b) * PAIR + 1 - x)
    order = [mine(0, 1), mine(1, 0), other(0, 1), mine(2, 2), other(1, 2), mine(3, 3), other(2, 3), other(3, 0)]
    pieces = [[got["n1", p], got["sum", p]] for p in range(2)] + [[got["n2", p], got["m4", p]] for p in range(2)]
    places = [2 * half, 2 * half + 1, 2 - 2 * half, 3 - 2 * half]
    sums = [(got[n], got[n + "2"]) for n in "ABCD"]
    return fit(jnp.stack(order).astype(jnp.int32), end, sums, pieces, jnp.stack(places).astype(jnp.int32))


def solution(mesh):
    return jax.shard_map(
        scheduled if mesh.shape["wide"] == LINE * PAIR else general,
        mesh=mesh,
        in_specs=(
            P(("grp", "wide"), "narrow"),
            P("grp", "wide"),
            P(("grp", "narrow"), "wide"),
            P(("grp", "wide"), "narrow"),
        ),
        out_specs=P(("grp", "wide"), "narrow"),
        check_vma=False,
    )
```

```python
import jax
import jax.numpy as jnp
from jax import lax
from jax.experimental import pallas as pl
from jax.experimental.pallas import tpu as pltpu
from jax.sharding import PartitionSpec as P

EX = 2
LINE, PAIR = 4, 2
DEEP = 1024
VMEM = 20 << 20
BF16, F32 = jnp.bfloat16, jnp.float32


def dot(a, b):
    return jnp.dot(a, b, preferred_element_type=F32)


def fit_kernel(sizes, choices, order_ref, end_ref, place_ref, *refs):
    sum_refs, refs = refs[: 2 * len(sizes)], refs[2 * len(sizes) :]
    piece_refs, (fit_ref, out_ref, turned_ref, rot_ref) = refs[:-4], refs[-4:]
    rows, ks = out_ref.shape
    size, seq = rows // order_ref.shape[0], rows // EX

    @pl.when(pl.program_id(0) == 0)
    def _():
        at = 0
        for piece, choice in enumerate(choices):
            width = piece_refs[at].shape[1]
            there = pl.ds(pl.multiple_of(place_ref[piece] * width, width), width)
            if choice == 1:
                out_ref[:, there] = piece_refs[at][...]
            else:
                out_ref[:, there] = jnp.where(end_ref[0] == 1, piece_refs[at][...], piece_refs[at + 1][...])
            at += choice

    slot = 0
    for mine_ref, other_ref in zip(sum_refs[::2], sum_refs[1::2]):
        for at in range(0, mine_ref.shape[0], size):
            here = pl.ds(at, size)
            there = pl.ds(pl.multiple_of(order_ref[slot] * size, size), size)
            rot_ref[there, :] = mine_ref[here, :] + other_ref[here, :]
            slot += 1
    turned_ref[...] = rot_ref[...].T.astype(BF16)
    step = min(512, ks)
    for at in range(0, ks, step):
        total = None
        for e in range(EX):
            here = pl.ds(e * seq, seq)
            grad = dot(turned_ref[:, here], out_ref[here, pl.ds(at, step)])
            total = grad * grad if total is None else total + grad * grad
        fit_ref[:, pl.ds(at, step)] = total * (1.0 / EX)


def fit(order, end, sums, pieces, places):
    rows = sum(mine.shape[0] for mine, _ in sums)
    ka = sums[0][0].shape[1]
    ks = sum(piece[0].shape[1] for piece in pieces)
    tile = 256 if ka % 256 == 0 else ka
    flat = [a for pair in sums for a in pair]
    outs = [a for piece in pieces for a in piece]
    return pl.pallas_call(
        lambda *refs: fit_kernel([pair[0].shape[0] for pair in sums], [len(piece) for piece in pieces], *refs),
        out_shape=jax.ShapeDtypeStruct((ka, ks), F32),
        grid_spec=pltpu.PrefetchScalarGridSpec(
            num_scalar_prefetch=3,
            grid=(ka // tile,),
            in_specs=[pl.BlockSpec((a.shape[0], tile), lambda i, *_: (0, i)) for a in flat]
            + [pl.BlockSpec(a.shape, lambda i, *_: (0, 0)) for a in outs],
            out_specs=pl.BlockSpec((tile, ks), lambda i, *_: (i, 0)),
            scratch_shapes=[
                pltpu.VMEM((rows, ks), BF16),
                pltpu.VMEM((tile, rows), BF16),
                pltpu.VMEM((rows, tile), F32),
            ],
        ),
        compiler_params=pltpu.CompilerParams(vmem_limit_bytes=VMEM),
        cost_estimate=pl.CostEstimate(
            flops=2 * rows * ka * ks, bytes_accessed=8 * rows * ka + 2 * rows * ks + 4 * ka * ks, transcendentals=0
        ),
        name="fit",
    )(order, end, places, *flat, *outs)


def rotate_kernel(choices, end_ref, *refs):
    blocks = refs[: sum(choices)]
    basis_ref, *before, sum_ref, rows_ref = refs[sum(choices) :]
    size = blocks[0].shape[0]
    at = 0
    for i, choice in enumerate(choices):
        here = pl.ds(i * size, size)
        if choice == 1:
            rows_ref[here, :] = blocks[at][...]
        else:
            rows_ref[here, :] = jnp.where(end_ref[0] == 1, blocks[at][...], blocks[at + 1][...])
        at += choice

    @pl.when(pl.program_id(0) == 0)
    def _():
        sum_ref[...] = before[0][...] if before else jnp.zeros_like(sum_ref)

    sum_ref[...] += dot(rows_ref[...], basis_ref[...])


def rotate(before, end, blocks, basis, first, steps):
    flat = [pair for block in blocks for pair in block]
    size, ka = flat[0][0].shape[0], basis.shape[1]
    rows = size * len(blocks)
    specs = []
    for block in blocks:
        for which, (_, skip) in enumerate(block):
            used = lambda e, which=which, n=len(block): 1 if n == 1 else jnp.where(e[0] == 1, 1 - which, which)
            specs.append(
                pl.BlockSpec((size, DEEP), lambda k, e, used=used, skip=skip: (0, (k + skip) * used(e)))
            )
    whole = pl.BlockSpec((rows, ka), lambda k, e: (0, 0))
    arrays = [a for a, _ in flat] + [basis] + ([] if before is None else [before])
    return pl.pallas_call(
        lambda *refs: rotate_kernel([len(block) for block in blocks], *refs),
        out_shape=jax.ShapeDtypeStruct((rows, ka), F32),
        grid_spec=pltpu.PrefetchScalarGridSpec(
            num_scalar_prefetch=1,
            grid=(steps,),
            in_specs=specs
            + [pl.BlockSpec((DEEP, ka), lambda k, e: (first + k, 0))]
            + ([] if before is None else [whole]),
            out_specs=whole,
            scratch_shapes=[pltpu.VMEM((rows, DEEP), BF16)],
        ),
        compiler_params=pltpu.CompilerParams(vmem_limit_bytes=VMEM),
        cost_estimate=pl.CostEstimate(
            flops=rows * ka, bytes_accessed=4 * rows * ka, transcendentals=0
        ),
        name="rotate",
    )(end, *arrays)


def swap_narrow(a):
    return lax.ppermute(a, "narrow", [(0, 1), (1, 0)])


def general(inputs, deltas, basis_in, basis_out):
    partial_in = dot(lax.all_gather(inputs, "wide", axis=0, tiled=True), basis_in)
    rotated_out = lax.psum(dot(deltas, basis_out), "wide").astype(BF16)
    order, zero = jnp.arange(EX, dtype=jnp.int32), jnp.zeros((1,), jnp.int32)
    return fit(order, zero, [(partial_in, swap_narrow(partial_in))], [[rotated_out]], zero)


def pairs(step, where=lambda z: True):
    out = []
    for z in range(LINE):
        for x in range(PAIR):
            if where(z):
                tz, tx = step(z, x)
                out.append((z * PAIR + x, tz * PAIR + tx))
    return out


def corner(z):
    return z in (0, LINE - 1)


def middle(z):
    return not corner(z)


ENDS = pairs(lambda z, x: (z ^ 1, x))
TO_ENDS = pairs(lambda z, x: (z ^ 1, x), middle)
FROM_ENDS = pairs(lambda z, x: (z ^ 1, x), corner)
MIDDLE = pairs(lambda z, x: (3 - z, x), middle)
ACROSS = pairs(lambda z, x: (z, 1 - x))
ACROSS_ENDS = pairs(lambda z, x: (z, 1 - x), corner)
ACROSS_MIDDLE = pairs(lambda z, x: (z, 1 - x), middle)


def send(a, perm):
    return lax.ppermute(a, "wide", perm)


def scheduled(inputs, deltas, basis_in, basis_out):
    w = lax.axis_index("wide")
    z, x = w // PAIR, w % PAIR
    at_end = (z == 0) | (z == LINE - 1)
    end = at_end.astype(jnp.int32).reshape(1)
    half = (z >= 2).astype(jnp.int32)
    steps = inputs.shape[1] // DEEP
    cuts = [0, 4 * steps // 14, 8 * steps // 14, 12 * steps // 14, steps]
    part = basis_out.shape[1] // 4
    got = {"own": inputs}

    def fence(*names):
        got.update(zip(names, lax.optimization_barrier(tuple(got[n] for n in names))))

    def pick(a, b):
        return jnp.where(at_end, got[a], got[b])

    def columns(a, h, p):
        return lax.dynamic_slice_in_dim(a, (2 * h + p) * part, part, 1)

    def turn(before, blocks, first, count):
        return rotate(before, end, [[(got[n], first) for n in block] for block in blocks], basis_in, first, count)

    def settle(p):
        got["sum", p] = (got["keep", p] + got["x5", p].astype(F32)).astype(BF16)
        got["m4", p] = send(got["sum", p], MIDDLE)
        got["n1", p] = send(got["sum", p], TO_ENDS)

    got["x1"] = send(got["own"], ACROSS)
    got["a1"] = send(got["own"], ENDS)
    got["m1"] = send(got["own"], MIDDLE)
    got["out"] = dot(deltas, basis_out)
    got["out16"] = got["out"].astype(BF16)
    fence("x1", "a1", "m1", "out", "out16")
    got["pick"] = pick("a1", "m1")
    fence("pick", "a1", "m1", "out16")
    got["x2"] = send(got["pick"], ACROSS)
    got["a2"] = send(got["m1"], TO_ENDS)
    got["m2"] = send(got["a1"], MIDDLE)
    got["r1"] = send(got["out16"], FROM_ENDS)
    got["A"] = turn(None, [["own"], ["a1"], ["x1"]], 0, steps)
    fence("x1", "x2", "a2", "m2", "r1", "A")
    got["pick"] = pick("a2", "m2")
    fence("pick", "m2", "x1", "out")
    got["x3"] = send(got["pick"], ACROSS)
    got["a3"] = send(got["m2"], TO_ENDS)
    here = got["out"] + got["r1"].astype(F32)
    for p in range(2):
        got["keep", p] = columns(here, half, p)
        got["m3", p] = send(columns(here, 1 - half, p), MIDDLE)
    got["e"] = send(got["x1"], FROM_ENDS)
    got["B"] = turn(None, [["a2", "m1"], ["x2"]], 0, steps)
    fence("x3", "a3", "e", "B")

    def x4(piece):
        got["x4", piece] = send(got["a3"][:, cuts[piece] * DEEP : cuts[piece + 1] * DEEP], ACROSS_ENDS)

    def last(piece):
        first = cuts[piece]
        blocks = [[(got["a3"], first), (got["m2"], first)], [(got["x3"], first)], [(got["x4", piece], 0), (got["e"], first)]]
        got["D"] = rotate(got.get("D"), end, blocks, basis_in, first, cuts[piece + 1] - first)

    def cross(p):
        got["keep", p] += got["m3", p]
        got["x5", p] = send(got["keep", p].astype(BF16), ACROSS_MIDDLE)

    x4(0)
    fence(("m3", 0), ("m3", 1), "a3")
    cross(0)
    cross(1)
    fence(("x4", 0), ("x5", 0), "a3")
    x4(1)
    settle(0)
    last(0)
    fence(("x4", 1), ("x5", 1), ("m4", 0), ("n1", 0), "D", "a3")
    x4(2)
    got["n2", 0] = send(got["m4", 0], TO_ENDS)
    settle(1)
    last(1)
    fence(("x4", 2), ("m4", 1), ("n1", 1), ("n2", 0), "A", "B", "D", "a3")
    x4(3)
    got["n2", 1] = send(got["m4", 1], TO_ENDS)
    got["A2"] = swap_narrow(got["A"])
    got["B2"] = swap_narrow(got["B"])
    last(2)
    fence(("x4", 3), ("n2", 1), "A2", "B2", "D")
    last(3)
    got["D2"] = swap_narrow(got["D"])

    flip = jnp.where(z >= 2, 3, 0)
    line = lambda a, b: jnp.where(at_end, a, b) ^ flip
    mine, other = (lambda a, b: line(a, b) * PAIR + x), (lambda a, b: line(a, b) * PAIR + 1 - x)
    order = [mine(0, 1), mine(1, 0), other(0, 1), mine(2, 2), other(1, 2), mine(3, 3), other(2, 3), other(3, 0)]
    pieces = [[got["n1", p], got["sum", p]] for p in range(2)] + [[got["n2", p], got["m4", p]] for p in range(2)]
    places = [2 * half, 2 * half + 1, 2 - 2 * half, 3 - 2 * half]
    sums = [(got[n], got[n + "2"]) for n in "ABD"]
    return fit(jnp.stack(order).astype(jnp.int32), end, sums, pieces, jnp.stack(places).astype(jnp.int32))


def solution(mesh):
    return jax.shard_map(
        scheduled if mesh.shape["wide"] == LINE * PAIR else general,
        mesh=mesh,
        in_specs=(
            P(("grp", "wide"), "narrow"),
            P("grp", "wide"),
            P(("grp", "narrow"), "wide"),
            P(("grp", "wide"), "narrow"),
        ),
        out_specs=P(("grp", "wide"), "narrow"),
        check_vma=False,
    )
```

```python
import jax
import jax.numpy as jnp
from jax import lax
from jax.experimental import pallas as pl
from jax.experimental.pallas import tpu as pltpu
from jax.sharding import PartitionSpec as P

EX = 2
LINE, PAIR = 4, 2
DEEP = 1024
VMEM = 20 << 20
BF16, F32 = jnp.bfloat16, jnp.float32


def dot(a, b):
    return jnp.dot(a, b, preferred_element_type=F32)


def fit_kernel(sizes, choices, order_ref, end_ref, place_ref, *refs):
    sum_refs, refs = refs[: 2 * len(sizes)], refs[2 * len(sizes) :]
    piece_refs, (fit_ref, out_ref, turned_ref, rot_ref) = refs[:-4], refs[-4:]
    rows, ks = out_ref.shape
    size, seq = rows // order_ref.shape[0], rows // EX

    @pl.when(pl.program_id(0) == 0)
    def _():
        at = 0
        for piece, choice in enumerate(choices):
            width = piece_refs[at].shape[1]
            there = pl.ds(pl.multiple_of(place_ref[piece] * width, width), width)
            if choice == 1:
                out_ref[:, there] = piece_refs[at][...]
            else:
                out_ref[:, there] = jnp.where(end_ref[0] == 1, piece_refs[at][...], piece_refs[at + 1][...])
            at += choice

    slot = 0
    for mine_ref, other_ref in zip(sum_refs[::2], sum_refs[1::2]):
        for at in range(0, mine_ref.shape[0], size):
            here = pl.ds(at, size)
            there = pl.ds(pl.multiple_of(order_ref[slot] * size, size), size)
            rot_ref[there, :] = mine_ref[here, :] + other_ref[here, :]
            slot += 1
    turned_ref[...] = rot_ref[...].T.astype(BF16)
    step = min(512, ks)
    for at in range(0, ks, step):
        total = None
        for e in range(EX):
            here = pl.ds(e * seq, seq)
            grad = dot(turned_ref[:, here], out_ref[here, pl.ds(at, step)])
            total = grad * grad if total is None else total + grad * grad
        fit_ref[:, pl.ds(at, step)] = total * (1.0 / EX)


def fit(order, end, sums, pieces, places):
    rows = sum(mine.shape[0] for mine, _ in sums)
    ka = sums[0][0].shape[1]
    ks = sum(piece[0].shape[1] for piece in pieces)
    tile = 256 if ka % 256 == 0 else ka
    flat = [a for pair in sums for a in pair]
    outs = [a for piece in pieces for a in piece]
    return pl.pallas_call(
        lambda *refs: fit_kernel([pair[0].shape[0] for pair in sums], [len(piece) for piece in pieces], *refs),
        out_shape=jax.ShapeDtypeStruct((ka, ks), F32),
        grid_spec=pltpu.PrefetchScalarGridSpec(
            num_scalar_prefetch=3,
            grid=(ka // tile,),
            in_specs=[pl.BlockSpec((a.shape[0], tile), lambda i, *_: (0, i)) for a in flat]
            + [pl.BlockSpec(a.shape, lambda i, *_: (0, 0)) for a in outs],
            out_specs=pl.BlockSpec((tile, ks), lambda i, *_: (i, 0)),
            scratch_shapes=[
                pltpu.VMEM((rows, ks), BF16),
                pltpu.VMEM((tile, rows), BF16),
                pltpu.VMEM((rows, tile), F32),
            ],
        ),
        compiler_params=pltpu.CompilerParams(vmem_limit_bytes=56 << 20),
        cost_estimate=pl.CostEstimate(
            flops=2 * rows * ka * ks, bytes_accessed=8 * rows * ka + 2 * rows * ks + 4 * ka * ks, transcendentals=0
        ),
        name="fit",
    )(order, end, places, *flat, *outs)


def rotate_kernel(choices, end_ref, *refs):
    blocks = refs[: sum(choices)]
    basis_ref, *before, sum_ref, rows_ref = refs[sum(choices) :]
    size = blocks[0].shape[0]
    at = 0
    for i, choice in enumerate(choices):
        here = pl.ds(i * size, size)
        if choice == 1:
            rows_ref[here, :] = blocks[at][...]
        else:
            rows_ref[here, :] = jnp.where(end_ref[0] == 1, blocks[at][...], blocks[at + 1][...])
        at += choice

    @pl.when(pl.program_id(0) == 0)
    def _():
        sum_ref[...] = before[0][...] if before else jnp.zeros_like(sum_ref)

    sum_ref[...] += dot(rows_ref[...], basis_ref[...])


def rotate(before, end, blocks, basis, first, steps):
    flat = [pair for block in blocks for pair in block]
    size, ka = flat[0][0].shape[0], basis.shape[1]
    rows = size * len(blocks)
    specs = []
    for block in blocks:
        for which, (_, skip) in enumerate(block):
            used = lambda e, which=which, n=len(block): 1 if n == 1 else jnp.where(e[0] == 1, 1 - which, which)
            specs.append(
                pl.BlockSpec((size, DEEP), lambda k, e, used=used, skip=skip: (0, (k + skip) * used(e)))
            )
    whole = pl.BlockSpec((rows, ka), lambda k, e: (0, 0))
    arrays = [a for a, _ in flat] + [basis] + ([] if before is None else [before])
    return pl.pallas_call(
        lambda *refs: rotate_kernel([len(block) for block in blocks], *refs),
        out_shape=jax.ShapeDtypeStruct((rows, ka), F32),
        grid_spec=pltpu.PrefetchScalarGridSpec(
            num_scalar_prefetch=1,
            grid=(steps,),
            in_specs=specs
            + [pl.BlockSpec((DEEP, ka), lambda k, e: (first + k, 0))]
            + ([] if before is None else [whole]),
            out_specs=whole,
            scratch_shapes=[pltpu.VMEM((rows, DEEP), BF16)],
        ),
        compiler_params=pltpu.CompilerParams(vmem_limit_bytes=VMEM),
        cost_estimate=pl.CostEstimate(
            flops=rows * ka, bytes_accessed=4 * rows * ka, transcendentals=0
        ),
        name="rotate",
    )(end, *arrays)


def swap_narrow(a):
    return lax.ppermute(a, "narrow", [(0, 1), (1, 0)])


def general(inputs, deltas, basis_in, basis_out):
    partial_in = dot(lax.all_gather(inputs, "wide", axis=0, tiled=True), basis_in)
    rotated_out = lax.psum(dot(deltas, basis_out), "wide").astype(BF16)
    order, zero = jnp.arange(EX, dtype=jnp.int32), jnp.zeros((1,), jnp.int32)
    return fit(order, zero, [(partial_in, swap_narrow(partial_in))], [[rotated_out]], zero)


def pairs(step, where=lambda z: True):
    out = []
    for z in range(LINE):
        for x in range(PAIR):
            if where(z):
                tz, tx = step(z, x)
                out.append((z * PAIR + x, tz * PAIR + tx))
    return out


def corner(z):
    return z in (0, LINE - 1)


def middle(z):
    return not corner(z)


ENDS = pairs(lambda z, x: (z ^ 1, x))
TO_ENDS = pairs(lambda z, x: (z ^ 1, x), middle)
FROM_ENDS = pairs(lambda z, x: (z ^ 1, x), corner)
MIDDLE = pairs(lambda z, x: (3 - z, x), middle)
ACROSS = pairs(lambda z, x: (z, 1 - x))
ACROSS_ENDS = pairs(lambda z, x: (z, 1 - x), corner)
ACROSS_MIDDLE = pairs(lambda z, x: (z, 1 - x), middle)


def send(a, perm):
    return lax.ppermute(a, "wide", perm)


def scheduled(inputs, deltas, basis_in, basis_out):
    w = lax.axis_index("wide")
    z, x = w // PAIR, w % PAIR
    at_end = (z == 0) | (z == LINE - 1)
    end = at_end.astype(jnp.int32).reshape(1)
    half = (z >= 2).astype(jnp.int32)
    steps = inputs.shape[1] // DEEP
    cuts = [0, 4 * steps // 14, 8 * steps // 14, 12 * steps // 14, steps]
    part = basis_out.shape[1] // 4
    got = {"own": inputs}

    def fence(*names):
        got.update(zip(names, lax.optimization_barrier(tuple(got[n] for n in names))))

    def pick(a, b):
        return jnp.where(at_end, got[a], got[b])

    def columns(a, h):
        return lax.dynamic_slice_in_dim(a, h * 2 * part, 2 * part, 1)

    def turn(before, blocks, first, count):
        return rotate(before, end, [[(got[n], first) for n in block] for block in blocks], basis_in, first, count)

    def settle(p):
        got["sum", p] = (got["keep", p] + got["x5", p].astype(F32)).astype(BF16)
        got["m4", p] = send(got["sum", p], MIDDLE)
        got["n1", p] = send(got["sum", p], TO_ENDS)

    got["x1"] = send(got["own"], ACROSS)
    got["a1"] = send(got["own"], ENDS)
    got["m1"] = send(got["own"], MIDDLE)
    got["give"] = dot(deltas, columns(basis_out, 1 - half))
    got["r1", 0] = send(got["give"].astype(BF16), FROM_ENDS)
    got["keep"] = dot(deltas, columns(basis_out, half))
    got["r1", 1] = send(got["keep"].astype(BF16), FROM_ENDS)
    fence("x1", "a1", "m1", "give", "keep")
    got["pick"] = pick("a1", "m1")
    fence("pick", "a1", "m1", "x1")
    got["x2"] = send(got["pick"], ACROSS)
    got["a2"] = send(got["m1"], TO_ENDS)
    got["m2"] = send(got["a1"], MIDDLE)
    some = steps // 2
    got["A"] = turn(None, [["own"], ["a1"], ["x1"]], 0, some)
    fence(("r1", 0), "give", "A")
    got["give"] += got["r1", 0].astype(F32)
    got["A"] = turn(got["A"], [["own"], ["a1"], ["x1"]], some, steps - some)
    fence("x1", "x2", "a2", "m2", "give", "keep", ("r1", 1), "A")
    got["m3"] = send(got["give"], MIDDLE)
    got["pick"] = pick("a2", "m2")
    fence("pick", "m2", "x1", "keep")
    got["x3"] = send(got["pick"], ACROSS)
    got["a3"] = send(got["m2"], TO_ENDS)
    got["e"] = send(got["x1"], FROM_ENDS)
    got["B"] = turn(None, [["a2", "m1"], ["x2"]], 0, steps)
    fence("x3", "a3", "e", "B")
    got["keep"] += got["r1", 1].astype(F32)

    def x4(piece):
        got["x4", piece] = send(got["a3"][:, cuts[piece] * DEEP : cuts[piece + 1] * DEEP], ACROSS_ENDS)

    def last(piece):
        first = cuts[piece]
        blocks = [[(got["a3"], first), (got["m2"], first)], [(got["x3"], first)], [(got["x4", piece], 0), (got["e"], first)]]
        got["D"] = rotate(got.get("D"), end, blocks, basis_in, first, cuts[piece + 1] - first)

    def cross(p):
        here = slice(p * part, (p + 1) * part)
        got["keep", p] = got["keep"][:, here] + got["m3"][:, here]
        got["x5", p] = send(got["keep", p].astype(BF16), ACROSS_MIDDLE)

    x4(0)
    fence("m3", "a3")
    cross(0)
    cross(1)
    fence(("x4", 0), ("x5", 0), "a3")
    x4(1)
    settle(0)
    last(0)
    fence(("x4", 1), ("x5", 1), ("m4", 0), ("n1", 0), "D", "a3")
    x4(2)
    got["n2", 0] = send(got["m4", 0], TO_ENDS)
    settle(1)
    last(1)
    fence(("x4", 2), ("m4", 1), ("n2", 0), "A", "B", "D", "a3")
    x4(3)
    got["n2", 1] = send(got["m4", 1], TO_ENDS)
    got["A2"] = swap_narrow(got["A"])
    got["B2"] = swap_narrow(got["B"])
    last(2)
    fence(("x4", 3), ("n1", 1), ("n2", 1), "A2", "B2", "D")
    last(3)
    got["D2"] = swap_narrow(got["D"])

    flip = jnp.where(z >= 2, 3, 0)
    line = lambda a, b: jnp.where(at_end, a, b) ^ flip
    mine, other = (lambda a, b: line(a, b) * PAIR + x), (lambda a, b: line(a, b) * PAIR + 1 - x)
    order = [mine(0, 1), mine(1, 0), other(0, 1), mine(2, 2), other(1, 2), mine(3, 3), other(2, 3), other(3, 0)]
    pieces = [[got["n1", p], got["sum", p]] for p in range(2)] + [[got["n2", p], got["m4", p]] for p in range(2)]
    places = [2 * half, 2 * half + 1, 2 - 2 * half, 3 - 2 * half]
    sums = [(got[n], got[n + "2"]) for n in "ABD"]
    return fit(jnp.stack(order).astype(jnp.int32), end, sums, pieces, jnp.stack(places).astype(jnp.int32))


def solution(mesh):
    return jax.shard_map(
        scheduled if mesh.shape["wide"] == LINE * PAIR else general,
        mesh=mesh,
        in_specs=(
            P(("grp", "wide"), "narrow"),
            P("grp", "wide"),
            P(("grp", "narrow"), "wide"),
            P(("grp", "wide"), "narrow"),
        ),
        out_specs=P(("grp", "wide"), "narrow"),
        check_vma=False,
    )
```

```python
import jax
import jax.numpy as jnp
from jax import lax
from jax.experimental import pallas as pl
from jax.experimental.pallas import tpu as pltpu
from jax.sharding import PartitionSpec as P

EX = 2
LINE, PAIR = 4, 2
DEEP = 1024
VMEM = 20 << 20
BF16, F32 = jnp.bfloat16, jnp.float32


def dot(a, b):
    return jnp.dot(a, b, preferred_element_type=F32)


def fit_kernel(sizes, choices, order_ref, end_ref, place_ref, *refs):
    sum_refs, refs = refs[: 2 * len(sizes)], refs[2 * len(sizes) :]
    piece_refs, (fit_ref, out_ref, turned_ref, rot_ref) = refs[:-4], refs[-4:]
    rows, ks = out_ref.shape
    size, seq = rows // order_ref.shape[0], rows // EX

    @pl.when(pl.program_id(0) == 0)
    def _():
        at = 0
        for piece, choice in enumerate(choices):
            width = piece_refs[at].shape[1]
            there = pl.ds(pl.multiple_of(place_ref[piece] * width, width), width)
            if choice == 1:
                out_ref[:, there] = piece_refs[at][...]
            else:
                out_ref[:, there] = jnp.where(end_ref[0] == 1, piece_refs[at][...], piece_refs[at + 1][...])
            at += choice

    slot = 0
    for mine_ref, other_ref in zip(sum_refs[::2], sum_refs[1::2]):
        for at in range(0, mine_ref.shape[0], size):
            here = pl.ds(at, size)
            there = pl.ds(pl.multiple_of(order_ref[slot] * size, size), size)
            rot_ref[there, :] = mine_ref[here, :] + other_ref[here, :]
            slot += 1
    turned_ref[...] = rot_ref[...].T.astype(BF16)
    step = min(512, ks)
    for at in range(0, ks, step):
        total = None
        for e in range(EX):
            here = pl.ds(e * seq, seq)
            grad = dot(turned_ref[:, here], out_ref[here, pl.ds(at, step)])
            total = grad * grad if total is None else total + grad * grad
        fit_ref[:, pl.ds(at, step)] = total * (1.0 / EX)


def fit(order, end, sums, pieces, places):
    rows = sum(mine.shape[0] for mine, _ in sums)
    ka = sums[0][0].shape[1]
    ks = sum(piece[0].shape[1] for piece in pieces)
    tile = 256 if ka % 256 == 0 else ka
    flat = [a for pair in sums for a in pair]
    outs = [a for piece in pieces for a in piece]
    return pl.pallas_call(
        lambda *refs: fit_kernel([pair[0].shape[0] for pair in sums], [len(piece) for piece in pieces], *refs),
        out_shape=jax.ShapeDtypeStruct((ka, ks), F32),
        grid_spec=pltpu.PrefetchScalarGridSpec(
            num_scalar_prefetch=3,
            grid=(ka // tile,),
            in_specs=[pl.BlockSpec((a.shape[0], tile), lambda i, *_: (0, i)) for a in flat]
            + [pl.BlockSpec(a.shape, lambda i, *_: (0, 0)) for a in outs],
            out_specs=pl.BlockSpec((tile, ks), lambda i, *_: (i, 0)),
            scratch_shapes=[
                pltpu.VMEM((rows, ks), BF16),
                pltpu.VMEM((tile, rows), BF16),
                pltpu.VMEM((rows, tile), F32),
            ],
        ),
        compiler_params=pltpu.CompilerParams(vmem_limit_bytes=56 << 20),
        cost_estimate=pl.CostEstimate(
            flops=2 * rows * ka * ks, bytes_accessed=8 * rows * ka + 2 * rows * ks + 4 * ka * ks, transcendentals=0
        ),
        name="fit",
    )(order, end, places, *flat, *outs)


def rotate_kernel(choices, end_ref, *refs):
    blocks = refs[: sum(choices)]
    basis_ref, *before, sum_ref, rows_ref = refs[sum(choices) :]
    size = blocks[0].shape[0]
    at = 0
    for i, choice in enumerate(choices):
        here = pl.ds(i * size, size)
        if choice == 1:
            rows_ref[here, :] = blocks[at][...]
        else:
            rows_ref[here, :] = jnp.where(end_ref[0] == 1, blocks[at][...], blocks[at + 1][...])
        at += choice

    @pl.when(pl.program_id(0) == 0)
    def _():
        sum_ref[...] = before[0][...] if before else jnp.zeros_like(sum_ref)

    sum_ref[...] += dot(rows_ref[...], basis_ref[...])


def rotate(before, end, blocks, basis, first, steps):
    flat = [pair for block in blocks for pair in block]
    size, ka = flat[0][0].shape[0], basis.shape[1]
    rows = size * len(blocks)
    specs = []
    for block in blocks:
        for which, (_, skip) in enumerate(block):
            used = lambda e, which=which, n=len(block): 1 if n == 1 else jnp.where(e[0] == 1, 1 - which, which)
            specs.append(
                pl.BlockSpec((size, DEEP), lambda k, e, used=used, skip=skip: (0, (k + skip) * used(e)))
            )
    whole = pl.BlockSpec((rows, ka), lambda k, e: (0, 0))
    arrays = [a for a, _ in flat] + [basis] + ([] if before is None else [before])
    return pl.pallas_call(
        lambda *refs: rotate_kernel([len(block) for block in blocks], *refs),
        out_shape=jax.ShapeDtypeStruct((rows, ka), F32),
        grid_spec=pltpu.PrefetchScalarGridSpec(
            num_scalar_prefetch=1,
            grid=(steps,),
            in_specs=specs
            + [pl.BlockSpec((DEEP, ka), lambda k, e: (first + k, 0))]
            + ([] if before is None else [whole]),
            out_specs=whole,
            scratch_shapes=[pltpu.VMEM((rows, DEEP), BF16)],
        ),
        compiler_params=pltpu.CompilerParams(vmem_limit_bytes=VMEM),
        cost_estimate=pl.CostEstimate(
            flops=rows * ka, bytes_accessed=4 * rows * ka, transcendentals=0
        ),
        name="rotate",
    )(end, *arrays)


def swap_narrow(a):
    return lax.ppermute(a, "narrow", [(0, 1), (1, 0)])


def general(inputs, deltas, basis_in, basis_out):
    partial_in = dot(lax.all_gather(inputs, "wide", axis=0, tiled=True), basis_in)
    rotated_out = lax.psum(dot(deltas, basis_out), "wide").astype(BF16)
    order, zero = jnp.arange(EX, dtype=jnp.int32), jnp.zeros((1,), jnp.int32)
    return fit(order, zero, [(partial_in, swap_narrow(partial_in))], [[rotated_out]], zero)


def pairs(step, where=lambda z: True):
    out = []
    for z in range(LINE):
        for x in range(PAIR):
            if where(z):
                tz, tx = step(z, x)
                out.append((z * PAIR + x, tz * PAIR + tx))
    return out


def corner(z):
    return z in (0, LINE - 1)


def middle(z):
    return not corner(z)


ENDS = pairs(lambda z, x: (z ^ 1, x))
TO_ENDS = pairs(lambda z, x: (z ^ 1, x), middle)
FROM_ENDS = pairs(lambda z, x: (z ^ 1, x), corner)
MIDDLE = pairs(lambda z, x: (3 - z, x), middle)
ACROSS = pairs(lambda z, x: (z, 1 - x))
ACROSS_ENDS = pairs(lambda z, x: (z, 1 - x), corner)
ACROSS_MIDDLE = pairs(lambda z, x: (z, 1 - x), middle)


def send(a, perm):
    return lax.ppermute(a, "wide", perm)


def scheduled(inputs, deltas, basis_in, basis_out):
    w = lax.axis_index("wide")
    z, x = w // PAIR, w % PAIR
    at_end = (z == 0) | (z == LINE - 1)
    end = at_end.astype(jnp.int32).reshape(1)
    half = (z >= 2).astype(jnp.int32)
    steps = inputs.shape[1] // DEEP
    cuts = [0, 4 * steps // 14, 8 * steps // 14, 12 * steps // 14, steps]
    part = basis_out.shape[1] // 4
    got = {"own": inputs}

    def fence(*names):
        got.update(zip(names, lax.optimization_barrier(tuple(got[n] for n in names))))

    def pick(a, b):
        return jnp.where(at_end, got[a], got[b])

    def columns(a, h):
        return lax.dynamic_slice_in_dim(a, h * 2 * part, 2 * part, 1)

    def turn(before, blocks, first, count):
        return rotate(before, end, [[(got[n], first) for n in block] for block in blocks], basis_in, first, count)

    def settle(p):
        got["sum", p] = (got["keep", p] + got["x5", p].astype(F32)).astype(BF16)
        got["m4", p] = send(got["sum", p], MIDDLE)
        got["n1", p] = send(got["sum", p], TO_ENDS)

    flip = jnp.where(z >= 2, 3, 0)
    line = lambda a, b: jnp.where(at_end, a, b) ^ flip
    mine, other = (lambda a, b: line(a, b) * PAIR + x), (lambda a, b: line(a, b) * PAIR + 1 - x)
    order = [mine(0, 1), mine(1, 0), other(0, 1), mine(2, 2), other(1, 2), mine(3, 3), other(2, 0), other(3, 3)]
    got["order"] = jnp.stack(order).astype(jnp.int32)
    places = [2 * half, 2 * half + 1, 2 - 2 * half, 3 - 2 * half]
    got["places"] = jnp.stack(places).astype(jnp.int32)

    got["x1"] = send(got["own"], ACROSS)
    got["a1"] = send(got["own"], ENDS)
    got["m1"] = send(got["own"], MIDDLE)
    got["give"] = dot(deltas, columns(basis_out, 1 - half))
    got["r1", 0] = send(got["give"].astype(BF16), FROM_ENDS)
    got["keep"] = dot(deltas, columns(basis_out, half))
    got["keep16"] = got["keep"].astype(BF16)
    fence("x1", "a1", "m1", "give", "keep", "keep16", "order", "places")
    got["pick"] = pick("a1", "m1")
    fence("pick", "a1", "m1", "x1")
    got["x2"] = send(got["pick"], ACROSS)
    got["a2"] = send(got["m1"], TO_ENDS)
    got["m2"] = send(got["a1"], MIDDLE)
    fence(("r1", 0), "x1", "give", "keep16")
    got["r1", 1] = send(got["keep16"], FROM_ENDS)
    got["give"] += got["r1", 0].astype(F32)
    for p in range(2):
        got["give", p] = got["give"][:, p * part : (p + 1) * part]
    got["A"] = turn(None, [["own"], ["a1"], ["x1"]], 0, steps)
    fence("x1", "x2", "a2", "m2", ("give", 0), ("give", 1), "keep", ("r1", 1), "A")
    got["x3"] = send(got["a2"], ACROSS_ENDS)
    got["a3"] = send(got["m2"], TO_ENDS)
    for p in range(2):
        got["m3", p] = send(got["give", p], MIDDLE)
    got["e"] = send(got["x1"], FROM_ENDS)
    got["keep"] += got["r1", 1].astype(F32)
    some = steps // 2
    got["B"] = turn(None, [["a2", "m1"], ["x2"]], 0, some)
    fence(("m3", 0), "keep", "B")

    def cross(p):
        got["keep", p] = got["keep"][:, p * part : (p + 1) * part] + got["m3", p]
        got["x5", p] = send(got["keep", p].astype(BF16), ACROSS_MIDDLE)

    cross(0)
    got["B"] = turn(got["B"], [["a2", "m1"], ["x2"]], some, steps - some)
    fence("x3", "a3", "e", ("x5", 0), "B")

    def x4(piece):
        here = slice(cuts[piece] * DEEP, cuts[piece + 1] * DEEP)
        got["x4", piece] = send(jnp.where(at_end, got["a3"][:, here], got["m2"][:, here]), ACROSS)

    def last(piece):
        first = cuts[piece]
        blocks = [[(got["a3"], first), (got["m2"], first)], [(got["x3"], first), (got["e"], first)], [(got["x4", piece], 0)]]
        got["D"] = rotate(got.get("D"), end, blocks, basis_in, first, cuts[piece + 1] - first)

    x4(0)
    settle(0)
    fence(("m3", 1), "a3", "m2")
    cross(1)
    fence(("x4", 0), ("m4", 0), ("n1", 0), "a3", "m2")
    x4(1)
    got["n2", 0] = send(got["m4", 0], TO_ENDS)
    last(0)
    fence(("x4", 1), ("x5", 1), "D", "a3", "m2")
    x4(2)
    settle(1)
    last(1)
    fence(("x4", 2), ("m4", 1), ("n2", 0), "A", "B", "D", "a3", "m2")
    x4(3)
    got["n2", 1] = send(got["m4", 1], TO_ENDS)
    got["A2"] = swap_narrow(got["A"])
    got["B2"] = swap_narrow(got["B"])
    last(2)
    fence(("x4", 3), ("n1", 1), ("n2", 1), "A2", "B2", "D")
    last(3)
    got["D2"] = swap_narrow(got["D"])

    pieces = [[got["n1", p], got["sum", p]] for p in range(2)] + [[got["n2", p], got["m4", p]] for p in range(2)]
    sums = [(got[n], got[n + "2"]) for n in "ABD"]
    return fit(got["order"], end, sums, pieces, got["places"])


def solution(mesh):
    return jax.shard_map(
        scheduled if mesh.shape["wide"] == LINE * PAIR else general,
        mesh=mesh,
        in_specs=(
            P(("grp", "wide"), "narrow"),
            P("grp", "wide"),
            P(("grp", "narrow"), "wide"),
            P(("grp", "wide"), "narrow"),
        ),
        out_specs=P(("grp", "wide"), "narrow"),
        check_vma=False,
    )
```

```python
import jax
import jax.numpy as jnp
from jax import lax
from jax.experimental import pallas as pl
from jax.experimental.pallas import tpu as pltpu
from jax.sharding import PartitionSpec as P

EX = 2
LINE, PAIR = 4, 2
DEEP = 1024
VMEM = 20 << 20
BF16, F32 = jnp.bfloat16, jnp.float32


def dot(a, b):
    return jnp.dot(a, b, preferred_element_type=F32)


def fit_kernel(count, choices, order_ref, end_ref, place_ref, *refs):
    sum_refs, refs = refs[: 2 * count], refs[2 * count :]
    piece_refs, (fit_ref, out_ref, turned_ref, rot_ref) = refs[:-4], refs[-4:]
    rows = rot_ref.shape[0]
    size, seq = rows // order_ref.shape[0], rows // EX
    i, j = pl.program_id(0), pl.program_id(1)

    at = 0
    for piece, choice in enumerate(choices):

        @pl.when((i == 0) & (j == piece))
        def _(at=at, piece=piece, choice=choice):
            if choice == 1:
                out_ref[piece] = piece_refs[at][...]
            else:
                out_ref[piece] = jnp.where(end_ref[0] == 1, piece_refs[at][...], piece_refs[at + 1][...])

        at += choice

    @pl.when(j == 0)
    def _():
        slot = 0
        for mine_ref, other_ref in zip(sum_refs[::2], sum_refs[1::2]):
            for at in range(0, mine_ref.shape[0], size):
                here = pl.ds(at, size)
                there = pl.ds(pl.multiple_of(order_ref[slot] * size, size), size)
                rot_ref[there, :] = mine_ref[here, :] + other_ref[here, :]
                slot += 1
        turned_ref[...] = rot_ref[...].T.astype(BF16)

    total = None
    for e in range(EX):
        here = pl.ds(e * seq, seq)
        grad = dot(turned_ref[:, here], out_ref[j, here, :])
        total = grad * grad if total is None else total + grad * grad
    fit_ref[...] = total * (1.0 / EX)


def fit(order, end, sums, pieces, places):
    rows = sum(mine.shape[0] for mine, _ in sums)
    ka, part = sums[0][0].shape[1], pieces[0][0].shape[1]
    ks = len(pieces) * part
    tile = 896 if ka % 896 == 0 else ka
    flat = [a for pair in sums for a in pair]
    outs = [a for piece in pieces for a in piece]
    return pl.pallas_call(
        lambda *refs: fit_kernel(len(sums), [len(piece) for piece in pieces], *refs),
        out_shape=jax.ShapeDtypeStruct((ka, ks), F32),
        grid_spec=pltpu.PrefetchScalarGridSpec(
            num_scalar_prefetch=3,
            grid=(ka // tile, len(pieces)),
            in_specs=[pl.BlockSpec((a.shape[0], tile), lambda i, j, *_: (0, i)) for a in flat]
            + [pl.BlockSpec(a.shape, lambda i, j, *_: (0, 0)) for a in outs],
            out_specs=pl.BlockSpec((tile, part), lambda i, j, order, end, places: (i, places[j])),
            scratch_shapes=[
                pltpu.VMEM((len(pieces), rows, part), BF16),
                pltpu.VMEM((tile, rows), BF16),
                pltpu.VMEM((rows, tile), F32),
            ],
        ),
        compiler_params=pltpu.CompilerParams(vmem_limit_bytes=56 << 20),
        cost_estimate=pl.CostEstimate(
            flops=2 * rows * ka * ks, bytes_accessed=8 * rows * ka + 2 * rows * ks + 4 * ka * ks, transcendentals=0
        ),
        name="fit",
    )(order, end, places, *flat, *outs)


def rotate_kernel(choices, end_ref, *refs):
    blocks = refs[: sum(choices)]
    basis_ref, *before, sum_ref, rows_ref = refs[sum(choices) :]
    size = blocks[0].shape[0]
    at = 0
    for i, choice in enumerate(choices):
        here = pl.ds(i * size, size)
        if choice == 1:
            rows_ref[here, :] = blocks[at][...]
        else:
            rows_ref[here, :] = jnp.where(end_ref[0] == 1, blocks[at][...], blocks[at + 1][...])
        at += choice

    @pl.when(pl.program_id(0) == 0)
    def _():
        sum_ref[...] = before[0][...] if before else jnp.zeros_like(sum_ref)

    sum_ref[...] += dot(rows_ref[...], basis_ref[...])


def rotate(before, end, blocks, basis, first, steps):
    flat = [pair for block in blocks for pair in block]
    size, ka = flat[0][0].shape[0], basis.shape[1]
    rows = size * len(blocks)
    specs = []
    for block in blocks:
        for which, (_, skip) in enumerate(block):
            used = lambda e, which=which, n=len(block): 1 if n == 1 else jnp.where(e[0] == 1, 1 - which, which)
            specs.append(
                pl.BlockSpec((size, DEEP), lambda k, e, used=used, skip=skip: (0, (k + skip) * used(e)))
            )
    whole = pl.BlockSpec((rows, ka), lambda k, e: (0, 0))
    arrays = [a for a, _ in flat] + [basis] + ([] if before is None else [before])
    return pl.pallas_call(
        lambda *refs: rotate_kernel([len(block) for block in blocks], *refs),
        out_shape=jax.ShapeDtypeStruct((rows, ka), F32),
        grid_spec=pltpu.PrefetchScalarGridSpec(
            num_scalar_prefetch=1,
            grid=(steps,),
            in_specs=specs
            + [pl.BlockSpec((DEEP, ka), lambda k, e: (first + k, 0))]
            + ([] if before is None else [whole]),
            out_specs=whole,
            scratch_shapes=[pltpu.VMEM((rows, DEEP), BF16)],
        ),
        compiler_params=pltpu.CompilerParams(vmem_limit_bytes=VMEM),
        cost_estimate=pl.CostEstimate(
            flops=rows * ka, bytes_accessed=4 * rows * ka, transcendentals=0
        ),
        name="rotate",
    )(end, *arrays)


def swap_narrow(a):
    return lax.ppermute(a, "narrow", [(0, 1), (1, 0)])


def general(inputs, deltas, basis_in, basis_out):
    partial_in = dot(lax.all_gather(inputs, "wide", axis=0, tiled=True), basis_in)
    rotated_out = lax.psum(dot(deltas, basis_out), "wide").astype(BF16)
    order, zero = jnp.arange(EX, dtype=jnp.int32), jnp.zeros((1,), jnp.int32)
    return fit(order, zero, [(partial_in, swap_narrow(partial_in))], [[rotated_out]], zero)


def pairs(step, where=lambda z: True):
    out = []
    for z in range(LINE):
        for x in range(PAIR):
            if where(z):
                tz, tx = step(z, x)
                out.append((z * PAIR + x, tz * PAIR + tx))
    return out


def corner(z):
    return z in (0, LINE - 1)


def middle(z):
    return not corner(z)


ENDS = pairs(lambda z, x: (z ^ 1, x))
TO_ENDS = pairs(lambda z, x: (z ^ 1, x), middle)
FROM_ENDS = pairs(lambda z, x: (z ^ 1, x), corner)
MIDDLE = pairs(lambda z, x: (3 - z, x), middle)
ACROSS = pairs(lambda z, x: (z, 1 - x))
ACROSS_ENDS = pairs(lambda z, x: (z, 1 - x), corner)
ACROSS_MIDDLE = pairs(lambda z, x: (z, 1 - x), middle)


def send(a, perm):
    return lax.ppermute(a, "wide", perm)


def scheduled(inputs, deltas, basis_in, basis_out):
    w = lax.axis_index("wide")
    z, x = w // PAIR, w % PAIR
    at_end = (z == 0) | (z == LINE - 1)
    end = at_end.astype(jnp.int32).reshape(1)
    half = (z >= 2).astype(jnp.int32)
    steps = inputs.shape[1] // DEEP
    cuts = [0, 6 * steps // 14, 11 * steps // 14, steps]
    part = basis_out.shape[1] // 4
    got = {"own": inputs}

    def fence(*names):
        got.update(zip(names, lax.optimization_barrier(tuple(got[n] for n in names))))

    def pick(a, b):
        return jnp.where(at_end, got[a], got[b])

    def columns(a, h):
        return lax.dynamic_slice_in_dim(a, h * 2 * part, 2 * part, 1)

    def turn(before, blocks, first, count):
        return rotate(before, end, [[(got[n], first) for n in block] for block in blocks], basis_in, first, count)

    def settle(p):
        got["sum", p] = (got["keep", p] + got["x5", p].astype(F32)).astype(BF16)
        got["m4", p] = send(got["sum", p], MIDDLE)
        got["n1", p] = send(got["sum", p], TO_ENDS)

    flip = jnp.where(z >= 2, 3, 0)
    line = lambda a, b: jnp.where(at_end, a, b) ^ flip
    mine, other = (lambda a, b: line(a, b) * PAIR + x), (lambda a, b: line(a, b) * PAIR + 1 - x)
    order = [mine(0, 1), mine(1, 0), other(0, 1), mine(2, 2), other(1, 2), mine(3, 3), other(2, 0), other(3, 3)]
    got["order"] = jnp.stack(order).astype(jnp.int32)
    places = [2 * half, 2 * half + 1, 2 - 2 * half, 3 - 2 * half]
    got["places"] = jnp.stack(places).astype(jnp.int32)

    got["x1"] = send(got["own"], ACROSS)
    got["a1"] = send(got["own"], ENDS)
    got["m1"] = send(got["own"], MIDDLE)
    got["give"] = dot(deltas, columns(basis_out, 1 - half))
    got["r1", 0] = send(got["give"].astype(BF16), FROM_ENDS)
    got["keep"] = dot(deltas, columns(basis_out, half))
    got["keep16"] = got["keep"].astype(BF16)
    fence("x1", "a1", "m1", "give", "keep", "keep16", "order", "places")
    got["pick"] = pick("a1", "m1")
    fence("pick", "a1", "m1", "x1")
    got["x2"] = send(got["pick"], ACROSS)
    got["a2"] = send(got["m1"], TO_ENDS)
    got["m2"] = send(got["a1"], MIDDLE)
    fence(("r1", 0), "x1", "give", "keep16")
    got["r1", 1] = send(got["keep16"], FROM_ENDS)
    got["give"] += got["r1", 0].astype(F32)
    for p in range(2):
        got["give", p] = got["give"][:, p * part : (p + 1) * part]
    got["A"] = turn(None, [["own"], ["a1"], ["x1"]], 0, steps)
    fence("x1", "x2", "a2", "m2", ("give", 0), ("give", 1), "keep", ("r1", 1), "A")
    got["x3"] = send(got["a2"], ACROSS_ENDS)
    got["a3"] = send(got["m2"], TO_ENDS)
    for p in range(2):
        got["m3", p] = send(got["give", p], MIDDLE)
    got["e"] = send(got["x1"], FROM_ENDS)
    got["keep"] += got["r1", 1].astype(F32)
    some = steps // 2
    got["B"] = turn(None, [["a2", "m1"], ["x2"]], 0, some)
    fence(("m3", 0), "keep", "B")

    def cross(p):
        got["keep", p] = got["keep"][:, p * part : (p + 1) * part] + got["m3", p]
        got["x5", p] = send(got["keep", p].astype(BF16), ACROSS_MIDDLE)

    cross(0)
    got["B"] = turn(got["B"], [["a2", "m1"], ["x2"]], some, steps - some)
    fence("x3", "a3", "e", ("x5", 0), ("m3", 1), "B")

    def x4(piece):
        here = slice(cuts[piece] * DEEP, cuts[piece + 1] * DEEP)
        got["x4", piece] = send(jnp.where(at_end, got["a3"][:, here], got["m2"][:, here]), ACROSS)

    def last(piece):
        first = cuts[piece]
        blocks = [[(got["a3"], first), (got["m2"], first)], [(got["x3"], first), (got["e"], first)], [(got["x4", piece], 0)]]
        got["D"] = rotate(got.get("D"), end, blocks, basis_in, first, cuts[piece + 1] - first)

    cross(1)
    settle(0)
    x4(0)
    fence(("x5", 1), ("m4", 0), ("n1", 0), ("sum", 0))
    settle(1)
    got["n2", 0] = send(got["m4", 0], TO_ENDS)
    got["R", 0] = pick(("n1", 0), ("sum", 0))
    fence(("x4", 0), ("m4", 1), ("n1", 1), ("sum", 1), ("R", 0), "a3", "m2")
    got["n2", 1] = send(got["m4", 1], TO_ENDS)
    x4(1)
    got["R", 1] = pick(("n1", 1), ("sum", 1))
    last(0)
    fence(("x4", 1), ("n2", 0), ("m4", 0), ("R", 1), "A", "B", "D", "a3", "m2")
    x4(2)
    got["A2"] = swap_narrow(got["A"])
    got["B2"] = swap_narrow(got["B"])
    got["R", 2] = pick(("n2", 0), ("m4", 0))
    last(1)
    fence(("x4", 2), ("n2", 1), ("R", 2), "A2", "B2", "D")
    last(2)
    got["D2"] = swap_narrow(got["D"])

    pieces = [[got["R", p]] for p in range(3)] + [[got["n2", 1], got["m4", 1]]]
    sums = [(got[n], got[n + "2"]) for n in "ABD"]
    return fit(got["order"], end, sums, pieces, got["places"])


def solution(mesh):
    return jax.shard_map(
        scheduled if mesh.shape["wide"] == LINE * PAIR else general,
        mesh=mesh,
        in_specs=(
            P(("grp", "wide"), "narrow"),
            P("grp", "wide"),
            P(("grp", "narrow"), "wide"),
            P(("grp", "wide"), "narrow"),
        ),
        out_specs=P(("grp", "wide"), "narrow"),
        check_vma=False,
    )
```

```python
import jax
import jax.numpy as jnp
from jax import lax
from jax.experimental import pallas as pl
from jax.experimental.pallas import tpu as pltpu
from jax.sharding import PartitionSpec as P

EX = 2
LINE, PAIR = 4, 2
DEEP = 1024
VMEM = 20 << 20
BF16, F32 = jnp.bfloat16, jnp.float32


def dot(a, b):
    return jnp.dot(a, b, preferred_element_type=F32)


def fit_kernel(counts, choices, order_ref, end_ref, place_ref, *refs):
    sum_refs, refs = refs[: sum(counts)], refs[sum(counts) :]
    piece_refs, (fit_ref, out_ref, turned_ref, rot_ref) = refs[:-4], refs[-4:]
    rows, ks = out_ref.shape
    size, seq = rows // order_ref.shape[0], rows // EX

    @pl.when(pl.program_id(0) == 0)
    def _():
        at = 0
        for piece, choice in enumerate(choices):
            width = piece_refs[at].shape[1]
            there = pl.ds(pl.multiple_of(place_ref[piece] * width, width), width)
            if choice == 1:
                out_ref[:, there] = piece_refs[at][...]
            else:
                out_ref[:, there] = jnp.where(end_ref[0] == 1, piece_refs[at][...], piece_refs[at + 1][...])
            at += choice

    slot, first = 0, 0
    for count in counts:
        halves = sum_refs[first : first + count]
        first += count
        for at in range(0, halves[0].shape[0], size):
            here = pl.ds(at, size)
            there = pl.ds(pl.multiple_of(order_ref[slot] * size, size), size)
            rot_ref[there, :] = sum(ref[here, :] for ref in halves).astype(BF16)
            slot += 1
    turned_ref[...] = rot_ref[...].T
    step = min(512, ks)
    for at in range(0, ks, step):
        total = None
        for e in range(EX):
            here = pl.ds(e * seq, seq)
            grad = dot(turned_ref[:, here], out_ref[here, pl.ds(at, step)])
            total = grad * grad if total is None else total + grad * grad
        fit_ref[:, pl.ds(at, step)] = total * (1.0 / EX)


def fit(order, end, sums, pieces, places):
    rows = sum(halves[0].shape[0] for halves in sums)
    ka = sums[0][0].shape[1]
    ks = sum(piece[0].shape[1] for piece in pieces)
    tile = 256 if ka % 256 == 0 else ka
    flat = [a for halves in sums for a in halves]
    outs = [a for piece in pieces for a in piece]
    return pl.pallas_call(
        lambda *refs: fit_kernel([len(halves) for halves in sums], [len(piece) for piece in pieces], *refs),
        out_shape=jax.ShapeDtypeStruct((ka, ks), F32),
        grid_spec=pltpu.PrefetchScalarGridSpec(
            num_scalar_prefetch=3,
            grid=(ka // tile,),
            in_specs=[pl.BlockSpec((a.shape[0], tile), lambda i, *_: (0, i)) for a in flat]
            + [pl.BlockSpec(a.shape, lambda i, *_: (0, 0)) for a in outs],
            out_specs=pl.BlockSpec((tile, ks), lambda i, *_: (i, 0)),
            scratch_shapes=[
                pltpu.VMEM((rows, ks), BF16),
                pltpu.VMEM((tile, rows), BF16),
                pltpu.VMEM((rows, tile), BF16),
            ],
        ),
        compiler_params=pltpu.CompilerParams(vmem_limit_bytes=56 << 20),
        cost_estimate=pl.CostEstimate(
            flops=2 * rows * ka * ks, bytes_accessed=8 * rows * ka + 2 * rows * ks + 4 * ka * ks, transcendentals=0
        ),
        name="fit",
    )(order, end, places, *flat, *outs)


def rotate_kernel(choices, end_ref, *refs):
    blocks = refs[: sum(choices)]
    left_ref, right_ref, *before, sum_ref, rows_ref = refs[sum(choices) :]
    size = blocks[0].shape[0]
    at = 0
    for i, choice in enumerate(choices):
        here = pl.ds(i * size, size)
        if choice == 1:
            rows_ref[here, :] = blocks[at][...]
        else:
            rows_ref[here, :] = jnp.where(end_ref[0] == 1, blocks[at][...], blocks[at + 1][...])
        at += choice

    @pl.when(pl.program_id(0) == 0)
    def _():
        sum_ref[...] = before[0][...] if before else jnp.zeros_like(sum_ref)

    half = left_ref.shape[1]
    sum_ref[:, :half] += dot(rows_ref[...], left_ref[...])
    sum_ref[:, half:] += dot(rows_ref[...], right_ref[...])


def rotate(before, end, blocks, basis, first, steps):
    flat = [pair for block in blocks for pair in block]
    size, ka = flat[0][0].shape[0], basis.shape[1]
    rows = size * len(blocks)
    specs = []
    for block in blocks:
        for which, (_, skip) in enumerate(block):
            used = lambda e, which=which, n=len(block): 1 if n == 1 else jnp.where(e[0] == 1, 1 - which, which)
            specs.append(
                pl.BlockSpec((size, DEEP), lambda k, e, used=used, skip=skip: (0, (k + skip) * used(e)))
            )
    whole = pl.BlockSpec((rows, ka), lambda k, e: (0, 0))
    arrays = [a for a, _ in flat] + [basis, basis] + ([] if before is None else [before])
    return pl.pallas_call(
        lambda *refs: rotate_kernel([len(block) for block in blocks], *refs),
        out_shape=jax.ShapeDtypeStruct((rows, ka), F32),
        grid_spec=pltpu.PrefetchScalarGridSpec(
            num_scalar_prefetch=1,
            grid=(steps,),
            in_specs=specs
            + [pl.BlockSpec((DEEP, ka // 2), lambda k, e, side=side: (first + k, side)) for side in range(2)]
            + ([] if before is None else [whole]),
            out_specs=whole,
            scratch_shapes=[pltpu.VMEM((rows, DEEP), BF16)],
        ),
        compiler_params=pltpu.CompilerParams(vmem_limit_bytes=VMEM),
        cost_estimate=pl.CostEstimate(
            flops=rows * ka, bytes_accessed=4 * rows * ka, transcendentals=0
        ),
        name="rotate",
    )(end, *arrays)


def swap_narrow(a):
    return lax.ppermute(a, "narrow", [(0, 1), (1, 0)])


def general(inputs, deltas, basis_in, basis_out):
    partial_in = dot(lax.all_gather(inputs, "wide", axis=0, tiled=True), basis_in)
    rotated_out = lax.psum(dot(deltas, basis_out), "wide").astype(BF16)
    order, zero = jnp.arange(EX, dtype=jnp.int32), jnp.zeros((1,), jnp.int32)
    return fit(order, zero, [(partial_in, swap_narrow(partial_in))], [[rotated_out]], zero)


def pairs(step, where=lambda z: True):
    out = []
    for z in range(LINE):
        for x in range(PAIR):
            if where(z):
                tz, tx = step(z, x)
                out.append((z * PAIR + x, tz * PAIR + tx))
    return out


def corner(z):
    return z in (0, LINE - 1)


def middle(z):
    return not corner(z)


ENDS = pairs(lambda z, x: (z ^ 1, x))
TO_ENDS = pairs(lambda z, x: (z ^ 1, x), middle)
FROM_ENDS = pairs(lambda z, x: (z ^ 1, x), corner)
MIDDLE = pairs(lambda z, x: (3 - z, x), middle)
ACROSS = pairs(lambda z, x: (z, 1 - x))
ACROSS_ENDS = pairs(lambda z, x: (z, 1 - x), corner)
ACROSS_MIDDLE = pairs(lambda z, x: (z, 1 - x), middle)


def send(a, perm):
    return lax.ppermute(a, "wide", perm)


def scheduled(inputs, deltas, basis_in, basis_out):
    w = lax.axis_index("wide")
    z, x = w // PAIR, w % PAIR
    at_end = (z == 0) | (z == LINE - 1)
    end = at_end.astype(jnp.int32).reshape(1)
    half = (z >= 2).astype(jnp.int32)
    steps = inputs.shape[1] // DEEP
    cuts = [0, 4 * steps // 14, 9 * steps // 14, steps]
    part = basis_out.shape[1] // 4
    got = {"own": inputs}

    def fence(*names):
        got.update(zip(names, lax.optimization_barrier(tuple(got[n] for n in names))))

    def pick(a, b):
        return jnp.where(at_end, got[a], got[b])

    def columns(a, h):
        return lax.dynamic_slice_in_dim(a, h * 2 * part, 2 * part, 1)

    def turn(before, blocks, first, count):
        return rotate(before, end, [[(got[n], first) for n in block] for block in blocks], basis_in, first, count)

    def settle(p):
        got["sum", p] = (got["keep", p] + got["x5", p].astype(F32)).astype(BF16)
        got["m4", p] = send(got["sum", p], MIDDLE)
        got["n1", p] = send(got["sum", p], TO_ENDS)

    flip = jnp.where(z >= 2, 3, 0)
    line = lambda a, b: jnp.where(at_end, a, b) ^ flip
    mine, other = (lambda a, b: line(a, b) * PAIR + x), (lambda a, b: line(a, b) * PAIR + 1 - x)
    order = [mine(0, 1), mine(1, 0), other(0, 1), mine(2, 2), other(1, 2), mine(3, 3), other(2, 3), other(3, 0)]
    got["order"] = jnp.stack(order).astype(jnp.int32)
    places = [2 * half, 2 * half + 1, 2 - 2 * half, 3 - 2 * half]
    got["places"] = jnp.stack(places).astype(jnp.int32)

    got["x1"] = send(got["own"], ACROSS)
    got["a1"] = send(got["own"], ENDS)
    got["m1"] = send(got["own"], MIDDLE)
    got["give"] = dot(deltas, columns(basis_out, 1 - half))
    got["r1", 0] = send(got["give"].astype(BF16), FROM_ENDS)
    got["keep"] = dot(deltas, columns(basis_out, half))
    got["keep16"] = got["keep"].astype(BF16)
    fence("x1", "a1", "m1", "give", "keep", "keep16", "order", "places")
    got["x2"] = send(got["a1"], ACROSS_ENDS)
    got["x2", "m"] = send(got["m1"], ACROSS_MIDDLE)
    got["a2"] = send(got["m1"], TO_ENDS)
    got["m2"] = send(got["a1"], MIDDLE)
    fence(("r1", 0), "x1", "give", "keep16")
    got["r1", 1] = send(got["keep16"], FROM_ENDS)
    got["give"] += got["r1", 0].astype(F32)
    for p in range(2):
        got["give", p] = got["give"][:, p * part : (p + 1) * part]
    fence(("give", 0), ("give", 1), "x1")
    got["A"] = turn(None, [["own"], ["a1"], ["x1"]], 0, steps)
    fence("x1", "x2", ("x2", "m"), "a2", "m2", ("give", 0), ("give", 1), "keep", ("r1", 1), "A")
    got["x3"] = send(got["a2"], ACROSS_ENDS)
    got["x3", "m"] = send(got["m2"], ACROSS_MIDDLE)
    got["a3"] = send(got["m2"], TO_ENDS)
    got["m3", 0] = send(got["give", 0], MIDDLE)
    got["e"] = send(got["x1"], FROM_ENDS)
    got["keep"] += got["r1", 1].astype(F32)
    some = steps // 2
    second = [["a2", "m1"], ["x2", ("x2", "m")]]
    got["B"] = turn(None, second, 0, some)
    fence(("m3", 0), ("give", 1), "keep", "B")
    got["m3", 1] = send(got["give", 1], MIDDLE)
    got["B"] = turn(got["B"], second, some, steps - some)
    fence("x3", "B")
    fence(("x3", "m"), "a3", "e", "A", "B", ("m3", 0))

    def x4(piece):
        got["x4", piece] = send(got["a3"][:, cuts[piece] * DEEP : cuts[piece + 1] * DEEP], ACROSS_ENDS)

    def last(piece):
        first = cuts[piece]
        blocks = [["a3", "m2"], ["x3", ("x3", "m")]]
        blocks = [[(got[n], first) for n in b] for b in blocks] + [[(got["x4", piece], 0), (got["e"], first)]]
        got["D"] = rotate(got.get("D"), end, blocks, basis_in, first, cuts[piece + 1] - first)

    def cross(p):
        got["keep", p] = got["keep"][:, p * part : (p + 1) * part] + got["m3", p]
        got["x5", p] = send(got["keep", p].astype(BF16), ACROSS_MIDDLE)

    x4(0)
    cross(0)
    fence(("m3", 1), "A", "B")
    cross(1)
    fence(("x4", 0), ("x5", 0), "a3")
    x4(1)
    settle(0)
    got["A2"] = swap_narrow(got["A"])
    fence(("x5", 1), ("m4", 0), ("n1", 0), ("sum", 0), "A2", ("x4", 0))
    settle(1)
    got["n2", 0] = send(got["m4", 0], TO_ENDS)
    got["B2"] = swap_narrow(got["B"])
    got["A"] = (got["A"] + got["A2"]).astype(BF16)
    got["R", 0] = pick(("n1", 0), ("sum", 0))
    last(0)
    fence(("x4", 1), "A", ("R", 0), "B2", "D", "a3")
    x4(2)
    fence(("m4", 1), ("n1", 1), ("sum", 1), ("x4", 1))
    got["B"] = (got["B"] + got["B2"]).astype(BF16)
    got["R", 1] = pick(("n1", 1), ("sum", 1))
    last(1)
    fence(("x4", 2), ("n2", 0), ("m4", 0), ("R", 1), "B", "D")
    got["n2", 1] = send(got["m4", 1], TO_ENDS)
    got["R", 2] = pick(("n2", 0), ("m4", 0))
    last(2)
    fence(("n2", 1), ("R", 2), "D")
    got["D2"] = swap_narrow(got["D"])

    pieces = [[got["R", p]] for p in range(3)] + [[got["n2", 1], got["m4", 1]]]
    return fit(got["order"], end, [[got["A"]], [got["B"]], [got["D"], got["D2"]]], pieces, got["places"])


def solution(mesh):
    return jax.shard_map(
        scheduled if mesh.shape["wide"] == LINE * PAIR else general,
        mesh=mesh,
        in_specs=(
            P(("grp", "wide"), "narrow"),
            P("grp", "wide"),
            P(("grp", "narrow"), "wide"),
            P(("grp", "wide"), "narrow"),
        ),
        out_specs=P(("grp", "wide"), "narrow"),
        check_vma=False,
    )
```

```python
import jax
import jax.numpy as jnp
from jax import lax
from jax.experimental import pallas as pl
from jax.experimental.pallas import tpu as pltpu
from jax.sharding import PartitionSpec as P

EX = 2
LINE, PAIR = 4, 2
DEEP = 1024
VMEM = 22 << 20
BF16, F32 = jnp.bfloat16, jnp.float32


def dot(a, b):
    return jnp.dot(a, b, preferred_element_type=F32)


def fit_kernel(counts, choices, order_ref, end_ref, place_ref, *refs):
    sum_refs, refs = refs[: sum(counts)], refs[sum(counts) :]
    piece_refs, (fit_ref, out_ref, turned_ref, rot_ref) = refs[:-4], refs[-4:]
    rows, ks = out_ref.shape
    size, seq = rows // order_ref.shape[0], rows // EX

    @pl.when(pl.program_id(0) == 0)
    def _():
        at = 0
        for piece, choice in enumerate(choices):
            width = piece_refs[at].shape[1]
            there = pl.ds(pl.multiple_of(place_ref[piece] * width, width), width)
            if choice == 1:
                out_ref[:, there] = piece_refs[at][...]
            else:
                out_ref[:, there] = jnp.where(end_ref[0] == 1, piece_refs[at][...], piece_refs[at + 1][...])
            at += choice

    slot, first = 0, 0
    for count in counts:
        halves = sum_refs[first : first + count]
        first += count
        for at in range(0, halves[0].shape[0], size):
            here = pl.ds(at, size)
            there = pl.ds(pl.multiple_of(order_ref[slot] * size, size), size)
            rot_ref[there, :] = sum(ref[here, :] for ref in halves).astype(BF16)
            slot += 1
    turned_ref[...] = rot_ref[...].T
    step = min(512, ks)
    for at in range(0, ks, step):
        total = None
        for e in range(EX):
            here = pl.ds(e * seq, seq)
            grad = dot(turned_ref[:, here], out_ref[here, pl.ds(at, step)])
            total = grad * grad if total is None else total + grad * grad
        fit_ref[:, pl.ds(at, step)] = total * (1.0 / EX)


def fit(order, end, sums, pieces, places):
    rows = sum(halves[0].shape[0] for halves in sums)
    ka = sums[0][0].shape[1]
    ks = sum(piece[0].shape[1] for piece in pieces)
    tile = 256 if ka % 256 == 0 else ka
    flat = [a for halves in sums for a in halves]
    outs = [a for piece in pieces for a in piece]
    return pl.pallas_call(
        lambda *refs: fit_kernel([len(halves) for halves in sums], [len(piece) for piece in pieces], *refs),
        out_shape=jax.ShapeDtypeStruct((ka, ks), F32),
        grid_spec=pltpu.PrefetchScalarGridSpec(
            num_scalar_prefetch=3,
            grid=(ka // tile,),
            in_specs=[pl.BlockSpec((a.shape[0], tile), lambda i, *_: (0, i)) for a in flat]
            + [pl.BlockSpec(a.shape, lambda i, *_: (0, 0)) for a in outs],
            out_specs=pl.BlockSpec((tile, ks), lambda i, *_: (i, 0)),
            scratch_shapes=[
                pltpu.VMEM((rows, ks), BF16),
                pltpu.VMEM((tile, rows), BF16),
                pltpu.VMEM((rows, tile), BF16),
            ],
        ),
        compiler_params=pltpu.CompilerParams(vmem_limit_bytes=56 << 20),
        cost_estimate=pl.CostEstimate(
            flops=2 * rows * ka * ks, bytes_accessed=8 * rows * ka + 2 * rows * ks + 4 * ka * ks, transcendentals=0
        ),
        name="fit",
    )(order, end, places, *flat, *outs)


def rotate_kernel(choices, end_ref, *refs):
    blocks = refs[: sum(choices)]
    basis_ref, *before, sum_ref, rows_ref = refs[sum(choices) :]
    size = blocks[0].shape[0]
    at = 0
    for i, choice in enumerate(choices):
        here = pl.ds(i * size, size)
        if choice == 1:
            rows_ref[here, :] = blocks[at][...]
        else:
            rows_ref[here, :] = jnp.where(end_ref[0] == 1, blocks[at][...], blocks[at + 1][...])
        at += choice

    @pl.when(pl.program_id(0) == 0)
    def _():
        if not before:
            sum_ref[...] = jnp.zeros_like(sum_ref)
        at = 0
        for ref in before:
            sum_ref[pl.ds(at, ref.shape[0]), :] = ref[...]
            at += ref.shape[0]

    sum_ref[...] += dot(rows_ref[...], basis_ref[...])


def rotate(before, end, blocks, basis, first, steps):
    flat = [pair for block in blocks for pair in block]
    size, ka = flat[0][0].shape[0], basis.shape[1]
    rows = size * len(blocks)
    specs = []
    for block in blocks:
        for which, (_, skip) in enumerate(block):
            used = lambda e, which=which, n=len(block): 1 if n == 1 else jnp.where(e[0] == 1, 1 - which, which)
            specs.append(
                pl.BlockSpec((size, DEEP), lambda k, e, used=used, skip=skip: (0, (k + skip) * used(e)))
            )
    whole = pl.BlockSpec((rows, ka), lambda k, e: (0, 0))
    arrays = [a for a, _ in flat] + [basis] + before
    return pl.pallas_call(
        lambda *refs: rotate_kernel([len(block) for block in blocks], *refs),
        out_shape=jax.ShapeDtypeStruct((rows, ka), F32),
        grid_spec=pltpu.PrefetchScalarGridSpec(
            num_scalar_prefetch=1,
            grid=(steps,),
            in_specs=specs
            + [pl.BlockSpec((DEEP, ka), lambda k, e: (first + k, 0))]
            + [pl.BlockSpec(a.shape, lambda k, e: (0, 0)) for a in before],
            out_specs=whole,
            scratch_shapes=[pltpu.VMEM((rows, DEEP), BF16)],
        ),
        compiler_params=pltpu.CompilerParams(vmem_limit_bytes=VMEM),
        cost_estimate=pl.CostEstimate(
            flops=rows * ka, bytes_accessed=4 * rows * ka, transcendentals=0
        ),
        name="rotate",
    )(end, *arrays)


def swap_narrow(a):
    return lax.ppermute(a, "narrow", [(0, 1), (1, 0)])


def general(inputs, deltas, basis_in, basis_out):
    partial_in = dot(lax.all_gather(inputs, "wide", axis=0, tiled=True), basis_in)
    rotated_out = lax.psum(dot(deltas, basis_out), "wide").astype(BF16)
    order, zero = jnp.arange(EX, dtype=jnp.int32), jnp.zeros((1,), jnp.int32)
    return fit(order, zero, [(partial_in, swap_narrow(partial_in))], [[rotated_out]], zero)


def pairs(step, where=lambda z: True):
    out = []
    for z in range(LINE):
        for x in range(PAIR):
            if where(z):
                tz, tx = step(z, x)
                out.append((z * PAIR + x, tz * PAIR + tx))
    return out


def corner(z):
    return z in (0, LINE - 1)


def middle(z):
    return not corner(z)


ENDS = pairs(lambda z, x: (z ^ 1, x))
TO_ENDS = pairs(lambda z, x: (z ^ 1, x), middle)
FROM_ENDS = pairs(lambda z, x: (z ^ 1, x), corner)
MIDDLE = pairs(lambda z, x: (3 - z, x), middle)
ACROSS = pairs(lambda z, x: (z, 1 - x))
ACROSS_ENDS = pairs(lambda z, x: (z, 1 - x), corner)
ACROSS_MIDDLE = pairs(lambda z, x: (z, 1 - x), middle)


def send(a, perm):
    return lax.ppermute(a, "wide", perm)


def scheduled(inputs, deltas, basis_in, basis_out):
    w = lax.axis_index("wide")
    z, x = w // PAIR, w % PAIR
    at_end = (z == 0) | (z == LINE - 1)
    end = at_end.astype(jnp.int32).reshape(1)
    half = (z >= 2).astype(jnp.int32)
    steps = inputs.shape[1] // DEEP
    cuts = [0, 5 * steps // 14, 9 * steps // 14, steps]
    part = basis_out.shape[1] // 4
    got = {"own": inputs}

    def fence(*names):
        got.update(zip(names, lax.optimization_barrier(tuple(got[n] for n in names))))

    def pick(a, b):
        return jnp.where(at_end, got[a], got[b])

    def columns(a, h):
        return lax.dynamic_slice_in_dim(a, h * 2 * part, 2 * part, 1)

    def turn(before, blocks, first, count):
        return rotate(before, end, [[(got[n], first) for n in block] for block in blocks], basis_in, first, count)

    def settle(p):
        got["sum", p] = (got["keep", p] + got["x5", p].astype(F32)).astype(BF16)
        got["m4", p] = send(got["sum", p], MIDDLE)
        got["n1", p] = send(got["sum", p], TO_ENDS)

    flip = jnp.where(z >= 2, 3, 0)
    line = lambda a, b: jnp.where(at_end, a, b) ^ flip
    mine, other = (lambda a, b: line(a, b) * PAIR + x), (lambda a, b: line(a, b) * PAIR + 1 - x)
    order = [mine(0, 1), mine(1, 0), other(0, 1), mine(2, 2), other(1, 2), mine(3, 3), other(2, 3), other(3, 0)]
    got["order"] = jnp.stack(order).astype(jnp.int32)
    places = [2 * half, 2 * half + 1, 2 - 2 * half, 3 - 2 * half]
    got["places"] = jnp.stack(places).astype(jnp.int32)

    got["x1"] = send(got["own"], ACROSS)
    got["a1"] = send(got["own"], ENDS)
    got["m1"] = send(got["own"], MIDDLE)
    got["give"] = dot(deltas, columns(basis_out, 1 - half))
    got["r1", 0] = send(got["give"].astype(BF16), FROM_ENDS)
    got["keep"] = dot(deltas, columns(basis_out, half))
    got["keep16"] = got["keep"].astype(BF16)
    fence("x1", "a1", "m1", "give", "keep", "keep16", "order", "places")
    some = steps // 2
    got["x2"] = send(got["a1"], ACROSS_ENDS)
    got["x2", "m"] = send(got["m1"], ACROSS_MIDDLE)
    got["a2"] = send(got["m1"], TO_ENDS)
    got["m2"] = send(got["a1"], MIDDLE)
    blocks = [["own"], ["a1"], ["x1"]]
    got["A"] = turn([], blocks, 0, some)
    fence(("r1", 0), "x1", "give", "keep16", "A")
    got["r1", 1] = send(got["keep16"], FROM_ENDS)
    got["give"] += got["r1", 0].astype(F32)
    fence("x1", "x2", ("x2", "m"), "a2", "m2", "give", "keep", ("r1", 1), "A")
    got["x3"] = send(got["a2"], ACROSS_ENDS)
    got["x3", "m"] = send(got["m2"], ACROSS_MIDDLE)
    got["a3"] = send(got["m2"], TO_ENDS)
    got["m3"] = send(got["give"], MIDDLE)
    got["e"] = send(got["x1"], FROM_ENDS)
    got["keep"] += got["r1", 1].astype(F32)
    more = [["a2", "m1"], ["x2", ("x2", "m")]]
    got["B"] = turn([], more, 0, some)
    got["A"] = turn([got["A"], got["B"]], blocks + more, some, steps - some)
    fence("x3", "A", "keep")
    fence(("x3", "m"), "a3", "e", "A")

    def x4(piece):
        got["x4", piece] = send(got["a3"][:, cuts[piece] * DEEP : cuts[piece + 1] * DEEP], ACROSS_ENDS)

    def last(piece):
        first = cuts[piece]
        blocks = [["a3", "m2"], ["x3", ("x3", "m")]]
        blocks = [[(got[n], first) for n in b] for b in blocks] + [[(got["x4", piece], 0), (got["e"], first)]]
        got["D"] = rotate([got["D"]] if piece else [], end, blocks, basis_in, first, cuts[piece + 1] - first)

    def cross(p):
        here = slice(p * part, (p + 1) * part)
        got["keep", p] = got["keep"][:, here] + got["m3"][:, here]
        got["x5", p] = send(got["keep", p].astype(BF16), ACROSS_MIDDLE)

    x4(0)
    fence("m3", "A")
    cross(0)
    cross(1)
    fence(("x4", 0), ("x5", 0), "a3")
    x4(1)
    settle(0)
    fence(("x4", 1), ("x5", 1), ("m4", 0), ("n1", 0), ("sum", 0), "A", "a3")
    x4(2)
    settle(1)
    got["n2", 0] = send(got["m4", 0], TO_ENDS)
    got["A2"] = swap_narrow(got["A"])
    got["R", 0] = pick(("n1", 0), ("sum", 0))
    last(0)
    fence(("m4", 1), ("n1", 1), ("sum", 1), "A2", ("R", 0), "D")
    got["n2", 1] = send(got["m4", 1], TO_ENDS)
    got["A"] = (got["A"] + got["A2"]).astype(BF16)
    got["R", 1] = pick(("n1", 1), ("sum", 1))
    last(1)
    fence(("x4", 2), ("n2", 0), ("m4", 0), ("R", 1), "A", "D")
    got["R", 2] = pick(("n2", 0), ("m4", 0))
    last(2)
    fence(("n2", 1), ("R", 2), "D")
    got["D2"] = swap_narrow(got["D"])

    pieces = [[got["R", p]] for p in range(3)] + [[got["n2", 1], got["m4", 1]]]
    return fit(got["order"], end, [[got["A"]], [got["D"], got["D2"]]], pieces, got["places"])


def solution(mesh):
    return jax.shard_map(
        scheduled if mesh.shape["wide"] == LINE * PAIR else general,
        mesh=mesh,
        in_specs=(
            P(("grp", "wide"), "narrow"),
            P("grp", "wide"),
            P(("grp", "narrow"), "wide"),
            P(("grp", "wide"), "narrow"),
        ),
        out_specs=P(("grp", "wide"), "narrow"),
        check_vma=False,
    )
```

```python
import jax
import jax.numpy as jnp
from jax import lax
from jax.experimental import pallas as pl
from jax.experimental.pallas import tpu as pltpu
from jax.sharding import PartitionSpec as P

EX = 2
LINE, PAIR = 4, 2
DEEP = 1024
VMEM = 22 << 20
BF16, F32 = jnp.bfloat16, jnp.float32


def dot(a, b):
    return jnp.dot(a, b, preferred_element_type=F32)


def fit_kernel(counts, choices, order_ref, end_ref, place_ref, *refs):
    sum_refs, refs = refs[: sum(counts)], refs[sum(counts) :]
    piece_refs, (fit_ref, out_ref, turned_ref, rot_ref) = refs[:-4], refs[-4:]
    rows, ks = out_ref.shape
    size, seq = rows // order_ref.shape[0], rows // EX

    @pl.when(pl.program_id(0) == 0)
    def _():
        at = 0
        for piece, choice in enumerate(choices):
            width = piece_refs[at].shape[1]
            there = pl.ds(pl.multiple_of(place_ref[piece] * width, width), width)
            if choice == 1:
                out_ref[:, there] = piece_refs[at][...]
            else:
                out_ref[:, there] = jnp.where(end_ref[0] == 1, piece_refs[at][...], piece_refs[at + 1][...])
            at += choice

    slot, first = 0, 0
    for count in counts:
        halves = sum_refs[first : first + count]
        first += count
        for at in range(0, halves[0].shape[0], size):
            here = pl.ds(at, size)
            there = pl.ds(pl.multiple_of(order_ref[slot] * size, size), size)
            rot_ref[there, :] = sum(ref[here, :] for ref in halves).astype(BF16)
            slot += 1
    turned_ref[...] = rot_ref[...].T
    step = min(512, ks)
    for at in range(0, ks, step):
        total = None
        for e in range(EX):
            here = pl.ds(e * seq, seq)
            grad = dot(turned_ref[:, here], out_ref[here, pl.ds(at, step)])
            total = grad * grad if total is None else total + grad * grad
        fit_ref[:, pl.ds(at, step)] = total * (1.0 / EX)


def fit(order, end, sums, pieces, places):
    rows = sum(halves[0].shape[0] for halves in sums)
    ka = sums[0][0].shape[1]
    ks = sum(piece[0].shape[1] for piece in pieces)
    tile = 256 if ka % 256 == 0 else ka
    flat = [a for halves in sums for a in halves]
    outs = [a for piece in pieces for a in piece]
    return pl.pallas_call(
        lambda *refs: fit_kernel([len(halves) for halves in sums], [len(piece) for piece in pieces], *refs),
        out_shape=jax.ShapeDtypeStruct((ka, ks), F32),
        grid_spec=pltpu.PrefetchScalarGridSpec(
            num_scalar_prefetch=3,
            grid=(ka // tile,),
            in_specs=[pl.BlockSpec((a.shape[0], tile), lambda i, *_: (0, i)) for a in flat]
            + [pl.BlockSpec(a.shape, lambda i, *_: (0, 0)) for a in outs],
            out_specs=pl.BlockSpec((tile, ks), lambda i, *_: (i, 0)),
            scratch_shapes=[
                pltpu.VMEM((rows, ks), BF16),
                pltpu.VMEM((tile, rows), BF16),
                pltpu.VMEM((rows, tile), BF16),
            ],
        ),
        compiler_params=pltpu.CompilerParams(vmem_limit_bytes=56 << 20),
        cost_estimate=pl.CostEstimate(
            flops=2 * rows * ka * ks, bytes_accessed=8 * rows * ka + 2 * rows * ks + 4 * ka * ks, transcendentals=0
        ),
        name="fit",
    )(order, end, places, *flat, *outs)


def rotate_kernel(choices, end_ref, *refs):
    blocks = refs[: sum(choices)]
    basis_ref, *before, sum_ref, rows_ref = refs[sum(choices) :]
    size = blocks[0].shape[0]
    at = 0
    for i, choice in enumerate(choices):
        here = pl.ds(i * size, size)
        if choice == 1:
            rows_ref[here, :] = blocks[at][...]
        else:
            rows_ref[here, :] = jnp.where(end_ref[0] == 1, blocks[at][...], blocks[at + 1][...])
        at += choice

    @pl.when(pl.program_id(0) == 0)
    def _():
        if not before:
            sum_ref[...] = jnp.zeros_like(sum_ref)
        at = 0
        for ref in before:
            sum_ref[pl.ds(at, ref.shape[0]), :] = ref[...]
            at += ref.shape[0]

    sum_ref[...] += dot(rows_ref[...], basis_ref[...])


def rotate(before, end, blocks, basis, first, steps):
    flat = [pair for block in blocks for pair in block]
    size, ka = flat[0][0].shape[0], basis.shape[1]
    rows = size * len(blocks)
    specs = []
    for block in blocks:
        for which, (_, skip) in enumerate(block):
            used = lambda e, which=which, n=len(block): 1 if n == 1 else jnp.where(e[0] == 1, 1 - which, which)
            specs.append(
                pl.BlockSpec((size, DEEP), lambda k, e, used=used, skip=skip: (0, (k + skip) * used(e)))
            )
    whole = pl.BlockSpec((rows, ka), lambda k, e: (0, 0))
    arrays = [a for a, _ in flat] + [basis] + before
    return pl.pallas_call(
        lambda *refs: rotate_kernel([len(block) for block in blocks], *refs),
        out_shape=jax.ShapeDtypeStruct((rows, ka), F32),
        grid_spec=pltpu.PrefetchScalarGridSpec(
            num_scalar_prefetch=1,
            grid=(steps,),
            in_specs=specs
            + [pl.BlockSpec((DEEP, ka), lambda k, e: (first + k, 0))]
            + [pl.BlockSpec(a.shape, lambda k, e: (0, 0)) for a in before],
            out_specs=whole,
            scratch_shapes=[pltpu.VMEM((rows, DEEP), BF16)],
        ),
        compiler_params=pltpu.CompilerParams(vmem_limit_bytes=VMEM),
        cost_estimate=pl.CostEstimate(
            flops=rows * ka, bytes_accessed=4 * rows * ka, transcendentals=0
        ),
        name="rotate",
    )(end, *arrays)


def swap_narrow(a):
    return lax.ppermute(a, "narrow", [(0, 1), (1, 0)])


def general(inputs, deltas, basis_in, basis_out):
    partial_in = dot(lax.all_gather(inputs, "wide", axis=0, tiled=True), basis_in)
    rotated_out = lax.psum(dot(deltas, basis_out), "wide").astype(BF16)
    order, zero = jnp.arange(EX, dtype=jnp.int32), jnp.zeros((1,), jnp.int32)
    return fit(order, zero, [(partial_in, swap_narrow(partial_in))], [[rotated_out]], zero)


def pairs(step, where=lambda z: True):
    out = []
    for z in range(LINE):
        for x in range(PAIR):
            if where(z):
                tz, tx = step(z, x)
                out.append((z * PAIR + x, tz * PAIR + tx))
    return out


def corner(z):
    return z in (0, LINE - 1)


def middle(z):
    return not corner(z)


ENDS = pairs(lambda z, x: (z ^ 1, x))
TO_ENDS = pairs(lambda z, x: (z ^ 1, x), middle)
FROM_ENDS = pairs(lambda z, x: (z ^ 1, x), corner)
MIDDLE = pairs(lambda z, x: (3 - z, x), middle)
ACROSS = pairs(lambda z, x: (z, 1 - x))
ACROSS_ENDS = pairs(lambda z, x: (z, 1 - x), corner)
ACROSS_MIDDLE = pairs(lambda z, x: (z, 1 - x), middle)


def send(a, perm):
    return lax.ppermute(a, "wide", perm)


def scheduled(inputs, deltas, basis_in, basis_out):
    w = lax.axis_index("wide")
    z, x = w // PAIR, w % PAIR
    at_end = (z == 0) | (z == LINE - 1)
    end = at_end.astype(jnp.int32).reshape(1)
    half = (z >= 2).astype(jnp.int32)
    steps = inputs.shape[1] // DEEP
    cuts = [0, 8 * steps // 14, steps]
    part = basis_out.shape[1] // 4
    got = {"own": inputs}

    def fence(*names):
        got.update(zip(names, lax.optimization_barrier(tuple(got[n] for n in names))))

    def pick(a, b):
        return jnp.where(at_end, got[a], got[b])

    def columns(a, h):
        return lax.dynamic_slice_in_dim(a, h * 2 * part, 2 * part, 1)

    def turn(before, blocks, first, count):
        return rotate(before, end, [[(got[n], first) for n in block] for block in blocks], basis_in, first, count)

    def settle(p):
        got["sum", p] = (got["keep", p] + got["x5", p].astype(F32)).astype(BF16)
        got["m4", p] = send(got["sum", p], MIDDLE)
        got["n1", p] = send(got["sum", p], TO_ENDS)

    flip = jnp.where(z >= 2, 3, 0)
    line = lambda a, b: jnp.where(at_end, a, b) ^ flip
    mine, other = (lambda a, b: line(a, b) * PAIR + x), (lambda a, b: line(a, b) * PAIR + 1 - x)
    order = [mine(0, 1), mine(1, 0), other(0, 1), mine(2, 2), other(1, 2), mine(3, 3), other(2, 3), other(3, 0)]
    got["order"] = jnp.stack(order).astype(jnp.int32)
    places = [2 * half, 2 * half + 1, 2 - 2 * half, 3 - 2 * half]
    got["places"] = jnp.stack(places).astype(jnp.int32)

    got["x1"] = send(got["own"], ACROSS)
    got["a1"] = send(got["own"], ENDS)
    got["m1"] = send(got["own"], MIDDLE)
    got["out"] = dot(deltas, jnp.concatenate([columns(basis_out, 1 - half), columns(basis_out, half)], axis=1))
    got["r1"] = send(got["out"].astype(BF16), FROM_ENDS)
    fence("x1", "a1", "m1", "out", "order", "places")
    some = steps // 2
    got["x2"] = send(got["a1"], ACROSS_ENDS)
    got["x2", "m"] = send(got["m1"], ACROSS_MIDDLE)
    got["a2"] = send(got["m1"], TO_ENDS)
    got["m2"] = send(got["a1"], MIDDLE)
    blocks = [["own"], ["a1"], ["x1"]]
    got["A"] = turn([], blocks, 0, some)
    fence("x1", "x2", ("x2", "m"), "a2", "m2", "out", "r1", "A")
    got["x3"] = send(got["a2"], ACROSS_ENDS)
    got["x3", "m"] = send(got["m2"], ACROSS_MIDDLE)
    got["a3"] = send(got["m2"], TO_ENDS)
    cut = 2 * part
    got["m3"] = send(got["out"][:, :cut] + got["r1"][:, :cut].astype(F32), MIDDLE)
    got["e"] = send(got["x1"], FROM_ENDS)
    got["keep"] = got["out"][:, cut:] + got["r1"][:, cut:].astype(F32)
    more = [["a2", "m1"], ["x2", ("x2", "m")]]
    got["B"] = turn([], more, 0, some)
    got["A"] = turn([got["A"], got["B"]], blocks + more, some, steps - some)
    fence("x3", "A", "keep")
    fence(("x3", "m"), "a3", "e", "A")

    def x4(piece):
        got["x4", piece] = send(got["a3"][:, cuts[piece] * DEEP : cuts[piece + 1] * DEEP], ACROSS_ENDS)

    def last(piece):
        first = cuts[piece]
        blocks = [["a3", "m2"], ["x3", ("x3", "m")]]
        blocks = [[(got[n], first) for n in b] for b in blocks] + [[(got["x4", piece], 0), (got["e"], first)]]
        got["D"] = rotate([got["D"]] if piece else [], end, blocks, basis_in, first, cuts[piece + 1] - first)

    def cross(p):
        here = slice(p * part, (p + 1) * part)
        got["keep", p] = got["keep"][:, here] + got["m3"][:, here]
        got["x5", p] = send(got["keep", p].astype(BF16), ACROSS_MIDDLE)

    x4(0)
    got["A2"] = swap_narrow(got["A"])
    fence("m3", "A", "A2")
    cross(0)
    cross(1)
    fence(("x5", 0), "a3")
    settle(0)
    got["A"] = (got["A"] + got["A2"]).astype(BF16)
    fence(("x4", 0), ("x5", 1), ("m4", 0), ("n1", 0), ("sum", 0), "A", "a3")
    x4(1)
    settle(1)
    got["n2", 0] = send(got["m4", 0], TO_ENDS)
    got["R", 0] = pick(("n1", 0), ("sum", 0))
    last(0)
    fence(("x4", 1), ("m4", 1), ("n1", 1), ("sum", 1), ("R", 0), "D")
    got["n2", 1] = send(got["m4", 1], TO_ENDS)
    got["R", 1] = pick(("n1", 1), ("sum", 1))
    fence(("n2", 0), ("m4", 0), ("R", 1), "A", "D")
    got["R", 2] = pick(("n2", 0), ("m4", 0))
    last(1)
    fence(("n2", 1), ("R", 2), "D")
    got["D2"] = swap_narrow(got["D"])

    pieces = [[got["R", p]] for p in range(3)] + [[got["n2", 1], got["m4", 1]]]
    return fit(got["order"], end, [[got["A"]], [got["D"], got["D2"]]], pieces, got["places"])


def solution(mesh):
    return jax.shard_map(
        scheduled if mesh.shape["wide"] == LINE * PAIR else general,
        mesh=mesh,
        in_specs=(
            P(("grp", "wide"), "narrow"),
            P("grp", "wide"),
            P(("grp", "narrow"), "wide"),
            P(("grp", "wide"), "narrow"),
        ),
        out_specs=P(("grp", "wide"), "narrow"),
        check_vma=False,
    )
```

```python
import jax
import jax.numpy as jnp
from jax import lax
from jax.experimental import pallas as pl
from jax.experimental.pallas import tpu as pltpu
from jax.sharding import PartitionSpec as P

EX = 2
LINE, PAIR = 4, 2
DEEP = 1024
VMEM = 22 << 20
BF16, F32 = jnp.bfloat16, jnp.float32


def dot(a, b):
    return jnp.dot(a, b, preferred_element_type=F32)


def fit_kernel(counts, choices, order_ref, end_ref, place_ref, *refs):
    sum_refs, refs = refs[: sum(counts)], refs[sum(counts) :]
    piece_refs, (fit_ref, out_ref, turned_ref, rot_ref) = refs[:-4], refs[-4:]
    rows, ks = out_ref.shape
    size, seq = rows // order_ref.shape[0], rows // EX

    @pl.when(pl.program_id(0) == 0)
    def _():
        at = 0
        for piece, choice in enumerate(choices):
            width = piece_refs[at].shape[1]
            there = pl.ds(pl.multiple_of(place_ref[piece] * width, width), width)
            if choice == 1:
                out_ref[:, there] = piece_refs[at][...]
            else:
                out_ref[:, there] = jnp.where(end_ref[0] == 1, piece_refs[at][...], piece_refs[at + 1][...])
            at += choice

    slot, first = 0, 0
    for count in counts:
        halves = sum_refs[first : first + count]
        first += count
        for at in range(0, halves[0].shape[0], size):
            here = pl.ds(at, size)
            there = pl.ds(pl.multiple_of(order_ref[slot] * size, size), size)
            rot_ref[there, :] = sum(ref[here, :] for ref in halves).astype(BF16)
            slot += 1
    turned_ref[...] = rot_ref[...].T
    step = min(512, ks)
    for at in range(0, ks, step):
        total = None
        for e in range(EX):
            here = pl.ds(e * seq, seq)
            grad = dot(turned_ref[:, here], out_ref[here, pl.ds(at, step)])
            total = grad * grad if total is None else total + grad * grad
        fit_ref[:, pl.ds(at, step)] = total * (1.0 / EX)


def fit(order, end, sums, pieces, places):
    rows = sum(halves[0].shape[0] for halves in sums)
    ka = sums[0][0].shape[1]
    ks = sum(piece[0].shape[1] for piece in pieces)
    tile = 256 if ka % 256 == 0 else ka
    flat = [a for halves in sums for a in halves]
    outs = [a for piece in pieces for a in piece]
    return pl.pallas_call(
        lambda *refs: fit_kernel([len(halves) for halves in sums], [len(piece) for piece in pieces], *refs),
        out_shape=jax.ShapeDtypeStruct((ka, ks), F32),
        grid_spec=pltpu.PrefetchScalarGridSpec(
            num_scalar_prefetch=3,
            grid=(ka // tile,),
            in_specs=[pl.BlockSpec((a.shape[0], tile), lambda i, *_: (0, i)) for a in flat]
            + [pl.BlockSpec(a.shape, lambda i, *_: (0, 0)) for a in outs],
            out_specs=pl.BlockSpec((tile, ks), lambda i, *_: (i, 0)),
            scratch_shapes=[
                pltpu.VMEM((rows, ks), BF16),
                pltpu.VMEM((tile, rows), BF16),
                pltpu.VMEM((rows, tile), BF16),
            ],
        ),
        compiler_params=pltpu.CompilerParams(vmem_limit_bytes=56 << 20),
        cost_estimate=pl.CostEstimate(
            flops=2 * rows * ka * ks, bytes_accessed=8 * rows * ka + 2 * rows * ks + 4 * ka * ks, transcendentals=0
        ),
        name="fit",
    )(order, end, places, *flat, *outs)


def rotate_kernel(choices, end_ref, *refs):
    blocks = refs[: sum(choices)]
    basis_ref, *before, sum_ref, rows_ref = refs[sum(choices) :]
    size = blocks[0].shape[0]
    at = 0
    for i, choice in enumerate(choices):
        here = pl.ds(i * size, size)
        if choice == 1:
            rows_ref[here, :] = blocks[at][...]
        else:
            rows_ref[here, :] = jnp.where(end_ref[0] == 1, blocks[at][...], blocks[at + 1][...])
        at += choice

    @pl.when(pl.program_id(0) == 0)
    def _():
        if not before:
            sum_ref[...] = jnp.zeros_like(sum_ref)
        at = 0
        for ref in before:
            sum_ref[pl.ds(at, ref.shape[0]), :] = ref[...]
            at += ref.shape[0]

    sum_ref[...] += dot(rows_ref[...], basis_ref[...])


def rotate(before, end, blocks, basis, first, steps):
    flat = [pair for block in blocks for pair in block]
    size, ka = flat[0][0].shape[0], basis.shape[1]
    rows = size * len(blocks)
    specs = []
    for block in blocks:
        for which, (_, skip) in enumerate(block):
            used = lambda e, which=which, n=len(block): 1 if n == 1 else jnp.where(e[0] == 1, 1 - which, which)
            specs.append(
                pl.BlockSpec((size, DEEP), lambda k, e, used=used, skip=skip: (0, (k + skip) * used(e)))
            )
    whole = pl.BlockSpec((rows, ka), lambda k, e: (0, 0))
    arrays = [a for a, _ in flat] + [basis] + before
    return pl.pallas_call(
        lambda *refs: rotate_kernel([len(block) for block in blocks], *refs),
        out_shape=jax.ShapeDtypeStruct((rows, ka), F32),
        grid_spec=pltpu.PrefetchScalarGridSpec(
            num_scalar_prefetch=1,
            grid=(steps,),
            in_specs=specs
            + [pl.BlockSpec((DEEP, ka), lambda k, e: (first + k, 0))]
            + [pl.BlockSpec(a.shape, lambda k, e: (0, 0)) for a in before],
            out_specs=whole,
            scratch_shapes=[pltpu.VMEM((rows, DEEP), BF16)],
        ),
        compiler_params=pltpu.CompilerParams(vmem_limit_bytes=VMEM),
        cost_estimate=pl.CostEstimate(
            flops=rows * ka, bytes_accessed=4 * rows * ka, transcendentals=0
        ),
        name="rotate",
    )(end, *arrays)


def swap_narrow(a):
    return lax.ppermute(a, "narrow", [(0, 1), (1, 0)])


def general(inputs, deltas, basis_in, basis_out):
    partial_in = dot(lax.all_gather(inputs, "wide", axis=0, tiled=True), basis_in)
    rotated_out = lax.psum(dot(deltas, basis_out), "wide").astype(BF16)
    order, zero = jnp.arange(EX, dtype=jnp.int32), jnp.zeros((1,), jnp.int32)
    return fit(order, zero, [(partial_in, swap_narrow(partial_in))], [[rotated_out]], zero)


def pairs(step, where=lambda z: True):
    out = []
    for z in range(LINE):
        for x in range(PAIR):
            if where(z):
                tz, tx = step(z, x)
                out.append((z * PAIR + x, tz * PAIR + tx))
    return out


def corner(z):
    return z in (0, LINE - 1)


def middle(z):
    return not corner(z)


ENDS = pairs(lambda z, x: (z ^ 1, x))
TO_ENDS = pairs(lambda z, x: (z ^ 1, x), middle)
FROM_ENDS = pairs(lambda z, x: (z ^ 1, x), corner)
MIDDLE = pairs(lambda z, x: (3 - z, x), middle)
ACROSS = pairs(lambda z, x: (z, 1 - x))
ACROSS_ENDS = pairs(lambda z, x: (z, 1 - x), corner)
ACROSS_MIDDLE = pairs(lambda z, x: (z, 1 - x), middle)


def send(a, perm):
    return lax.ppermute(a, "wide", perm)


def scheduled(inputs, deltas, basis_in, basis_out):
    w = lax.axis_index("wide")
    z, x = w // PAIR, w % PAIR
    at_end = (z == 0) | (z == LINE - 1)
    end = at_end.astype(jnp.int32).reshape(1)
    half = (z >= 2).astype(jnp.int32)
    steps = inputs.shape[1] // DEEP
    cuts = [0, 8 * steps // 14, steps]
    part = basis_out.shape[1] // 4
    got = {"own": inputs}

    def fence(*names):
        got.update(zip(names, lax.optimization_barrier(tuple(got[n] for n in names))))

    def pick(a, b):
        return jnp.where(at_end, got[a], got[b])

    def columns(a, h):
        return lax.dynamic_slice_in_dim(a, h * 2 * part, 2 * part, 1)

    def turn(before, blocks, first, count):
        return rotate(before, end, [[(got[n], first) for n in block] for block in blocks], basis_in, first, count)

    def settle(p):
        got["sum", p] = (got["keep", p] + got["x5", p].astype(F32)).astype(BF16)
        got["m4", p] = send(got["sum", p], MIDDLE)
        got["n1", p] = send(got["sum", p], TO_ENDS)

    flip = jnp.where(z >= 2, 3, 0)
    line = lambda a, b: jnp.where(at_end, a, b) ^ flip
    mine, other = (lambda a, b: line(a, b) * PAIR + x), (lambda a, b: line(a, b) * PAIR + 1 - x)
    order = [mine(0, 1), mine(1, 0), other(0, 1), mine(2, 2), other(1, 2), mine(3, 3), other(2, 3), other(3, 0)]
    got["order"] = jnp.stack(order).astype(jnp.int32)
    places = [2 * half, 2 * half + 1, 2 - 2 * half, 3 - 2 * half]
    got["places"] = jnp.stack(places).astype(jnp.int32)

    got["x1"] = send(got["own"], ACROSS)
    got["a1"] = send(got["own"], ENDS)
    got["m1"] = send(got["own"], MIDDLE)
    got["out"] = dot(deltas, jnp.concatenate([columns(basis_out, 1 - half), columns(basis_out, half)], axis=1))
    got["r1"] = send(got["out"].astype(BF16), FROM_ENDS)
    fence("x1", "a1", "m1", "out", "order", "places")
    some = steps // 2
    got["x2"] = send(got["a1"], ACROSS_ENDS)
    got["x2", "m"] = send(got["m1"], ACROSS_MIDDLE)
    got["a2"] = send(got["m1"], TO_ENDS)
    got["m2"] = send(got["a1"], MIDDLE)
    blocks = [["own"], ["a1"], ["x1"]]
    got["A"] = turn([], blocks, 0, some)
    fence("x1", "x2", ("x2", "m"), "a2", "m2", "out", "r1", "A")
    got["x3"] = send(got["a2"], ACROSS_ENDS)
    got["x3", "m"] = send(got["m2"], ACROSS_MIDDLE)
    got["a3"] = send(got["m2"], TO_ENDS)
    cut = 2 * part
    got["m3"] = send(got["out"][:, :cut] + got["r1"][:, :cut].astype(F32), MIDDLE)
    got["e"] = send(got["x1"], FROM_ENDS)
    got["keep"] = got["out"][:, cut:] + got["r1"][:, cut:].astype(F32)
    more = [["a2", "m1"], ["x2", ("x2", "m")]]
    got["B"] = turn([], more, 0, some)
    got["A"] = turn([got["A"], got["B"]], blocks + more, some, steps - some)
    fence("x3", "A", "keep")
    fence(("x3", "m"), "a3", "e", "A")

    def x4(piece):
        got["x4", piece] = send(got["a3"][:, cuts[piece] * DEEP : cuts[piece + 1] * DEEP], ACROSS_ENDS)

    def last(piece):
        first = cuts[piece]
        blocks = [["a3", "m2"], ["x3", ("x3", "m")]]
        blocks = [[(got[n], first) for n in b] for b in blocks] + [[(got["x4", piece], 0), (got["e"], first)]]
        got["D"] = rotate([got["D"]] if piece else [], end, blocks, basis_in, first, cuts[piece + 1] - first)

    def cross(p):
        here = slice(p * part, (p + 1) * part)
        got["keep", p] = got["keep"][:, here] + got["m3"][:, here]
        got["x5", p] = send(got["keep", p].astype(BF16), ACROSS_MIDDLE)

    x4(0)
    fence("m3", "A")
    cross(0)
    cross(1)
    fence(("x5", 0), "a3")
    settle(0)
    fence(("x4", 0), ("x5", 1), ("m4", 0), ("n1", 0), ("sum", 0), "A", "a3")
    x4(1)
    settle(1)
    got["n2", 0] = send(got["m4", 0], TO_ENDS)
    got["A2"] = swap_narrow(got["A"])
    got["R", 0] = pick(("n1", 0), ("sum", 0))
    last(0)
    fence(("x4", 1), ("m4", 1), ("n1", 1), ("sum", 1), ("R", 0), "A2", "D")
    got["n2", 1] = send(got["m4", 1], TO_ENDS)
    got["A"] = (got["A"] + got["A2"]).astype(BF16)
    got["R", 1] = pick(("n1", 1), ("sum", 1))
    fence(("n2", 0), ("m4", 0), ("R", 1), "A", "D")
    got["R", 2] = pick(("n2", 0), ("m4", 0))
    last(1)
    fence(("n2", 1), ("R", 2), "D")
    got["D2"] = swap_narrow(got["D"])

    pieces = [[got["R", p]] for p in range(3)] + [[got["n2", 1], got["m4", 1]]]
    return fit(got["order"], end, [[got["A"]], [got["D"], got["D2"]]], pieces, got["places"])


def solution(mesh):
    return jax.shard_map(
        scheduled if mesh.shape["wide"] == LINE * PAIR else general,
        mesh=mesh,
        in_specs=(
            P(("grp", "wide"), "narrow"),
            P("grp", "wide"),
            P(("grp", "narrow"), "wide"),
            P(("grp", "wide"), "narrow"),
        ),
        out_specs=P(("grp", "wide"), "narrow"),
        check_vma=False,
    )
```

```python
import jax
import jax.numpy as jnp
from jax import lax
from jax.experimental import pallas as pl
from jax.experimental.pallas import tpu as pltpu
from jax.sharding import PartitionSpec as P

EX = 2
LINE, PAIR = 4, 2
DEEP = 1024
VMEM = 22 << 20
BF16, F32 = jnp.bfloat16, jnp.float32


def dot(a, b):
    return jnp.dot(a, b, preferred_element_type=F32)


def fit_kernel(counts, choices, order_ref, end_ref, place_ref, *refs):
    sum_refs, refs = refs[: sum(counts)], refs[sum(counts) :]
    piece_refs, (fit_ref, out_ref, turned_ref, rot_ref) = refs[:-4], refs[-4:]
    rows, ks = out_ref.shape
    size, seq = rows // order_ref.shape[0], rows // EX

    @pl.when(pl.program_id(0) == 0)
    def _():
        at = 0
        for piece, choice in enumerate(choices):
            width = piece_refs[at].shape[1]
            there = pl.ds(pl.multiple_of(place_ref[piece] * width, width), width)
            if choice == 1:
                out_ref[:, there] = piece_refs[at][...]
            else:
                out_ref[:, there] = jnp.where(end_ref[0] == 1, piece_refs[at][...], piece_refs[at + 1][...])
            at += choice

    slot, first = 0, 0
    for count in counts:
        halves = sum_refs[first : first + count]
        first += count
        for at in range(0, halves[0].shape[0], size):
            here = pl.ds(at, size)
            there = pl.ds(pl.multiple_of(order_ref[slot] * size, size), size)
            rot_ref[there, :] = sum(ref[here, :] for ref in halves).astype(BF16)
            slot += 1
    turned_ref[...] = rot_ref[...].T
    step = min(512, ks)
    for at in range(0, ks, step):
        total = None
        for e in range(EX):
            here = pl.ds(e * seq, seq)
            grad = dot(turned_ref[:, here], out_ref[here, pl.ds(at, step)])
            total = grad * grad if total is None else total + grad * grad
        fit_ref[:, pl.ds(at, step)] = total * (1.0 / EX)


def fit(order, end, sums, pieces, places):
    rows = sum(halves[0].shape[0] for halves in sums)
    ka = sums[0][0].shape[1]
    ks = sum(piece[0].shape[1] for piece in pieces)
    tile = 256 if ka % 256 == 0 else ka
    flat = [a for halves in sums for a in halves]
    outs = [a for piece in pieces for a in piece]
    return pl.pallas_call(
        lambda *refs: fit_kernel([len(halves) for halves in sums], [len(piece) for piece in pieces], *refs),
        out_shape=jax.ShapeDtypeStruct((ka, ks), F32),
        grid_spec=pltpu.PrefetchScalarGridSpec(
            num_scalar_prefetch=3,
            grid=(ka // tile,),
            in_specs=[pl.BlockSpec((a.shape[0], tile), lambda i, *_: (0, i)) for a in flat]
            + [pl.BlockSpec(a.shape, lambda i, *_: (0, 0)) for a in outs],
            out_specs=pl.BlockSpec((tile, ks), lambda i, *_: (i, 0)),
            scratch_shapes=[
                pltpu.VMEM((rows, ks), BF16),
                pltpu.VMEM((tile, rows), BF16),
                pltpu.VMEM((rows, tile), BF16),
            ],
        ),
        compiler_params=pltpu.CompilerParams(vmem_limit_bytes=56 << 20),
        cost_estimate=pl.CostEstimate(
            flops=2 * rows * ka * ks, bytes_accessed=8 * rows * ka + 2 * rows * ks + 4 * ka * ks, transcendentals=0
        ),
        name="fit",
    )(order, end, places, *flat, *outs)


def rotate_kernel(choices, end_ref, *refs):
    blocks = refs[: sum(choices)]
    basis_ref, *before, sum_ref, rows_ref = refs[sum(choices) :]
    size = blocks[0].shape[0]
    at = 0
    for i, choice in enumerate(choices):
        here = pl.ds(i * size, size)
        if choice == 1:
            rows_ref[here, :] = blocks[at][...]
        else:
            rows_ref[here, :] = jnp.where(end_ref[0] == 1, blocks[at][...], blocks[at + 1][...])
        at += choice

    @pl.when(pl.program_id(0) == 0)
    def _():
        if not before:
            sum_ref[...] = jnp.zeros_like(sum_ref)
        at = 0
        for ref in before:
            sum_ref[pl.ds(at, ref.shape[0]), :] = ref[...]
            at += ref.shape[0]

    sum_ref[...] += dot(rows_ref[...], basis_ref[...])


def rotate(before, end, blocks, basis, first, steps):
    flat = [pair for block in blocks for pair in block]
    size, ka = flat[0][0].shape[0], basis.shape[1]
    rows = size * len(blocks)
    specs = []
    for block in blocks:
        for which, (_, skip) in enumerate(block):
            used = lambda e, which=which, n=len(block): 1 if n == 1 else jnp.where(e[0] == 1, 1 - which, which)
            specs.append(
                pl.BlockSpec((size, DEEP), lambda k, e, used=used, skip=skip: (0, (k + skip) * used(e)))
            )
    whole = pl.BlockSpec((rows, ka), lambda k, e: (0, 0))
    arrays = [a for a, _ in flat] + [basis] + before
    return pl.pallas_call(
        lambda *refs: rotate_kernel([len(block) for block in blocks], *refs),
        out_shape=jax.ShapeDtypeStruct((rows, ka), F32),
        grid_spec=pltpu.PrefetchScalarGridSpec(
            num_scalar_prefetch=1,
            grid=(steps,),
            in_specs=specs
            + [pl.BlockSpec((DEEP, ka), lambda k, e: (first + k, 0))]
            + [pl.BlockSpec(a.shape, lambda k, e: (0, 0)) for a in before],
            out_specs=whole,
            scratch_shapes=[pltpu.VMEM((rows, DEEP), BF16)],
        ),
        compiler_params=pltpu.CompilerParams(vmem_limit_bytes=VMEM),
        cost_estimate=pl.CostEstimate(
            flops=rows * ka, bytes_accessed=4 * rows * ka, transcendentals=0
        ),
        name="rotate",
    )(end, *arrays)


def swap_narrow(a):
    return lax.ppermute(a, "narrow", [(0, 1), (1, 0)])


def general(inputs, deltas, basis_in, basis_out):
    partial_in = dot(lax.all_gather(inputs, "wide", axis=0, tiled=True), basis_in)
    rotated_out = lax.psum(dot(deltas, basis_out), "wide").astype(BF16)
    order, zero = jnp.arange(EX, dtype=jnp.int32), jnp.zeros((1,), jnp.int32)
    return fit(order, zero, [(partial_in, swap_narrow(partial_in))], [[rotated_out]], zero)


def pairs(step, where=lambda z: True):
    out = []
    for z in range(LINE):
        for x in range(PAIR):
            if where(z):
                tz, tx = step(z, x)
                out.append((z * PAIR + x, tz * PAIR + tx))
    return out


def corner(z):
    return z in (0, LINE - 1)


def middle(z):
    return not corner(z)


ENDS = pairs(lambda z, x: (z ^ 1, x))
TO_ENDS = pairs(lambda z, x: (z ^ 1, x), middle)
FROM_ENDS = pairs(lambda z, x: (z ^ 1, x), corner)
MIDDLE = pairs(lambda z, x: (3 - z, x), middle)
ACROSS = pairs(lambda z, x: (z, 1 - x))
ACROSS_ENDS = pairs(lambda z, x: (z, 1 - x), corner)
ACROSS_MIDDLE = pairs(lambda z, x: (z, 1 - x), middle)


def send(a, perm):
    return lax.ppermute(a, "wide", perm)


def scheduled(inputs, deltas, basis_in, basis_out):
    w = lax.axis_index("wide")
    z, x = w // PAIR, w % PAIR
    at_end = (z == 0) | (z == LINE - 1)
    end = at_end.astype(jnp.int32).reshape(1)
    half = (z >= 2).astype(jnp.int32)
    steps = inputs.shape[1] // DEEP
    cuts = [0, 6 * steps // 14, 11 * steps // 14, steps]
    part = basis_out.shape[1] // 4
    got = {"own": inputs}

    def fence(*names):
        got.update(zip(names, lax.optimization_barrier(tuple(got[n] for n in names))))

    def pick(a, b):
        return jnp.where(at_end, got[a], got[b])

    def columns(a, h):
        return lax.dynamic_slice_in_dim(a, h * 2 * part, 2 * part, 1)

    def turn(before, blocks, first, count):
        return rotate(before, end, [[(got[n], first) for n in block] for block in blocks], basis_in, first, count)

    def settle(p):
        got["sum", p] = (got["keep", p] + got["x5", p].astype(F32)).astype(BF16)
        got["m4", p] = send(got["sum", p], MIDDLE)
        got["n1", p] = send(got["sum", p], TO_ENDS)

    flip = jnp.where(z >= 2, 3, 0)
    line = lambda a, b: jnp.where(at_end, a, b) ^ flip
    mine, other = (lambda a, b: line(a, b) * PAIR + x), (lambda a, b: line(a, b) * PAIR + 1 - x)
    order = [mine(0, 1), mine(1, 0), other(0, 1), mine(2, 2), other(1, 2), mine(3, 3), other(2, 3), other(3, 0)]
    got["order"] = jnp.stack(order).astype(jnp.int32)
    places = [2 * half, 2 * half + 1, 2 - 2 * half, 3 - 2 * half]
    got["places"] = jnp.stack(places).astype(jnp.int32)

    got["x1"] = send(got["own"], ACROSS)
    got["a1"] = send(got["own"], ENDS)
    got["m1"] = send(got["own"], MIDDLE)
    got["out"] = dot(deltas, jnp.concatenate([columns(basis_out, 1 - half), columns(basis_out, half)], axis=1))
    got["r1"] = send(got["out"].astype(BF16), FROM_ENDS)
    fence("x1", "a1", "m1", "out", "order", "places")
    some = steps // 2
    got["x2"] = send(got["a1"], ACROSS_ENDS)
    got["x2", "m"] = send(got["m1"], ACROSS_MIDDLE)
    got["a2"] = send(got["m1"], TO_ENDS)
    got["m2"] = send(got["a1"], MIDDLE)
    blocks = [["own"], ["a1"], ["x1"]]
    got["A"] = turn([], blocks, 0, some)
    fence("x1", "x2", "a2", "m2", "out", "r1", "A")
    def columns_of(p, q):
        here = slice(p * part, q * part)
        return got["out"][:, here] + got["r1"][:, here].astype(F32)

    def cross(p):
        here = slice(p * part, (p + 1) * part)
        got["keep", p] = got["keep"][:, here] + got["m3", p]
        got["x5", p] = send(got["keep", p].astype(BF16), ACROSS_MIDDLE)

    got["x3"] = send(got["a2"], ACROSS_ENDS)
    got["m3", 0] = send(columns_of(0, 1), MIDDLE)
    got["a3"] = send(got["m2"], TO_ENDS)
    got["e"] = send(got["x1"], FROM_ENDS)
    fence(("x2", "m"), "m2", "out", "r1")
    got["x3m", 0] = send(got["m2"][:, : cuts[1] * DEEP], ACROSS_MIDDLE)
    got["give"], got["keep"] = columns_of(1, 2), columns_of(2, 4)
    more = [["a2", "m1"], ["x2", ("x2", "m")]]
    got["B"] = turn([], more, 0, some)
    fence(("m3", 0), ("x3m", 0), "give", "keep", "m2", "B")
    cross(0)
    got["m3", 1] = send(got["give"], MIDDLE)
    got["A"] = turn([got["A"], got["B"]], blocks + more, some, steps - some)
    fence("x3", "A")
    fence("a3", ("x5", 0), "A")

    def x4(piece):
        got["x4", piece] = send(got["a3"][:, cuts[piece] * DEEP : cuts[piece + 1] * DEEP], ACROSS_ENDS)

    def last(piece):
        first, count = cuts[piece], cuts[piece + 1] - cuts[piece]
        side = ("x3m", 0 if piece == 0 else 1)
        blocks = [
            [(got["a3"], first), (got["m2"], first)],
            [(got["x3"], first), (got[side], 0 if piece == 0 else first - cuts[1])],
            [(got["x4", piece], 0), (got["e"], first)],
        ]
        got["D"] = rotate([got["D"]] if piece else [], end, blocks, basis_in, first, count)

    x4(0)
    settle(0)
    fence(("m3", 1), "e", "m2")
    cross(1)
    got["x3m", 1] = send(got["m2"][:, cuts[1] * DEEP :], ACROSS_MIDDLE)
    fence(("x4", 0), ("m4", 0), ("n1", 0), ("sum", 0), ("x5", 1), "A", "a3")
    x4(1)
    got["n2", 0] = send(got["m4", 0], TO_ENDS)
    settle(1)
    got["R", 0] = pick(("n1", 0), ("sum", 0))
    last(0)
    fence(("x4", 1), ("m4", 1), ("n1", 1), ("sum", 1), ("x3m", 1), ("R", 0), "A", "D", "a3")
    x4(2)
    got["n2", 1] = send(got["m4", 1], TO_ENDS)
    got["A2"] = swap_narrow(got["A"])
    got["R", 1] = pick(("n1", 1), ("sum", 1))
    last(1)
    fence(("x4", 2), ("n2", 0), ("m4", 0), "A2", ("R", 1), "D")
    got["A"] = (got["A"] + got["A2"]).astype(BF16)
    got["R", 2] = pick(("n2", 0), ("m4", 0))
    last(2)
    fence(("n2", 1), ("R", 2), "A", "D")
    got["D2"] = swap_narrow(got["D"])

    pieces = [[got["R", p]] for p in range(3)] + [[got["n2", 1], got["m4", 1]]]
    return fit(got["order"], end, [[got["A"]], [got["D"], got["D2"]]], pieces, got["places"])


def solution(mesh):
    return jax.shard_map(
        scheduled if mesh.shape["wide"] == LINE * PAIR else general,
        mesh=mesh,
        in_specs=(
            P(("grp", "wide"), "narrow"),
            P("grp", "wide"),
            P(("grp", "narrow"), "wide"),
            P(("grp", "wide"), "narrow"),
        ),
        out_specs=P(("grp", "wide"), "narrow"),
        check_vma=False,
    )
```

```python
import jax
import jax.numpy as jnp
from jax import lax
from jax.experimental import pallas as pl
from jax.experimental.pallas import tpu as pltpu
from jax.sharding import PartitionSpec as P

EX = 2
LINE, PAIR = 4, 2
DEEP = 1024
VMEM = 22 << 20
BF16, F32 = jnp.bfloat16, jnp.float32


def dot(a, b):
    return jnp.dot(a, b, preferred_element_type=F32)


def fit_kernel(counts, choices, order_ref, end_ref, place_ref, *refs):
    sum_refs, refs = refs[: sum(counts)], refs[sum(counts) :]
    piece_refs, (fit_ref, out_ref, turned_ref, rot_ref) = refs[:-4], refs[-4:]
    rows, ks = out_ref.shape
    size, seq = rows // order_ref.shape[0], rows // EX

    @pl.when(pl.program_id(0) == 0)
    def _():
        at = 0
        for piece, choice in enumerate(choices):
            width = piece_refs[at].shape[1]
            there = pl.ds(pl.multiple_of(place_ref[piece] * width, width), width)
            if choice == 1:
                out_ref[:, there] = piece_refs[at][...]
            else:
                out_ref[:, there] = jnp.where(end_ref[0] == 1, piece_refs[at][...], piece_refs[at + 1][...])
            at += choice

    slot, first = 0, 0
    for count in counts:
        halves = sum_refs[first : first + count]
        first += count
        for at in range(0, halves[0].shape[0], size):
            here = pl.ds(at, size)
            there = pl.ds(pl.multiple_of(order_ref[slot] * size, size), size)
            rot_ref[there, :] = sum(ref[here, :] for ref in halves).astype(BF16)
            slot += 1
    turned_ref[...] = rot_ref[...].T
    step = min(256, ks)
    for at in range(0, ks, step):
        total = None
        for e in range(EX):
            here = pl.ds(e * seq, seq)
            grad = dot(turned_ref[:, here], out_ref[here, pl.ds(at, step)])
            total = grad * grad if total is None else total + grad * grad
        fit_ref[:, pl.ds(at, step)] = total * (1.0 / EX)


def fit(order, end, sums, pieces, places):
    rows = sum(halves[0].shape[0] for halves in sums)
    ka = sums[0][0].shape[1]
    ks = sum(piece[0].shape[1] for piece in pieces)
    tile = 256 if ka % 256 == 0 else ka
    flat = [a for halves in sums for a in halves]
    outs = [a for piece in pieces for a in piece]
    return pl.pallas_call(
        lambda *refs: fit_kernel([len(halves) for halves in sums], [len(piece) for piece in pieces], *refs),
        out_shape=jax.ShapeDtypeStruct((ka, ks), F32),
        grid_spec=pltpu.PrefetchScalarGridSpec(
            num_scalar_prefetch=3,
            grid=(ka // tile,),
            in_specs=[pl.BlockSpec((a.shape[0], tile), lambda i, *_: (0, i)) for a in flat]
            + [pl.BlockSpec(a.shape, lambda i, *_: (0, 0)) for a in outs],
            out_specs=pl.BlockSpec((tile, ks), lambda i, *_: (i, 0)),
            scratch_shapes=[
                pltpu.VMEM((rows, ks), BF16),
                pltpu.VMEM((tile, rows), BF16),
                pltpu.VMEM((rows, tile), BF16),
            ],
        ),
        compiler_params=pltpu.CompilerParams(vmem_limit_bytes=56 << 20),
        cost_estimate=pl.CostEstimate(
            flops=2 * rows * ka * ks, bytes_accessed=8 * rows * ka + 2 * rows * ks + 4 * ka * ks, transcendentals=0
        ),
        name="fit",
    )(order, end, places, *flat, *outs)


def rotate_kernel(choices, end_ref, *refs):
    blocks = refs[: sum(choices)]
    basis_ref, *before, sum_ref, rows_ref = refs[sum(choices) :]
    size = blocks[0].shape[0]
    at = 0
    for i, choice in enumerate(choices):
        here = pl.ds(i * size, size)
        if choice == 1:
            rows_ref[here, :] = blocks[at][...]
        else:
            rows_ref[here, :] = jnp.where(end_ref[0] == 1, blocks[at][...], blocks[at + 1][...])
        at += choice

    @pl.when(pl.program_id(0) == 0)
    def _():
        if not before:
            sum_ref[...] = jnp.zeros_like(sum_ref)
        at = 0
        for ref in before:
            sum_ref[pl.ds(at, ref.shape[0]), :] = ref[...]
            at += ref.shape[0]

    sum_ref[...] += dot(rows_ref[...], basis_ref[...])


def rotate(before, end, blocks, basis, first, steps):
    flat = [pair for block in blocks for pair in block]
    size, ka = flat[0][0].shape[0], basis.shape[1]
    rows = size * len(blocks)
    specs = []
    for block in blocks:
        for which, (_, skip) in enumerate(block):
            used = lambda e, which=which, n=len(block): 1 if n == 1 else jnp.where(e[0] == 1, 1 - which, which)
            specs.append(
                pl.BlockSpec((size, DEEP), lambda k, e, used=used, skip=skip: (0, (k + skip) * used(e)))
            )
    whole = pl.BlockSpec((rows, ka), lambda k, e: (0, 0))
    arrays = [a for a, _ in flat] + [basis] + before
    return pl.pallas_call(
        lambda *refs: rotate_kernel([len(block) for block in blocks], *refs),
        out_shape=jax.ShapeDtypeStruct((rows, ka), F32),
        grid_spec=pltpu.PrefetchScalarGridSpec(
            num_scalar_prefetch=1,
            grid=(steps,),
            in_specs=specs
            + [pl.BlockSpec((DEEP, ka), lambda k, e: (first + k, 0))]
            + [pl.BlockSpec(a.shape, lambda k, e: (0, 0)) for a in before],
            out_specs=whole,
            scratch_shapes=[pltpu.VMEM((rows, DEEP), BF16)],
        ),
        compiler_params=pltpu.CompilerParams(vmem_limit_bytes=VMEM),
        cost_estimate=pl.CostEstimate(
            flops=rows * ka, bytes_accessed=4 * rows * ka, transcendentals=0
        ),
        name="rotate",
    )(end, *arrays)


def swap_narrow(a):
    return lax.ppermute(a, "narrow", [(0, 1), (1, 0)])


def general(inputs, deltas, basis_in, basis_out):
    partial_in = dot(lax.all_gather(inputs, "wide", axis=0, tiled=True), basis_in)
    rotated_out = lax.psum(dot(deltas, basis_out), "wide").astype(BF16)
    order, zero = jnp.arange(EX, dtype=jnp.int32), jnp.zeros((1,), jnp.int32)
    return fit(order, zero, [(partial_in, swap_narrow(partial_in))], [[rotated_out]], zero)


def pairs(step, where=lambda z: True):
    out = []
    for z in range(LINE):
        for x in range(PAIR):
            if where(z):
                tz, tx = step(z, x)
                out.append((z * PAIR + x, tz * PAIR + tx))
    return out


def corner(z):
    return z in (0, LINE - 1)


def middle(z):
    return not corner(z)


ENDS = pairs(lambda z, x: (z ^ 1, x))
TO_ENDS = pairs(lambda z, x: (z ^ 1, x), middle)
FROM_ENDS = pairs(lambda z, x: (z ^ 1, x), corner)
MIDDLE = pairs(lambda z, x: (3 - z, x), middle)
ACROSS = pairs(lambda z, x: (z, 1 - x))
ACROSS_ENDS = pairs(lambda z, x: (z, 1 - x), corner)
ACROSS_MIDDLE = pairs(lambda z, x: (z, 1 - x), middle)


def send(a, perm):
    return lax.ppermute(a, "wide", perm)


def scheduled(inputs, deltas, basis_in, basis_out):
    w = lax.axis_index("wide")
    z, x = w // PAIR, w % PAIR
    at_end = (z == 0) | (z == LINE - 1)
    end = at_end.astype(jnp.int32).reshape(1)
    half = (z >= 2).astype(jnp.int32)
    steps = inputs.shape[1] // DEEP
    cuts = [0, 2 * steps // 14, 8 * steps // 14, steps]
    part = basis_out.shape[1] // 4
    got = {"own": inputs}

    def fence(*names):
        got.update(zip(names, lax.optimization_barrier(tuple(got[n] for n in names))))

    def pick(a, b):
        return jnp.where(at_end, got[a], got[b])

    def columns(a, h):
        return lax.dynamic_slice_in_dim(a, h * 2 * part, 2 * part, 1)

    def turn(before, blocks, first, count):
        return rotate(before, end, [[(got[n], first) for n in block] for block in blocks], basis_in, first, count)

    def settle(p):
        got["sum", p] = (got["keep", p] + got["x5", p].astype(F32)).astype(BF16)
        got["m4", p] = send(got["sum", p], MIDDLE)
        got["n1", p] = send(got["sum", p], TO_ENDS)

    flip = jnp.where(z >= 2, 3, 0)
    line = lambda a, b: jnp.where(at_end, a, b) ^ flip
    mine, other = (lambda a, b: line(a, b) * PAIR + x), (lambda a, b: line(a, b) * PAIR + 1 - x)
    order = [mine(0, 1), mine(1, 0), other(0, 1), mine(2, 2), other(1, 2), mine(3, 3), other(2, 3), other(3, 0)]
    got["order"] = jnp.stack(order).astype(jnp.int32)
    places = [2 * half, 2 * half + 1, 2 - 2 * half, 3 - 2 * half]
    got["places"] = jnp.stack(places).astype(jnp.int32)

    got["x1"] = send(got["own"], ACROSS)
    got["a1"] = send(got["own"], ENDS)
    got["m1"] = send(got["own"], MIDDLE)
    got["out"] = dot(deltas, jnp.concatenate([columns(basis_out, 1 - half), columns(basis_out, half)], axis=1))
    got["r1"] = send(got["out"].astype(BF16), FROM_ENDS)
    fence("x1", "a1", "m1", "out", "order", "places")
    some = steps // 2
    got["x2"] = send(got["a1"], ACROSS_ENDS)
    got["x2", "m"] = send(got["m1"], ACROSS_MIDDLE)
    got["a2"] = send(got["m1"], TO_ENDS)
    got["m2"] = send(got["a1"], MIDDLE)
    blocks = [["own"], ["a1"], ["x1"]]
    got["A"] = turn([], blocks, 0, some)
    fence("x1", "x2", "a2", "m2", "out", "r1", "A")
    def columns_of(p, q):
        here = slice(p * part, q * part)
        return got["out"][:, here] + got["r1"][:, here].astype(F32)

    def cross(p):
        here = slice(p * part, (p + 1) * part)
        got["keep", p] = got["keep"][:, here] + got["m3", p]
        got["x5", p] = send(got["keep", p].astype(BF16), ACROSS_MIDDLE)

    got["x3"] = send(got["a2"], ACROSS_ENDS)
    got["m3", 0] = send(columns_of(0, 1), MIDDLE)
    got["a3"] = send(got["m2"], TO_ENDS)
    got["e"] = send(got["x1"], FROM_ENDS)
    fence(("x2", "m"), "m2", "out", "r1")
    got["x3m", 0] = send(got["m2"][:, : cuts[2] * DEEP], ACROSS_MIDDLE)
    got["give"], got["keep"] = columns_of(1, 2), columns_of(2, 4)
    more = [["a2", "m1"], ["x2", ("x2", "m")]]
    got["B"] = turn([], more, 0, some)
    fence(("m3", 0), ("x3m", 0), "give", "keep", "m2", "B")
    cross(0)
    got["m3", 1] = send(got["give"], MIDDLE)
    got["A"] = turn([got["A"], got["B"]], blocks + more, some, steps - some)
    fence("x3", "A")
    fence("a3", ("x5", 0), "A")

    def x4(piece):
        got["x4", piece] = send(got["a3"][:, cuts[piece] * DEEP : cuts[piece + 1] * DEEP], ACROSS_ENDS)

    def last(piece):
        first, count = cuts[piece], cuts[piece + 1] - cuts[piece]
        side = piece // 2
        blocks = [
            [(got["a3"], first), (got["m2"], first)],
            [(got["x3"], first), (got["x3m", side], first - side * cuts[2])],
            [(got["x4", piece], 0), (got["e"], first)],
        ]
        got["D"] = rotate([got["D"]] if piece else [], end, blocks, basis_in, first, count)

    x4(0)
    settle(0)
    fence(("x4", 0), ("m3", 1), "e", "m2", "a3", "A")
    x4(1)
    cross(1)
    got["x3m", 1] = send(got["m2"][:, cuts[2] * DEEP :], ACROSS_MIDDLE)
    last(0)
    fence(("x4", 1), ("m4", 0), ("n1", 0), ("sum", 0), ("x5", 1), "D", "a3")
    x4(2)
    got["n2", 0] = send(got["m4", 0], TO_ENDS)
    settle(1)
    got["R", 0] = pick(("n1", 0), ("sum", 0))
    last(1)
    fence(("x4", 2), ("m4", 1), ("n1", 1), ("sum", 1), ("n2", 0), ("m4", 0), ("x3m", 1), ("R", 0), "A", "D")
    got["n2", 1] = send(got["m4", 1], TO_ENDS)
    got["A2"] = swap_narrow(got["A"])
    got["R", 1] = pick(("n1", 1), ("sum", 1))
    got["R", 2] = pick(("n2", 0), ("m4", 0))
    last(2)
    fence(("n2", 1), "A2", "D")
    got["D2"] = swap_narrow(got["D"])
    got["A"] = (got["A"] + got["A2"]).astype(BF16)

    pieces = [[got["R", p]] for p in range(3)] + [[got["n2", 1], got["m4", 1]]]
    return fit(got["order"], end, [[got["A"]], [got["D"], got["D2"]]], pieces, got["places"])


def solution(mesh):
    return jax.shard_map(
        scheduled if mesh.shape["wide"] == LINE * PAIR else general,
        mesh=mesh,
        in_specs=(
            P(("grp", "wide"), "narrow"),
            P("grp", "wide"),
            P(("grp", "narrow"), "wide"),
            P(("grp", "wide"), "narrow"),
        ),
        out_specs=P(("grp", "wide"), "narrow"),
        check_vma=False,
    )
```

```python
import jax
import jax.numpy as jnp
from jax import lax
from jax.experimental import pallas as pl
from jax.experimental.pallas import tpu as pltpu
from jax.sharding import PartitionSpec as P

EX = 2
LINE, PAIR = 4, 2
DEEP = 1024
VMEM = 22 << 20
BF16, F32 = jnp.bfloat16, jnp.float32


def dot(a, b):
    return jnp.dot(a, b, preferred_element_type=F32)


def fit_kernel(counts, choices, order_ref, end_ref, place_ref, *refs):
    sum_refs, refs = refs[: sum(counts)], refs[sum(counts) :]
    piece_refs, (fit_ref, out_ref, turned_ref, rot_ref) = refs[:-4], refs[-4:]
    rows, ks = out_ref.shape
    size, seq = rows // order_ref.shape[0], rows // EX

    @pl.when(pl.program_id(0) == 0)
    def _():
        at = 0
        for piece, choice in enumerate(choices):
            width = piece_refs[at].shape[1]
            there = pl.ds(pl.multiple_of(place_ref[piece] * width, width), width)
            if choice == 1:
                out_ref[:, there] = piece_refs[at][...]
            else:
                out_ref[:, there] = jnp.where(end_ref[0] == 1, piece_refs[at][...], piece_refs[at + 1][...])
            at += choice

    slot, first = 0, 0
    for count in counts:
        halves = sum_refs[first : first + count]
        first += count
        for at in range(0, halves[0].shape[0], size):
            here = pl.ds(at, size)
            there = pl.ds(pl.multiple_of(order_ref[slot] * size, size), size)
            rot_ref[there, :] = sum(ref[here, :] for ref in halves).astype(BF16)
            slot += 1
    turned_ref[...] = rot_ref[...].T
    step = min(256, ks)
    for at in range(0, ks, step):
        total = None
        for e in range(EX):
            here = pl.ds(e * seq, seq)
            grad = dot(turned_ref[:, here], out_ref[here, pl.ds(at, step)])
            total = grad * grad if total is None else total + grad * grad
        fit_ref[:, pl.ds(at, step)] = total * (1.0 / EX)


def fit(order, end, sums, pieces, places):
    rows = sum(halves[0].shape[0] for halves in sums)
    ka = sums[0][0].shape[1]
    ks = sum(piece[0].shape[1] for piece in pieces)
    tile = 256 if ka % 256 == 0 else ka
    flat = [a for halves in sums for a in halves]
    outs = [a for piece in pieces for a in piece]
    return pl.pallas_call(
        lambda *refs: fit_kernel([len(halves) for halves in sums], [len(piece) for piece in pieces], *refs),
        out_shape=jax.ShapeDtypeStruct((ka, ks), F32),
        grid_spec=pltpu.PrefetchScalarGridSpec(
            num_scalar_prefetch=3,
            grid=(ka // tile,),
            in_specs=[pl.BlockSpec((a.shape[0], tile), lambda i, *_: (0, i)) for a in flat]
            + [pl.BlockSpec(a.shape, lambda i, *_: (0, 0)) for a in outs],
            out_specs=pl.BlockSpec((tile, ks), lambda i, *_: (i, 0)),
            scratch_shapes=[
                pltpu.VMEM((rows, ks), BF16),
                pltpu.VMEM((tile, rows), BF16),
                pltpu.VMEM((rows, tile), BF16),
            ],
        ),
        compiler_params=pltpu.CompilerParams(vmem_limit_bytes=56 << 20),
        cost_estimate=pl.CostEstimate(
            flops=2 * rows * ka * ks, bytes_accessed=8 * rows * ka + 2 * rows * ks + 4 * ka * ks, transcendentals=0
        ),
        name="fit",
    )(order, end, places, *flat, *outs)


def rotate_kernel(choices, end_ref, *refs):
    blocks = refs[: sum(choices)]
    basis_ref, *before, sum_ref, rows_ref = refs[sum(choices) :]
    size = blocks[0].shape[0]
    at = 0
    for i, choice in enumerate(choices):
        here = pl.ds(i * size, size)
        if choice == 1:
            rows_ref[here, :] = blocks[at][...]
        else:
            rows_ref[here, :] = jnp.where(end_ref[0] == 1, blocks[at][...], blocks[at + 1][...])
        at += choice

    @pl.when(pl.program_id(0) == 0)
    def _():
        if not before:
            sum_ref[...] = jnp.zeros_like(sum_ref)
        at = 0
        for ref in before:
            sum_ref[pl.ds(at, ref.shape[0]), :] = ref[...]
            at += ref.shape[0]

    sum_ref[...] += dot(rows_ref[...], basis_ref[...])


def rotate(before, end, blocks, basis, first, steps):
    flat = [pair for block in blocks for pair in block]
    size, ka = flat[0][0].shape[0], basis.shape[1]
    rows = size * len(blocks)
    specs = []
    for block in blocks:
        for which, (_, skip) in enumerate(block):
            used = lambda e, which=which, n=len(block): 1 if n == 1 else jnp.where(e[0] == 1, 1 - which, which)
            specs.append(
                pl.BlockSpec((size, DEEP), lambda k, e, used=used, skip=skip: (0, (k + skip) * used(e)))
            )
    whole = pl.BlockSpec((rows, ka), lambda k, e: (0, 0))
    arrays = [a for a, _ in flat] + [basis] + before
    return pl.pallas_call(
        lambda *refs: rotate_kernel([len(block) for block in blocks], *refs),
        out_shape=jax.ShapeDtypeStruct((rows, ka), F32),
        grid_spec=pltpu.PrefetchScalarGridSpec(
            num_scalar_prefetch=1,
            grid=(steps,),
            in_specs=specs
            + [pl.BlockSpec((DEEP, ka), lambda k, e: (first + k, 0))]
            + [pl.BlockSpec(a.shape, lambda k, e: (0, 0)) for a in before],
            out_specs=whole,
            scratch_shapes=[pltpu.VMEM((rows, DEEP), BF16)],
        ),
        compiler_params=pltpu.CompilerParams(vmem_limit_bytes=VMEM),
        cost_estimate=pl.CostEstimate(
            flops=rows * ka, bytes_accessed=4 * rows * ka, transcendentals=0
        ),
        name="rotate",
    )(end, *arrays)


def swap_narrow(a):
    return lax.ppermute(a, "narrow", [(0, 1), (1, 0)])


def general(inputs, deltas, basis_in, basis_out):
    partial_in = dot(lax.all_gather(inputs, "wide", axis=0, tiled=True), basis_in)
    rotated_out = lax.psum(dot(deltas, basis_out), "wide").astype(BF16)
    order, zero = jnp.arange(EX, dtype=jnp.int32), jnp.zeros((1,), jnp.int32)
    return fit(order, zero, [(partial_in, swap_narrow(partial_in))], [[rotated_out]], zero)


def pairs(step, where=lambda z: True):
    out = []
    for z in range(LINE):
        for x in range(PAIR):
            if where(z):
                tz, tx = step(z, x)
                out.append((z * PAIR + x, tz * PAIR + tx))
    return out


def corner(z):
    return z in (0, LINE - 1)


def middle(z):
    return not corner(z)


ENDS = pairs(lambda z, x: (z ^ 1, x))
TO_ENDS = pairs(lambda z, x: (z ^ 1, x), middle)
FROM_ENDS = pairs(lambda z, x: (z ^ 1, x), corner)
MIDDLE = pairs(lambda z, x: (3 - z, x), middle)
ACROSS = pairs(lambda z, x: (z, 1 - x))
ACROSS_ENDS = pairs(lambda z, x: (z, 1 - x), corner)
ACROSS_MIDDLE = pairs(lambda z, x: (z, 1 - x), middle)


def send(a, perm):
    return lax.ppermute(a, "wide", perm)


def scheduled(inputs, deltas, basis_in, basis_out):
    w = lax.axis_index("wide")
    z, x = w // PAIR, w % PAIR
    at_end = (z == 0) | (z == LINE - 1)
    end = at_end.astype(jnp.int32).reshape(1)
    half = (z >= 2).astype(jnp.int32)
    steps = inputs.shape[1] // DEEP
    cuts = [0, 3 * steps // 14, 10 * steps // 14, steps]
    middle = 6 * steps // 14
    part = basis_out.shape[1] // 4
    got = {"own": inputs}

    def fence(*names):
        got.update(zip(names, lax.optimization_barrier(tuple(got[n] for n in names))))

    def pick(a, b):
        return jnp.where(at_end, got[a], got[b])

    def columns(a, h):
        return lax.dynamic_slice_in_dim(a, h * 2 * part, 2 * part, 1)

    def turn(before, blocks, first, count):
        return rotate(before, end, [[(got[n], first) for n in block] for block in blocks], basis_in, first, count)

    flip = jnp.where(z >= 2, 3, 0)
    line = lambda a, b: jnp.where(at_end, a, b) ^ flip
    mine, other = (lambda a, b: line(a, b) * PAIR + x), (lambda a, b: line(a, b) * PAIR + 1 - x)
    order = [mine(0, 1), mine(1, 0), other(0, 1), mine(2, 2), other(1, 2), mine(3, 3), other(2, 3), other(3, 0)]
    got["order"] = jnp.stack(order).astype(jnp.int32)
    places = [2 * half, 2 * half + 1, 2 - 2 * half, 3 - 2 * half]
    got["places"] = jnp.stack(places).astype(jnp.int32)

    got["x1"] = send(got["own"], ACROSS)
    got["a1"] = send(got["own"], ENDS)
    got["m1"] = send(got["own"], MIDDLE)
    got["out"] = dot(deltas, jnp.concatenate([columns(basis_out, 1 - half), columns(basis_out, half)], axis=1))
    got["r1"] = send(got["out"].astype(BF16), FROM_ENDS)
    fence("x1", "a1", "m1", "out", "order", "places")
    some = steps // 2
    got["x2"] = send(got["a1"], ACROSS_ENDS)
    got["x2", "m"] = send(got["m1"], ACROSS_MIDDLE)
    got["a2"] = send(got["m1"], TO_ENDS)
    got["m2"] = send(got["a1"], MIDDLE)
    blocks = [["own"], ["a1"], ["x1"]]
    got["A"] = turn([], blocks, 0, some)
    fence("x1", "x2", "a2", "m2", "out", "r1", "A")
    cut = 2 * part
    got["x3"] = send(got["a2"], ACROSS_ENDS)
    got["m3"] = send((got["out"][:, :cut] + got["r1"][:, :cut].astype(F32)).astype(BF16), MIDDLE)
    got["a3"] = send(got["m2"], TO_ENDS)
    got["e"] = send(got["x1"], FROM_ENDS)
    fence(("x2", "m"), "m2", "out", "r1")
    got["x3m", 0] = send(got["m2"][:, : middle * DEEP], ACROSS_MIDDLE)
    got["keep"] = got["out"][:, cut:] + got["r1"][:, cut:].astype(F32)
    more = [["a2", "m1"], ["x2", ("x2", "m")]]
    got["B"] = turn([], more, 0, some)
    fence("m3", ("x3m", 0), "keep", "m2", "B")
    got["keep"] += got["m3"].astype(F32)
    got["x5"] = send(got["keep"].astype(BF16), ACROSS_MIDDLE)
    got["x3m", 1] = send(got["m2"][:, middle * DEEP :], ACROSS_MIDDLE)
    got["A"] = turn([got["A"], got["B"]], blocks + more, some, steps - some)
    fence("x3", "A")
    fence("a3", "A")

    def x4(piece):
        got["x4", piece] = send(got["a3"][:, cuts[piece] * DEEP : cuts[piece + 1] * DEEP], ACROSS_ENDS)

    def last(piece, first, until):
        side = int(first >= middle)
        blocks = [
            [(got["a3"], first), (got["m2"], first)],
            [(got["x3"], first), (got["x3m", side], first - side * middle)],
            [(got["x4", piece], first - cuts[piece]), (got["e"], first)],
        ]
        got["D"] = rotate([got["D"]] if first else [], end, blocks, basis_in, first, until - first)

    x4(0)
    fence(("x4", 0), "x5", "e", "keep", "a3", "A")
    got["sum"] = (got["keep"] + got["x5"].astype(F32)).astype(BF16)
    got["m4"] = send(got["sum"], MIDDLE)
    got["n1"] = send(got["sum"], TO_ENDS)
    x4(1)
    last(0, 0, cuts[1])
    fence("m4", "n1", "sum", ("x4", 1), ("x3m", 1), "a3", "A", "D")
    got["n2", 0] = send(got["m4"][:, :part], TO_ENDS)
    x4(2)
    got["A2"] = swap_narrow(got["A"])
    got["R", 0] = pick("n1", "sum")
    last(1, cuts[1], middle)
    last(1, middle, cuts[2])
    fence(("x4", 2), ("n2", 0), "m4", ("R", 0), "A", "A2", "D")
    got["n2", 1] = send(got["m4"][:, part:], TO_ENDS)
    got["R", 1] = jnp.where(at_end, got["n2", 0], got["m4"][:, :part])
    last(2, cuts[2], steps)
    fence(("n2", 1), "D")
    got["D2"] = swap_narrow(got["D"])
    got["A"] = (got["A"] + got["A2"]).astype(BF16)

    pieces = [[got["R", 0][:, p * part : (p + 1) * part]] for p in range(2)]
    pieces = pieces + [[got["R", 1]], [got["n2", 1], got["m4"][:, part:]]]
    return fit(got["order"], end, [[got["A"]], [got["D"], got["D2"]]], pieces, got["places"])


def solution(mesh):
    return jax.shard_map(
        scheduled if mesh.shape["wide"] == LINE * PAIR else general,
        mesh=mesh,
        in_specs=(
            P(("grp", "wide"), "narrow"),
            P("grp", "wide"),
            P(("grp", "narrow"), "wide"),
            P(("grp", "wide"), "narrow"),
        ),
        out_specs=P(("grp", "wide"), "narrow"),
        check_vma=False,
    )
```

```python
import jax
import jax.numpy as jnp
from jax import lax
from jax.experimental import pallas as pl
from jax.experimental.pallas import tpu as pltpu
from jax.sharding import PartitionSpec as P

EX = 2
LINE, PAIR = 4, 2
DEEP = 1024
VMEM = 22 << 20
BF16, F32 = jnp.bfloat16, jnp.float32


def dot(a, b):
    return jnp.dot(a, b, preferred_element_type=F32)


def fit_kernel(counts, choices, order_ref, end_ref, place_ref, *refs):
    sum_refs, refs = refs[: sum(counts)], refs[sum(counts) :]
    piece_refs, (fit_ref, out_ref, turned_ref, rot_ref) = refs[:-4], refs[-4:]
    rows, ks = out_ref.shape
    size, seq = rows // order_ref.shape[0], rows // EX

    @pl.when(pl.program_id(0) == 0)
    def _():
        at = 0
        for piece, choice in enumerate(choices):
            width = piece_refs[at].shape[1]
            there = pl.ds(pl.multiple_of(place_ref[piece] * width, width), width)
            if choice == 1:
                out_ref[:, there] = piece_refs[at][...]
            else:
                out_ref[:, there] = jnp.where(end_ref[0] == 1, piece_refs[at][...], piece_refs[at + 1][...])
            at += choice

    slot, first = 0, 0
    for count in counts:
        halves = sum_refs[first : first + count]
        first += count
        for at in range(0, halves[0].shape[0], size):
            here = pl.ds(at, size)
            there = pl.ds(pl.multiple_of(order_ref[slot] * size, size), size)
            rot_ref[there, :] = sum(ref[here, :] for ref in halves).astype(BF16)
            slot += 1
    turned_ref[...] = rot_ref[...].T
    step = min(256, ks)
    for at in range(0, ks, step):
        total = None
        for e in range(EX):
            here = pl.ds(e * seq, seq)
            grad = dot(turned_ref[:, here], out_ref[here, pl.ds(at, step)])
            total = grad * grad if total is None else total + grad * grad
        fit_ref[:, pl.ds(at, step)] = total * (1.0 / EX)


def fit(order, end, sums, pieces, places):
    rows = sum(halves[0].shape[0] for halves in sums)
    ka = sums[0][0].shape[1]
    ks = sum(piece[0].shape[1] for piece in pieces)
    tile = 256 if ka % 256 == 0 else ka
    flat = [a for halves in sums for a in halves]
    outs = [a for piece in pieces for a in piece]
    return pl.pallas_call(
        lambda *refs: fit_kernel([len(halves) for halves in sums], [len(piece) for piece in pieces], *refs),
        out_shape=jax.ShapeDtypeStruct((ka, ks), F32),
        grid_spec=pltpu.PrefetchScalarGridSpec(
            num_scalar_prefetch=3,
            grid=(ka // tile,),
            in_specs=[pl.BlockSpec((a.shape[0], tile), lambda i, *_: (0, i)) for a in flat]
            + [pl.BlockSpec(a.shape, lambda i, *_: (0, 0)) for a in outs],
            out_specs=pl.BlockSpec((tile, ks), lambda i, *_: (i, 0)),
            scratch_shapes=[
                pltpu.VMEM((rows, ks), BF16),
                pltpu.VMEM((tile, rows), BF16),
                pltpu.VMEM((rows, tile), BF16),
            ],
        ),
        compiler_params=pltpu.CompilerParams(vmem_limit_bytes=56 << 20),
        cost_estimate=pl.CostEstimate(
            flops=2 * rows * ka * ks, bytes_accessed=8 * rows * ka + 2 * rows * ks + 4 * ka * ks, transcendentals=0
        ),
        name="fit",
    )(order, end, places, *flat, *outs)


def rotate_kernel(choices, end_ref, *refs):
    blocks = refs[: sum(choices)]
    basis_ref, *before, sum_ref, rows_ref = refs[sum(choices) :]
    size = blocks[0].shape[0]
    at = 0
    for i, choice in enumerate(choices):
        here = pl.ds(i * size, size)
        if choice == 1:
            rows_ref[here, :] = blocks[at][...]
        else:
            rows_ref[here, :] = jnp.where(end_ref[0] == 1, blocks[at][...], blocks[at + 1][...])
        at += choice

    @pl.when(pl.program_id(0) == 0)
    def _():
        if not before:
            sum_ref[...] = jnp.zeros_like(sum_ref)
        at = 0
        for ref in before:
            sum_ref[pl.ds(at, ref.shape[0]), :] = ref[...]
            at += ref.shape[0]

    sum_ref[...] += dot(rows_ref[...], basis_ref[...])


def rotate(before, end, blocks, basis, first, steps):
    flat = [pair for block in blocks for pair in block]
    size, ka = flat[0][0].shape[0], basis.shape[1]
    rows = size * len(blocks)
    specs = []
    for block in blocks:
        for which, (_, skip) in enumerate(block):
            used = lambda e, which=which, n=len(block): 1 if n == 1 else jnp.where(e[0] == 1, 1 - which, which)
            specs.append(
                pl.BlockSpec((size, DEEP), lambda k, e, used=used, skip=skip: (0, (k + skip) * used(e)))
            )
    whole = pl.BlockSpec((rows, ka), lambda k, e: (0, 0))
    arrays = [a for a, _ in flat] + [basis] + before
    return pl.pallas_call(
        lambda *refs: rotate_kernel([len(block) for block in blocks], *refs),
        out_shape=jax.ShapeDtypeStruct((rows, ka), F32),
        grid_spec=pltpu.PrefetchScalarGridSpec(
            num_scalar_prefetch=1,
            grid=(steps,),
            in_specs=specs
            + [pl.BlockSpec((DEEP, ka), lambda k, e: (first + k, 0))]
            + [pl.BlockSpec(a.shape, lambda k, e: (0, 0)) for a in before],
            out_specs=whole,
            scratch_shapes=[pltpu.VMEM((rows, DEEP), BF16)],
        ),
        compiler_params=pltpu.CompilerParams(vmem_limit_bytes=VMEM),
        cost_estimate=pl.CostEstimate(
            flops=rows * ka, bytes_accessed=4 * rows * ka, transcendentals=0
        ),
        name="rotate",
    )(end, *arrays)


def swap_narrow(a):
    return lax.ppermute(a, "narrow", [(0, 1), (1, 0)])


def general(inputs, deltas, basis_in, basis_out):
    partial_in = dot(lax.all_gather(inputs, "wide", axis=0, tiled=True), basis_in)
    rotated_out = lax.psum(dot(deltas, basis_out), "wide").astype(BF16)
    order, zero = jnp.arange(EX, dtype=jnp.int32), jnp.zeros((1,), jnp.int32)
    return fit(order, zero, [(partial_in, swap_narrow(partial_in))], [[rotated_out]], zero)


def pairs(step, where=lambda z: True):
    out = []
    for z in range(LINE):
        for x in range(PAIR):
            if where(z):
                tz, tx = step(z, x)
                out.append((z * PAIR + x, tz * PAIR + tx))
    return out


def corner(z):
    return z in (0, LINE - 1)


def middle(z):
    return not corner(z)


ENDS = pairs(lambda z, x: (z ^ 1, x))
TO_ENDS = pairs(lambda z, x: (z ^ 1, x), middle)
FROM_ENDS = pairs(lambda z, x: (z ^ 1, x), corner)
MIDDLE = pairs(lambda z, x: (3 - z, x), middle)
ACROSS = pairs(lambda z, x: (z, 1 - x))
ACROSS_ENDS = pairs(lambda z, x: (z, 1 - x), corner)
ACROSS_MIDDLE = pairs(lambda z, x: (z, 1 - x), middle)


def send(a, perm):
    return lax.ppermute(a, "wide", perm)


def scheduled(inputs, deltas, basis_in, basis_out):
    w = lax.axis_index("wide")
    z, x = w // PAIR, w % PAIR
    at_end = (z == 0) | (z == LINE - 1)
    end = at_end.astype(jnp.int32).reshape(1)
    half = (z >= 2).astype(jnp.int32)
    steps = inputs.shape[1] // DEEP
    cuts = [0, 3 * steps // 14, 10 * steps // 14, steps]
    middle = 6 * steps // 14
    part = basis_out.shape[1] // 4
    got = {"own": inputs}

    def fence(*names):
        got.update(zip(names, lax.optimization_barrier(tuple(got[n] for n in names))))

    def pick(a, b):
        return jnp.where(at_end, got[a], got[b])

    def columns(a, h):
        return lax.dynamic_slice_in_dim(a, h * 2 * part, 2 * part, 1)

    def turn(before, blocks, first, count):
        return rotate(before, end, [[(got[n], first) for n in block] for block in blocks], basis_in, first, count)

    flip = jnp.where(z >= 2, 3, 0)
    line = lambda a, b: jnp.where(at_end, a, b) ^ flip
    mine, other = (lambda a, b: line(a, b) * PAIR + x), (lambda a, b: line(a, b) * PAIR + 1 - x)
    order = [mine(0, 1), mine(1, 0), other(0, 1), mine(2, 2), other(1, 2), mine(3, 3), other(2, 3), other(3, 0)]
    got["order"] = jnp.stack(order).astype(jnp.int32)
    got["places"] = jnp.stack([half, 1 - half])

    got["x1"] = send(got["own"], ACROSS)
    got["a1"] = send(got["own"], ENDS)
    got["m1"] = send(got["own"], MIDDLE)
    got["out"] = dot(deltas, jnp.concatenate([columns(basis_out, 1 - half), columns(basis_out, half)], axis=1))
    got["r1"] = send(got["out"].astype(BF16), FROM_ENDS)
    fence("x1", "a1", "m1", "out", "order", "places")
    some = steps // 2
    got["x2"] = send(got["a1"], ACROSS_ENDS)
    got["x2", "m"] = send(got["m1"], ACROSS_MIDDLE)
    got["a2"] = send(got["m1"], TO_ENDS)
    got["m2"] = send(got["a1"], MIDDLE)
    blocks = [["own"], ["a1"], ["x1"]]
    got["A"] = turn([], blocks, 0, some)
    fence("x1", "x2", "a2", "m2", "out", "r1", "A")
    cut = 2 * part
    got["x3"] = send(got["a2"], ACROSS_ENDS)
    got["m3"] = send((got["out"][:, :cut] + got["r1"][:, :cut].astype(F32)).astype(BF16), MIDDLE)
    got["a3"] = send(got["m2"], TO_ENDS)
    got["e"] = send(got["x1"], FROM_ENDS)
    fence(("x2", "m"), "m2", "out", "r1")
    got["x3m", 0] = send(got["m2"][:, : middle * DEEP], ACROSS_MIDDLE)
    got["keep"] = got["out"][:, cut:] + got["r1"][:, cut:].astype(F32)
    more = [["a2", "m1"], ["x2", ("x2", "m")]]
    got["B"] = turn([], more, 0, some)
    fence("m3", ("x3m", 0), "keep", "m2", "B")
    got["keep"] += got["m3"].astype(F32)
    got["x5"] = send(got["keep"].astype(BF16), ACROSS_MIDDLE)
    got["x3m", 1] = send(got["m2"][:, middle * DEEP :], ACROSS_MIDDLE)
    got["A"] = turn([got["A"], got["B"]], blocks + more, some, steps - some)
    fence("x3", "A")
    fence("a3", "A")

    def x4(piece):
        got["x4", piece] = send(got["a3"][:, cuts[piece] * DEEP : cuts[piece + 1] * DEEP], ACROSS_ENDS)

    def last(piece, first, until):
        side = int(first >= middle)
        blocks = [
            [(got["a3"], first), (got["m2"], first)],
            [(got["x3"], first), (got["x3m", side], first - side * middle)],
            [(got["x4", piece], first - cuts[piece]), (got["e"], first)],
        ]
        got["D"] = rotate([got["D"]] if first else [], end, blocks, basis_in, first, until - first)

    x4(0)
    fence(("x4", 0), "x5", "e", "keep", "a3", "A")
    got["sum"] = (got["keep"] + got["x5"].astype(F32)).astype(BF16)
    got["m4"] = send(got["sum"], MIDDLE)
    got["n1"] = send(got["sum"], TO_ENDS)
    x4(1)
    last(0, 0, cuts[1])
    fence(("x4", 1), ("x3m", 1), "m4", "n1", "sum", "a3", "A", "D")
    x4(2)
    got["n2"] = send(got["m4"], TO_ENDS)
    got["A2"] = swap_narrow(got["A"])
    got["R"] = pick("n1", "sum")
    last(1, cuts[1], middle)
    last(1, middle, cuts[2])
    fence(("x4", 2), "A", "A2", "R", "D")
    late = (cuts[2] + steps) // 2
    last(2, cuts[2], late)
    fence("n2", "m4", "R", "A", "A2", "D")
    last(2, late, steps)
    got["D2"] = swap_narrow(got["D"])
    got["A"] = (got["A"] + got["A2"]).astype(BF16)

    pieces, places = [[got["R"]], [got["n2"], got["m4"]]], got["places"]
    return fit(got["order"], end, [[got["A"]], [got["D"], got["D2"]]], pieces, places)


def solution(mesh):
    return jax.shard_map(
        scheduled if mesh.shape["wide"] == LINE * PAIR else general,
        mesh=mesh,
        in_specs=(
            P(("grp", "wide"), "narrow"),
            P("grp", "wide"),
            P(("grp", "narrow"), "wide"),
            P(("grp", "wide"), "narrow"),
        ),
        out_specs=P(("grp", "wide"), "narrow"),
        check_vma=False,
    )
```

```python
import jax
import jax.numpy as jnp
from jax import lax
from jax.experimental import pallas as pl
from jax.experimental.pallas import tpu as pltpu
from jax.sharding import PartitionSpec as P

EX = 2
LINE, PAIR = 4, 2
DEEP = 1024
VMEM = 22 << 20
BF16, F32 = jnp.bfloat16, jnp.float32


def dot(a, b):
    return jnp.dot(a, b, preferred_element_type=F32)


def fit_kernel(counts, choices, order_ref, end_ref, place_ref, *refs):
    sum_refs, refs = refs[: sum(counts)], refs[sum(counts) :]
    piece_refs, (fit_ref, out_ref, turned_ref, rot_ref) = refs[:-4], refs[-4:]
    rows, ks = out_ref.shape
    size, seq = rows // order_ref.shape[0], rows // EX

    @pl.when(pl.program_id(0) == 0)
    def _():
        at = 0
        for piece, choice in enumerate(choices):
            width = piece_refs[at].shape[1]
            there = pl.ds(pl.multiple_of(place_ref[piece] * width, width), width)
            if choice == 1:
                out_ref[:, there] = piece_refs[at][...]
            else:
                out_ref[:, there] = jnp.where(end_ref[0] == 1, piece_refs[at][...], piece_refs[at + 1][...])
            at += choice

    slot, first = 0, 0
    for count in counts:
        halves = sum_refs[first : first + count]
        first += count
        for at in range(0, halves[0].shape[0], size):
            here = pl.ds(at, size)
            there = pl.ds(pl.multiple_of(order_ref[slot] * size, size), size)
            rot_ref[there, :] = sum(ref[here, :] for ref in halves).astype(BF16)
            slot += 1
    turned_ref[...] = rot_ref[...].T
    step = min(256, ks)
    for at in range(0, ks, step):
        total = None
        for e in range(EX):
            here = pl.ds(e * seq, seq)
            grad = dot(turned_ref[:, here], out_ref[here, pl.ds(at, step)])
            total = grad * grad if total is None else total + grad * grad
        fit_ref[:, pl.ds(at, step)] = total * (1.0 / EX)


def fit(order, end, sums, pieces, places):
    rows = sum(halves[0].shape[0] for halves in sums)
    ka = sums[0][0].shape[1]
    ks = sum(piece[0].shape[1] for piece in pieces)
    tile = 256 if ka % 256 == 0 else ka
    flat = [a for halves in sums for a in halves]
    outs = [a for piece in pieces for a in piece]
    return pl.pallas_call(
        lambda *refs: fit_kernel([len(halves) for halves in sums], [len(piece) for piece in pieces], *refs),
        out_shape=jax.ShapeDtypeStruct((ka, ks), F32),
        grid_spec=pltpu.PrefetchScalarGridSpec(
            num_scalar_prefetch=3,
            grid=(ka // tile,),
            in_specs=[pl.BlockSpec((a.shape[0], tile), lambda i, *_: (0, i)) for a in flat]
            + [pl.BlockSpec(a.shape, lambda i, *_: (0, 0)) for a in outs],
            out_specs=pl.BlockSpec((tile, ks), lambda i, *_: (i, 0)),
            scratch_shapes=[
                pltpu.VMEM((rows, ks), BF16),
                pltpu.VMEM((tile, rows), BF16),
                pltpu.VMEM((rows, tile), BF16),
            ],
        ),
        compiler_params=pltpu.CompilerParams(vmem_limit_bytes=56 << 20),
        cost_estimate=pl.CostEstimate(
            flops=2 * rows * ka * ks, bytes_accessed=8 * rows * ka + 2 * rows * ks + 4 * ka * ks, transcendentals=0
        ),
        name="fit",
    )(order, end, places, *flat, *outs)


def rotate_kernel(choices, end_ref, *refs):
    blocks = refs[: sum(choices)]
    basis_ref, *before, sum_ref, rows_ref = refs[sum(choices) :]
    size = blocks[0].shape[0]
    at = 0
    for i, choice in enumerate(choices):
        here = pl.ds(i * size, size)
        if choice == 1:
            rows_ref[here, :] = blocks[at][...]
        else:
            rows_ref[here, :] = jnp.where(end_ref[0] == 1, blocks[at][...], blocks[at + 1][...])
        at += choice

    @pl.when(pl.program_id(0) == 0)
    def _():
        if not before:
            sum_ref[...] = jnp.zeros_like(sum_ref)
        at = 0
        for ref in before:
            sum_ref[pl.ds(at, ref.shape[0]), :] = ref[...]
            at += ref.shape[0]

    sum_ref[...] += dot(rows_ref[...], basis_ref[...])


def rotate(before, end, blocks, basis, first, steps):
    flat = [pair for block in blocks for pair in block]
    size, ka = flat[0][0].shape[0], basis.shape[1]
    rows = size * len(blocks)
    specs = []
    for block in blocks:
        for which, (_, skip) in enumerate(block):
            used = lambda e, which=which, n=len(block): 1 if n == 1 else jnp.where(e[0] == 1, 1 - which, which)
            specs.append(
                pl.BlockSpec((size, DEEP), lambda k, e, used=used, skip=skip: (0, (k + skip) * used(e)))
            )
    whole = pl.BlockSpec((rows, ka), lambda k, e: (0, 0))
    arrays = [a for a, _ in flat] + [basis] + before
    return pl.pallas_call(
        lambda *refs: rotate_kernel([len(block) for block in blocks], *refs),
        out_shape=jax.ShapeDtypeStruct((rows, ka), F32),
        grid_spec=pltpu.PrefetchScalarGridSpec(
            num_scalar_prefetch=1,
            grid=(steps,),
            in_specs=specs
            + [pl.BlockSpec((DEEP, ka), lambda k, e: (first + k, 0))]
            + [pl.BlockSpec(a.shape, lambda k, e: (0, 0)) for a in before],
            out_specs=whole,
            scratch_shapes=[pltpu.VMEM((rows, DEEP), BF16)],
        ),
        compiler_params=pltpu.CompilerParams(vmem_limit_bytes=VMEM),
        cost_estimate=pl.CostEstimate(
            flops=rows * ka, bytes_accessed=4 * rows * ka, transcendentals=0
        ),
        name="rotate",
    )(end, *arrays)


def swap_narrow(a):
    return lax.ppermute(a, "narrow", [(0, 1), (1, 0)])


def general(inputs, deltas, basis_in, basis_out):
    partial_in = dot(lax.all_gather(inputs, "wide", axis=0, tiled=True), basis_in)
    rotated_out = lax.psum(dot(deltas, basis_out), "wide").astype(BF16)
    order, zero = jnp.arange(EX, dtype=jnp.int32), jnp.zeros((1,), jnp.int32)
    return fit(order, zero, [(partial_in, swap_narrow(partial_in))], [[rotated_out]], zero)


def pairs(step, where=lambda z: True):
    out = []
    for z in range(LINE):
        for x in range(PAIR):
            if where(z):
                tz, tx = step(z, x)
                out.append((z * PAIR + x, tz * PAIR + tx))
    return out


def corner(z):
    return z in (0, LINE - 1)


def middle(z):
    return not corner(z)


ENDS = pairs(lambda z, x: (z ^ 1, x))
TO_ENDS = pairs(lambda z, x: (z ^ 1, x), middle)
FROM_ENDS = pairs(lambda z, x: (z ^ 1, x), corner)
MIDDLE = pairs(lambda z, x: (3 - z, x), middle)
ACROSS = pairs(lambda z, x: (z, 1 - x))
ACROSS_ENDS = pairs(lambda z, x: (z, 1 - x), corner)
ACROSS_MIDDLE = pairs(lambda z, x: (z, 1 - x), middle)


def send(a, perm):
    return lax.ppermute(a, "wide", perm)


def scheduled(inputs, deltas, basis_in, basis_out):
    w = lax.axis_index("wide")
    z, x = w // PAIR, w % PAIR
    at_end = (z == 0) | (z == LINE - 1)
    end = at_end.astype(jnp.int32).reshape(1)
    half = (z >= 2).astype(jnp.int32)
    steps = inputs.shape[1] // DEEP
    cuts = [0, 6 * steps // 14, 10 * steps // 14, steps]
    part = basis_out.shape[1] // 4
    got = {"own": inputs}

    def fence(*names):
        got.update(zip(names, lax.optimization_barrier(tuple(got[n] for n in names))))

    def pick(a, b):
        return jnp.where(at_end, got[a], got[b])

    def columns(a, h):
        return lax.dynamic_slice_in_dim(a, h * 2 * part, 2 * part, 1)

    def turn(before, blocks, first, count):
        return rotate(before, end, [[(got[n], first) for n in block] for block in blocks], basis_in, first, count)

    flip = jnp.where(z >= 2, 3, 0)
    line = lambda a, b: jnp.where(at_end, a, b) ^ flip
    mine, other = (lambda a, b: line(a, b) * PAIR + x), (lambda a, b: line(a, b) * PAIR + 1 - x)
    order = [mine(0, 1), mine(1, 0), other(0, 1), mine(2, 2), other(1, 2), mine(3, 3), other(2, 3), other(3, 0)]
    got["order"] = jnp.stack(order).astype(jnp.int32)
    got["places"] = jnp.stack([half, 1 - half])

    got["x1"] = send(got["own"], ACROSS)
    got["a1"] = send(got["own"], ENDS)
    got["m1"] = send(got["own"], MIDDLE)
    got["out"] = dot(deltas, jnp.concatenate([columns(basis_out, 1 - half), columns(basis_out, half)], axis=1))
    got["r1"] = send(got["out"].astype(BF16), FROM_ENDS)
    fence("x1", "a1", "m1", "out", "order", "places")
    some = steps // 2
    got["x2"] = send(got["a1"], ACROSS_ENDS)
    got["x2", "m"] = send(got["m1"], ACROSS_MIDDLE)
    got["a2"] = send(got["m1"], TO_ENDS)
    got["m2"] = send(got["a1"], MIDDLE)
    blocks = [["own"], ["a1"], ["x1"]]
    got["A"] = turn([], blocks, 0, some)
    cut = 2 * part
    fence("r1", "out", "A")
    got["give"] = (got["out"][:, :cut] + got["r1"][:, :cut].astype(F32)).astype(BF16)
    fence("x1", "x2", "a2", "m2", "out", "r1", "give", "A")
    got["x3"] = send(got["a2"], ACROSS_ENDS)
    got["m3"] = send(got["give"], MIDDLE)
    got["a3"] = send(got["m2"], TO_ENDS)
    got["e"] = send(got["x1"], FROM_ENDS)
    fence(("x2", "m"), "m2", "out", "r1")
    got["x3m", 0] = send(got["m2"][:, : cuts[1] * DEEP], ACROSS_MIDDLE)
    got["keep"] = got["out"][:, cut:] + got["r1"][:, cut:].astype(F32)
    fence("keep", ("x2", "m"))
    more = [["a2", "m1"], ["x2", ("x2", "m")]]
    got["B"] = turn([], more, 0, some)
    fence("m3", ("x3m", 0), "keep", "m2", "B")
    got["keep"] += got["m3"].astype(F32)
    got["x5"] = send(got["keep"].astype(BF16), ACROSS_MIDDLE)
    got["x3m", 1] = send(got["m2"][:, cuts[1] * DEEP :], ACROSS_MIDDLE)
    got["A"] = turn([got["A"], got["B"]], blocks + more, some, steps - some)
    fence("x3", "A")
    fence("a3", "A")

    def x4(piece):
        got["x4", piece] = send(got["a3"][:, cuts[piece] * DEEP : cuts[piece + 1] * DEEP], ACROSS_ENDS)

    def last(piece):
        first, until, side = cuts[piece], cuts[piece + 1], int(piece > 0)
        blocks = [
            [(got["a3"], first), (got["m2"], first)],
            [(got["x3"], first), (got["x3m", side], first - side * cuts[1])],
            [(got["x4", piece], 0), (got["e"], first)],
        ]
        got["D"] = rotate([got["D"]] if piece else [], end, blocks, basis_in, first, until - first)

    x4(0)
    fence("x5", "e", "keep", "A")
    got["sum"] = (got["keep"] + got["x5"].astype(F32)).astype(BF16)
    got["m4"] = send(got["sum"], MIDDLE)
    got["n1"] = send(got["sum"], TO_ENDS)
    fence(("x4", 0), "a3", "A", "sum")
    x4(1)
    last(0)
    fence(("x4", 1), ("x3m", 1), "m4", "n1", "sum", "a3", "A", "D")
    x4(2)
    got["n2"] = send(got["m4"], TO_ENDS)
    got["A2"] = swap_narrow(got["A"])
    got["R"] = pick("n1", "sum")
    last(1)
    fence(("x4", 2), "A", "A2", "R", "D")
    last(2)
    fence("n2", "m4", "R", "A", "A2", "D")
    got["D2"] = swap_narrow(got["D"])
    got["A"] = (got["A"] + got["A2"]).astype(BF16)

    pieces, places = [[got["R"]], [got["n2"], got["m4"]]], got["places"]
    return fit(got["order"], end, [[got["A"]], [got["D"], got["D2"]]], pieces, places)


def solution(mesh):
    return jax.shard_map(
        scheduled if mesh.shape["wide"] == LINE * PAIR else general,
        mesh=mesh,
        in_specs=(
            P(("grp", "wide"), "narrow"),
            P("grp", "wide"),
            P(("grp", "narrow"), "wide"),
            P(("grp", "wide"), "narrow"),
        ),
        out_specs=P(("grp", "wide"), "narrow"),
        check_vma=False,
    )
```

```python
import jax
import jax.numpy as jnp
from jax import lax
from jax.experimental import pallas as pl
from jax.experimental.pallas import tpu as pltpu
from jax.sharding import PartitionSpec as P

EX = 2
LINE, PAIR = 4, 2
DEEP = 1024
VMEM = 22 << 20
BF16, F32 = jnp.bfloat16, jnp.float32


def dot(a, b):
    return jnp.dot(a, b, preferred_element_type=F32)


def fit_kernel(counts, choices, order_ref, end_ref, place_ref, *refs):
    sum_refs, refs = refs[: sum(counts)], refs[sum(counts) :]
    piece_refs, (fit_ref, out_ref, turned_ref, rot_ref) = refs[:-4], refs[-4:]
    rows, ks = out_ref.shape
    size, seq = rows // order_ref.shape[0], rows // EX

    @pl.when(pl.program_id(0) == 0)
    def _():
        at = 0
        for piece, choice in enumerate(choices):
            width = piece_refs[at].shape[1]
            there = pl.ds(pl.multiple_of(place_ref[piece] * width, width), width)
            if choice == 1:
                out_ref[:, there] = piece_refs[at][...]
            else:
                out_ref[:, there] = jnp.where(end_ref[0] == 1, piece_refs[at][...], piece_refs[at + 1][...])
            at += choice

    slot, first = 0, 0
    for count in counts:
        halves = sum_refs[first : first + count]
        first += count
        for at in range(0, halves[0].shape[0], size):
            here = pl.ds(at, size)
            there = pl.ds(pl.multiple_of(order_ref[slot] * size, size), size)
            rot_ref[there, :] = sum(ref[here, :] for ref in halves).astype(BF16)
            slot += 1
    turned_ref[...] = rot_ref[...].T
    step = min(256, ks)
    for at in range(0, ks, step):
        total = None
        for e in range(EX):
            here = pl.ds(e * seq, seq)
            grad = dot(turned_ref[:, here], out_ref[here, pl.ds(at, step)])
            total = grad * grad if total is None else total + grad * grad
        fit_ref[:, pl.ds(at, step)] = total * (1.0 / EX)


def fit(order, end, sums, pieces, places):
    rows = sum(halves[0].shape[0] for halves in sums)
    ka = sums[0][0].shape[1]
    ks = sum(piece[0].shape[1] for piece in pieces)
    tile = 256 if ka % 256 == 0 else ka
    flat = [a for halves in sums for a in halves]
    outs = [a for piece in pieces for a in piece]
    return pl.pallas_call(
        lambda *refs: fit_kernel([len(halves) for halves in sums], [len(piece) for piece in pieces], *refs),
        out_shape=jax.ShapeDtypeStruct((ka, ks), F32),
        grid_spec=pltpu.PrefetchScalarGridSpec(
            num_scalar_prefetch=3,
            grid=(ka // tile,),
            in_specs=[pl.BlockSpec((a.shape[0], tile), lambda i, *_: (0, i)) for a in flat]
            + [pl.BlockSpec(a.shape, lambda i, *_: (0, 0)) for a in outs],
            out_specs=pl.BlockSpec((tile, ks), lambda i, *_: (i, 0)),
            scratch_shapes=[
                pltpu.VMEM((rows, ks), BF16),
                pltpu.VMEM((tile, rows), BF16),
                pltpu.VMEM((rows, tile), BF16),
            ],
        ),
        compiler_params=pltpu.CompilerParams(vmem_limit_bytes=32 << 20),
        cost_estimate=pl.CostEstimate(
            flops=2 * rows * ka * ks, bytes_accessed=8 * rows * ka + 2 * rows * ks + 4 * ka * ks, transcendentals=0
        ),
        name="fit",
    )(order, end, places, *flat, *outs)


def rotate_kernel(choices, end_ref, *refs):
    blocks = refs[: sum(choices)]
    basis_ref, *before, sum_ref, rows_ref = refs[sum(choices) :]
    size = blocks[0].shape[0]
    at = 0
    for i, choice in enumerate(choices):
        here = pl.ds(i * size, size)
        if choice == 1:
            rows_ref[here, :] = blocks[at][...]
        else:
            rows_ref[here, :] = jnp.where(end_ref[0] == 1, blocks[at][...], blocks[at + 1][...])
        at += choice

    @pl.when(pl.program_id(0) == 0)
    def _():
        if not before:
            sum_ref[...] = jnp.zeros_like(sum_ref)
        at = 0
        for ref in before:
            sum_ref[pl.ds(at, ref.shape[0]), :] = ref[...]
            at += ref.shape[0]

    sum_ref[...] += dot(rows_ref[...], basis_ref[...])


def rotate(before, end, blocks, basis, first, steps):
    flat = [pair for block in blocks for pair in block]
    size, ka = flat[0][0].shape[0], basis.shape[1]
    rows = size * len(blocks)
    specs = []
    for block in blocks:
        for which, (_, skip) in enumerate(block):
            used = lambda e, which=which, n=len(block): 1 if n == 1 else jnp.where(e[0] == 1, 1 - which, which)
            specs.append(
                pl.BlockSpec((size, DEEP), lambda k, e, used=used, skip=skip: (0, (k + skip) * used(e)))
            )
    whole = pl.BlockSpec((rows, ka), lambda k, e: (0, 0))
    arrays = [a for a, _ in flat] + [basis] + before
    return pl.pallas_call(
        lambda *refs: rotate_kernel([len(block) for block in blocks], *refs),
        out_shape=jax.ShapeDtypeStruct((rows, ka), F32),
        grid_spec=pltpu.PrefetchScalarGridSpec(
            num_scalar_prefetch=1,
            grid=(steps,),
            in_specs=specs
            + [pl.BlockSpec((DEEP, ka), lambda k, e: (first + k, 0))]
            + [pl.BlockSpec(a.shape, lambda k, e: (0, 0)) for a in before],
            out_specs=whole,
            scratch_shapes=[pltpu.VMEM((rows, DEEP), BF16)],
        ),
        compiler_params=pltpu.CompilerParams(vmem_limit_bytes=VMEM),
        cost_estimate=pl.CostEstimate(
            flops=rows * ka, bytes_accessed=4 * rows * ka, transcendentals=0
        ),
        name="rotate",
    )(end, *arrays)


def swap_narrow(a):
    return lax.ppermute(a, "narrow", [(0, 1), (1, 0)])


def general(inputs, deltas, basis_in, basis_out):
    partial_in = dot(lax.all_gather(inputs, "wide", axis=0, tiled=True), basis_in)
    rotated_out = lax.psum(dot(deltas, basis_out), "wide").astype(BF16)
    order, zero = jnp.arange(EX, dtype=jnp.int32), jnp.zeros((1,), jnp.int32)
    return fit(order, zero, [(partial_in, swap_narrow(partial_in))], [[rotated_out]], zero)


def pairs(step, where=lambda z: True):
    out = []
    for z in range(LINE):
        for x in range(PAIR):
            if where(z):
                tz, tx = step(z, x)
                out.append((z * PAIR + x, tz * PAIR + tx))
    return out


def corner(z):
    return z in (0, LINE - 1)


def middle(z):
    return not corner(z)


ENDS = pairs(lambda z, x: (z ^ 1, x))
TO_ENDS = pairs(lambda z, x: (z ^ 1, x), middle)
FROM_ENDS = pairs(lambda z, x: (z ^ 1, x), corner)
MIDDLE = pairs(lambda z, x: (3 - z, x), middle)
ACROSS = pairs(lambda z, x: (z, 1 - x))
ACROSS_ENDS = pairs(lambda z, x: (z, 1 - x), corner)
ACROSS_MIDDLE = pairs(lambda z, x: (z, 1 - x), middle)


def send(a, perm):
    return lax.ppermute(a, "wide", perm)


def scheduled(inputs, deltas, basis_in, basis_out):
    w = lax.axis_index("wide")
    z, x = w // PAIR, w % PAIR
    at_end = (z == 0) | (z == LINE - 1)
    end = at_end.astype(jnp.int32).reshape(1)
    half = (z >= 2).astype(jnp.int32)
    steps = inputs.shape[1] // DEEP
    cuts = [0, 5 * steps // 14, 9 * steps // 14, steps]
    part = basis_out.shape[1] // 4
    got = {"own": inputs}

    def fence(*names):
        got.update(zip(names, lax.optimization_barrier(tuple(got[n] for n in names))))

    def pick(a, b):
        return jnp.where(at_end, got[a], got[b])

    def columns(a, h):
        return lax.dynamic_slice_in_dim(a, h * 2 * part, 2 * part, 1)

    def turn(before, blocks, first, count):
        return rotate(before, end, [[(got[n], first) for n in block] for block in blocks], basis_in, first, count)

    flip = jnp.where(z >= 2, 3, 0)
    line = lambda a, b: jnp.where(at_end, a, b) ^ flip
    mine, other = (lambda a, b: line(a, b) * PAIR + x), (lambda a, b: line(a, b) * PAIR + 1 - x)
    order = [mine(0, 1), mine(1, 0), other(0, 1), mine(2, 2), other(1, 2), mine(3, 3), other(2, 3), other(3, 0)]
    got["order"] = jnp.stack(order).astype(jnp.int32)
    got["places"] = jnp.stack([half, 1 - half])

    got["x1"] = send(got["own"], ACROSS)
    got["a1"] = send(got["own"], ENDS)
    got["m1"] = send(got["own"], MIDDLE)
    got["out"] = dot(deltas, jnp.concatenate([columns(basis_out, 1 - half), columns(basis_out, half)], axis=1))
    got["r1"] = send(got["out"].astype(BF16), FROM_ENDS)
    fence("x1", "a1", "m1", "out", "order", "places")
    some = steps // 2
    got["x2"] = send(got["a1"], ACROSS_ENDS)
    got["x2", "m"] = send(got["m1"], ACROSS_MIDDLE)
    got["a2"] = send(got["m1"], TO_ENDS)
    got["m2"] = send(got["a1"], MIDDLE)
    blocks = [["own"], ["a1"], ["x1"]]
    got["A"] = turn([], blocks, 0, some)
    cut = 2 * part
    fence("r1", "out", "A")
    got["give"] = (got["out"][:, :cut] + got["r1"][:, :cut].astype(F32)).astype(BF16)
    fence("x1", "x2", "a2", "m2", "out", "r1", "give", "A")
    got["x3"] = send(got["a2"], ACROSS_ENDS)
    got["m3"] = send(got["give"], MIDDLE)
    got["a3"] = send(got["m2"], TO_ENDS)
    got["e"] = send(got["x1"], FROM_ENDS)
    fence(("x2", "m"), "m2", "out", "r1")
    got["x3m", 0] = send(got["m2"][:, : cuts[1] * DEEP], ACROSS_MIDDLE)
    got["keep"] = got["out"][:, cut:] + got["r1"][:, cut:].astype(F32)
    fence("keep", ("x2", "m"))
    more = [["a2", "m1"], ["x2", ("x2", "m")]]
    got["B"] = turn([], more, 0, some)
    fence("m3", ("x3m", 0), "keep", "m2", "B")
    got["keep"] += got["m3"].astype(F32)
    got["x5"] = send(got["keep"].astype(BF16), ACROSS_MIDDLE)
    got["x3m", 1] = send(got["m2"][:, cuts[1] * DEEP :], ACROSS_MIDDLE)
    got["A"] = turn([got["A"], got["B"]], blocks + more, some, steps - some)
    fence("x3", "A")
    fence("a3", "A")

    def x4(piece):
        got["x4", piece] = send(got["a3"][:, cuts[piece] * DEEP : cuts[piece + 1] * DEEP], ACROSS_ENDS)

    def last(piece):
        first, until, side = cuts[piece], cuts[piece + 1], int(piece > 0)
        blocks = [
            [(got["a3"], first), (got["m2"], first)],
            [(got["x3"], first), (got["x3m", side], first - side * cuts[1])],
            [(got["x4", piece], 0), (got["e"], first)],
        ]
        got["D"] = rotate([got["D"]] if piece else [], end, blocks, basis_in, first, until - first)

    x4(0)
    fence("x5", "e", "keep", "A")
    got["sum"] = (got["keep"] + got["x5"].astype(F32)).astype(BF16)
    got["m4"] = send(got["sum"], MIDDLE)
    got["n1"] = send(got["sum"], TO_ENDS)
    fence(("x4", 0), "a3", "A", "sum")
    x4(1)
    last(0)
    fence(("x4", 1), ("x3m", 1), "m4", "n1", "sum", "a3", "A", "D")
    x4(2)
    got["n2"] = send(got["m4"], TO_ENDS)
    got["A2"] = swap_narrow(got["A"])
    got["R"] = pick("n1", "sum")
    last(1)
    fence(("x4", 2), "A", "A2", "R", "D")
    last(2)
    fence("n2", "m4", "R", "A", "A2", "D")
    got["D2"] = swap_narrow(got["D"])
    got["A"] = (got["A"] + got["A2"]).astype(BF16)

    pieces, places = [[got["R"]], [got["n2"], got["m4"]]], got["places"]
    return fit(got["order"], end, [[got["A"]], [got["D"], got["D2"]]], pieces, places)


def solution(mesh):
    return jax.shard_map(
        scheduled if mesh.shape["wide"] == LINE * PAIR else general,
        mesh=mesh,
        in_specs=(
            P(("grp", "wide"), "narrow"),
            P("grp", "wide"),
            P(("grp", "narrow"), "wide"),
            P(("grp", "wide"), "narrow"),
        ),
        out_specs=P(("grp", "wide"), "narrow"),
        check_vma=False,
    )
```

```python
import jax
import jax.numpy as jnp
from jax import lax
from jax.experimental import pallas as pl
from jax.experimental.pallas import tpu as pltpu
from jax.sharding import PartitionSpec as P

EX = 2
LINE, PAIR = 4, 2
DEEP = 1024
VMEM = 22 << 20
BF16, F32 = jnp.bfloat16, jnp.float32


def dot(a, b):
    return jnp.dot(a, b, preferred_element_type=F32)


def fit_kernel(counts, choices, order_ref, end_ref, place_ref, *refs):
    sum_refs, refs = refs[: sum(counts)], refs[sum(counts) :]
    piece_refs, (fit_ref, out_ref, turned_ref, rot_ref) = refs[:-4], refs[-4:]
    rows, ks = out_ref.shape
    size, seq = rows // order_ref.shape[0], rows // EX

    @pl.when(pl.program_id(0) == 0)
    def _():
        at = 0
        for piece, choice in enumerate(choices):
            width = piece_refs[at].shape[1]
            there = pl.ds(pl.multiple_of(place_ref[piece] * width, width), width)
            if choice == 1:
                out_ref[:, there] = piece_refs[at][...]
            else:
                out_ref[:, there] = jnp.where(end_ref[0] == 1, piece_refs[at][...], piece_refs[at + 1][...])
            at += choice

    slot, first = 0, 0
    for count in counts:
        halves = sum_refs[first : first + count]
        first += count
        for at in range(0, halves[0].shape[0], size):
            here = pl.ds(at, size)
            there = pl.ds(pl.multiple_of(order_ref[slot] * size, size), size)
            rot_ref[there, :] = sum(ref[here, :] for ref in halves).astype(BF16)
            slot += 1
    turned_ref[...] = rot_ref[...].T
    step = min(256, ks)
    for at in range(0, ks, step):
        total = None
        for e in range(EX):
            here = pl.ds(e * seq, seq)
            grad = dot(turned_ref[:, here], out_ref[here, pl.ds(at, step)])
            total = grad * grad if total is None else total + grad * grad
        fit_ref[:, pl.ds(at, step)] = total * (1.0 / EX)


def fit(order, end, sums, pieces, places):
    rows = sum(halves[0].shape[0] for halves in sums)
    ka = sums[0][0].shape[1]
    ks = sum(piece[0].shape[1] for piece in pieces)
    tile = 256 if ka % 256 == 0 else ka
    flat = [a for halves in sums for a in halves]
    outs = [a for piece in pieces for a in piece]
    return pl.pallas_call(
        lambda *refs: fit_kernel([len(halves) for halves in sums], [len(piece) for piece in pieces], *refs),
        out_shape=jax.ShapeDtypeStruct((ka, ks), F32),
        grid_spec=pltpu.PrefetchScalarGridSpec(
            num_scalar_prefetch=3,
            grid=(ka // tile,),
            in_specs=[pl.BlockSpec((a.shape[0], tile), lambda i, *_: (0, i)) for a in flat]
            + [pl.BlockSpec(a.shape, lambda i, *_: (0, 0)) for a in outs],
            out_specs=pl.BlockSpec((tile, ks), lambda i, *_: (i, 0)),
            scratch_shapes=[
                pltpu.VMEM((rows, ks), BF16),
                pltpu.VMEM((tile, rows), BF16),
                pltpu.VMEM((rows, tile), BF16),
            ],
        ),
        compiler_params=pltpu.CompilerParams(vmem_limit_bytes=32 << 20),
        cost_estimate=pl.CostEstimate(
            flops=2 * rows * ka * ks, bytes_accessed=8 * rows * ka + 2 * rows * ks + 4 * ka * ks, transcendentals=0
        ),
        name="fit",
    )(order, end, places, *flat, *outs)


def rotate_kernel(choices, end_ref, *refs):
    blocks = refs[: sum(choices)]
    basis_ref, *before, sum_ref, rows_ref = refs[sum(choices) :]
    size = blocks[0].shape[0]
    at = 0
    for i, choice in enumerate(choices):
        here = pl.ds(i * size, size)
        if choice == 1:
            rows_ref[here, :] = blocks[at][...]
        else:
            rows_ref[here, :] = jnp.where(end_ref[0] == 1, blocks[at][...], blocks[at + 1][...])
        at += choice

    @pl.when(pl.program_id(0) == 0)
    def _():
        if not before:
            sum_ref[...] = jnp.zeros_like(sum_ref)
        at = 0
        for ref in before:
            sum_ref[pl.ds(at, ref.shape[0]), :] = ref[...]
            at += ref.shape[0]

    sum_ref[...] += dot(rows_ref[...], basis_ref[...])


def rotate(before, end, blocks, basis, first, steps):
    flat = [pair for block in blocks for pair in block]
    size, ka = flat[0][0].shape[0], basis.shape[1]
    rows = size * len(blocks)
    specs = []
    for block in blocks:
        for which, (_, skip) in enumerate(block):
            used = lambda e, which=which, n=len(block): 1 if n == 1 else jnp.where(e[0] == 1, 1 - which, which)
            specs.append(
                pl.BlockSpec((size, DEEP), lambda k, e, used=used, skip=skip: (0, (k + skip) * used(e)))
            )
    whole = pl.BlockSpec((rows, ka), lambda k, e: (0, 0))
    arrays = [a for a, _ in flat] + [basis] + before
    return pl.pallas_call(
        lambda *refs: rotate_kernel([len(block) for block in blocks], *refs),
        out_shape=jax.ShapeDtypeStruct((rows, ka), F32),
        grid_spec=pltpu.PrefetchScalarGridSpec(
            num_scalar_prefetch=1,
            grid=(steps,),
            in_specs=specs
            + [pl.BlockSpec((DEEP, ka), lambda k, e: (first + k, 0))]
            + [pl.BlockSpec(a.shape, lambda k, e: (0, 0)) for a in before],
            out_specs=whole,
            scratch_shapes=[pltpu.VMEM((rows, DEEP), BF16)],
        ),
        compiler_params=pltpu.CompilerParams(vmem_limit_bytes=VMEM),
        cost_estimate=pl.CostEstimate(
            flops=rows * ka, bytes_accessed=4 * rows * ka, transcendentals=0
        ),
        name="rotate",
    )(end, *arrays)


def swap_narrow(a):
    return lax.ppermute(a, "narrow", [(0, 1), (1, 0)])


def general(inputs, deltas, basis_in, basis_out):
    partial_in = dot(lax.all_gather(inputs, "wide", axis=0, tiled=True), basis_in)
    rotated_out = lax.psum(dot(deltas, basis_out), "wide").astype(BF16)
    order, zero = jnp.arange(EX, dtype=jnp.int32), jnp.zeros((1,), jnp.int32)
    return fit(order, zero, [(partial_in, swap_narrow(partial_in))], [[rotated_out]], zero)


def pairs(step, where=lambda z: True):
    out = []
    for z in range(LINE):
        for x in range(PAIR):
            if where(z):
                tz, tx = step(z, x)
                out.append((z * PAIR + x, tz * PAIR + tx))
    return out


def corner(z):
    return z in (0, LINE - 1)


def middle(z):
    return not corner(z)


ENDS = pairs(lambda z, x: (z ^ 1, x))
TO_ENDS = pairs(lambda z, x: (z ^ 1, x), middle)
FROM_ENDS = pairs(lambda z, x: (z ^ 1, x), corner)
MIDDLE = pairs(lambda z, x: (3 - z, x), middle)
ACROSS = pairs(lambda z, x: (z, 1 - x))
ACROSS_ENDS = pairs(lambda z, x: (z, 1 - x), corner)
ACROSS_MIDDLE = pairs(lambda z, x: (z, 1 - x), middle)


def send(a, perm):
    return lax.ppermute(a, "wide", perm)


def scheduled(inputs, deltas, basis_in, basis_out):
    w = lax.axis_index("wide")
    z, x = w // PAIR, w % PAIR
    at_end = (z == 0) | (z == LINE - 1)
    end = at_end.astype(jnp.int32).reshape(1)
    half = (z >= 2).astype(jnp.int32)
    steps = inputs.shape[1] // DEEP
    cuts = [0, 5 * steps // 14, 9 * steps // 14, 12 * steps // 14, steps]
    part = basis_out.shape[1] // 4
    got = {"own": inputs}

    def fence(*names):
        got.update(zip(names, lax.optimization_barrier(tuple(got[n] for n in names))))

    def pick(a, b):
        return jnp.where(at_end, got[a], got[b])

    def columns(a, h):
        return lax.dynamic_slice_in_dim(a, h * 2 * part, 2 * part, 1)

    def turn(before, blocks, first, count):
        return rotate(before, end, [[(got[n], first) for n in block] for block in blocks], basis_in, first, count)

    flip = jnp.where(z >= 2, 3, 0)
    line = lambda a, b: jnp.where(at_end, a, b) ^ flip
    mine, other = (lambda a, b: line(a, b) * PAIR + x), (lambda a, b: line(a, b) * PAIR + 1 - x)
    order = [mine(0, 1), mine(1, 0), other(0, 1), mine(2, 2), other(1, 2), mine(3, 3), other(2, 3), other(3, 0)]
    got["order"] = jnp.stack(order).astype(jnp.int32)
    got["places"] = jnp.stack([half, 1 - half])

    got["x1"] = send(got["own"], ACROSS)
    got["a1"] = send(got["own"], ENDS)
    got["m1"] = send(got["own"], MIDDLE)
    got["out"] = dot(deltas, jnp.concatenate([columns(basis_out, 1 - half), columns(basis_out, half)], axis=1))
    got["r1"] = send(got["out"].astype(BF16), FROM_ENDS)
    fence("x1", "a1", "m1", "out", "order", "places")
    some = steps // 2
    got["x2"] = send(got["a1"], ACROSS_ENDS)
    got["x2", "m"] = send(got["m1"], ACROSS_MIDDLE)
    got["a2"] = send(got["m1"], TO_ENDS)
    got["m2"] = send(got["a1"], MIDDLE)
    blocks = [["own"], ["a1"], ["x1"]]
    got["A"] = turn([], blocks, 0, some)
    cut = 2 * part
    fence("r1", "out", "A")
    got["give"] = (got["out"][:, :cut] + got["r1"][:, :cut].astype(F32)).astype(BF16)
    fence("x1", "x2", "a2", "m2", "out", "r1", "give", "A")
    got["x3"] = send(got["a2"], ACROSS_ENDS)
    got["m3"] = send(got["give"], MIDDLE)
    got["a3"] = send(got["m2"], TO_ENDS)
    got["e"] = send(got["x1"], FROM_ENDS)
    fence(("x2", "m"), "m2", "out", "r1")
    got["x3m", 0] = send(got["m2"][:, : cuts[1] * DEEP], ACROSS_MIDDLE)
    got["keep"] = got["out"][:, cut:] + got["r1"][:, cut:].astype(F32)
    fence("keep", ("x2", "m"))
    more = [["a2", "m1"], ["x2", ("x2", "m")]]
    got["B"] = turn([], more, 0, some)
    fence("m3", ("x3m", 0), "keep", "m2", "B")
    got["keep"] += got["m3"].astype(F32)
    got["x5"] = send(got["keep"].astype(BF16), ACROSS_MIDDLE)
    got["x3m", 1] = send(got["m2"][:, cuts[1] * DEEP :], ACROSS_MIDDLE)
    got["A"] = turn([got["A"], got["B"]], blocks + more, some, steps - some)
    fence("x3", "A")
    fence("a3", "A")

    def x4(piece):
        got["x4", piece] = send(got["a3"][:, cuts[piece] * DEEP : cuts[piece + 1] * DEEP], ACROSS_ENDS)

    def last(piece):
        first, until, side = cuts[piece], cuts[piece + 1], int(piece > 0)
        blocks = [
            [(got["a3"], first), (got["m2"], first)],
            [(got["x3"], first), (got["x3m", side], first - side * cuts[1])],
            [(got["x4", piece], 0), (got["e"], first)],
        ]
        got["D"] = rotate([got["D"]] if piece else [], end, blocks, basis_in, first, until - first)

    x4(0)
    fence("x5", "e", "keep", "A")
    got["sum"] = (got["keep"] + got["x5"].astype(F32)).astype(BF16)
    got["m4"] = send(got["sum"], MIDDLE)
    got["n1"] = send(got["sum"], TO_ENDS)
    fence(("x4", 0), "a3", "A", "sum")
    x4(1)
    last(0)
    fence(("x4", 1), ("x3m", 1), "m4", "n1", "sum", "a3", "A", "D")
    x4(2)
    got["n2"] = send(got["m4"], TO_ENDS)
    got["A2"] = swap_narrow(got["A"])
    got["R"] = pick("n1", "sum")
    last(1)
    fence(("x4", 2), "A", "A2", "R", "D", "a3")
    x4(3)
    last(2)
    fence(("x4", 3), "A", "A2", "R", "D")
    last(3)
    fence("n2", "m4", "R", "A", "A2", "D")
    got["D2"] = swap_narrow(got["D"])
    got["A"] = (got["A"] + got["A2"]).astype(BF16)

    pieces, places = [[got["R"]], [got["n2"], got["m4"]]], got["places"]
    return fit(got["order"], end, [[got["A"]], [got["D"], got["D2"]]], pieces, places)


def solution(mesh):
    return jax.shard_map(
        scheduled if mesh.shape["wide"] == LINE * PAIR else general,
        mesh=mesh,
        in_specs=(
            P(("grp", "wide"), "narrow"),
            P("grp", "wide"),
            P(("grp", "narrow"), "wide"),
            P(("grp", "wide"), "narrow"),
        ),
        out_specs=P(("grp", "wide"), "narrow"),
        check_vma=False,
    )
```

```python
import jax
import jax.numpy as jnp
from jax import lax
from jax.experimental import pallas as pl
from jax.experimental.pallas import tpu as pltpu
from jax.sharding import PartitionSpec as P

EX = 2
LINE, PAIR = 4, 2
DEEP = 512
VMEM = 16 << 20
BF16, F32 = jnp.bfloat16, jnp.float32


def dot(a, b):
    return jnp.dot(a, b, preferred_element_type=F32)


def fit_kernel(counts, choices, order_ref, end_ref, place_ref, *refs):
    sum_refs, refs = refs[: sum(counts)], refs[sum(counts) :]
    piece_refs, (fit_ref, out_ref, turned_ref, rot_ref) = refs[:-4], refs[-4:]
    rows, ks = out_ref.shape
    size, seq = rows // order_ref.shape[0], rows // EX

    @pl.when(pl.program_id(0) == 0)
    def _():
        at = 0
        for piece, choice in enumerate(choices):
            width = piece_refs[at].shape[1]
            there = pl.ds(pl.multiple_of(place_ref[piece] * width, width), width)
            if choice == 1:
                out_ref[:, there] = piece_refs[at][...]
            else:
                out_ref[:, there] = jnp.where(end_ref[0] == 1, piece_refs[at][...], piece_refs[at + 1][...])
            at += choice

    slot, first = 0, 0
    for count in counts:
        halves = sum_refs[first : first + count]
        first += count
        for at in range(0, halves[0].shape[0], size):
            here = pl.ds(at, size)
            there = pl.ds(pl.multiple_of(order_ref[slot] * size, size), size)
            rot_ref[there, :] = sum(ref[here, :] for ref in halves).astype(BF16)
            slot += 1
    turned_ref[...] = rot_ref[...].T
    step = min(256, ks)
    for at in range(0, ks, step):
        total = None
        for e in range(EX):
            here = pl.ds(e * seq, seq)
            grad = dot(turned_ref[:, here], out_ref[here, pl.ds(at, step)])
            total = grad * grad if total is None else total + grad * grad
        fit_ref[:, pl.ds(at, step)] = total * (1.0 / EX)


def fit(order, end, sums, pieces, places):
    rows = sum(halves[0].shape[0] for halves in sums)
    ka = sums[0][0].shape[1]
    ks = sum(piece[0].shape[1] for piece in pieces)
    tile = 256 if ka % 256 == 0 else ka
    flat = [a for halves in sums for a in halves]
    outs = [a for piece in pieces for a in piece]
    return pl.pallas_call(
        lambda *refs: fit_kernel([len(halves) for halves in sums], [len(piece) for piece in pieces], *refs),
        out_shape=jax.ShapeDtypeStruct((ka, ks), F32),
        grid_spec=pltpu.PrefetchScalarGridSpec(
            num_scalar_prefetch=3,
            grid=(ka // tile,),
            in_specs=[pl.BlockSpec((a.shape[0], tile), lambda i, *_: (0, i)) for a in flat]
            + [pl.BlockSpec(a.shape, lambda i, *_: (0, 0)) for a in outs],
            out_specs=pl.BlockSpec((tile, ks), lambda i, *_: (i, 0)),
            scratch_shapes=[
                pltpu.VMEM((rows, ks), BF16),
                pltpu.VMEM((tile, rows), BF16),
                pltpu.VMEM((rows, tile), BF16),
            ],
        ),
        compiler_params=pltpu.CompilerParams(vmem_limit_bytes=32 << 20),
        cost_estimate=pl.CostEstimate(
            flops=2 * rows * ka * ks, bytes_accessed=8 * rows * ka + 2 * rows * ks + 4 * ka * ks, transcendentals=0
        ),
        name="fit",
    )(order, end, places, *flat, *outs)


def rotate_kernel(choices, end_ref, *refs):
    blocks = refs[: sum(choices)]
    basis_ref, *before, sum_ref, rows_ref = refs[sum(choices) :]
    size = blocks[0].shape[0]
    at = 0
    for i, choice in enumerate(choices):
        here = pl.ds(i * size, size)
        if choice == 1:
            rows_ref[here, :] = blocks[at][...]
        else:
            rows_ref[here, :] = jnp.where(end_ref[0] == 1, blocks[at][...], blocks[at + 1][...])
        at += choice

    @pl.when(pl.program_id(0) == 0)
    def _():
        if not before:
            sum_ref[...] = jnp.zeros_like(sum_ref)
        at = 0
        for ref in before:
            sum_ref[pl.ds(at, ref.shape[0]), :] = ref[...]
            at += ref.shape[0]

    sum_ref[...] += dot(rows_ref[...], basis_ref[...])


def rotate(before, end, blocks, basis, first, steps):
    flat = [pair for block in blocks for pair in block]
    size, ka = flat[0][0].shape[0], basis.shape[1]
    rows = size * len(blocks)
    specs = []
    for block in blocks:
        for which, (_, skip) in enumerate(block):
            used = lambda e, which=which, n=len(block): 1 if n == 1 else jnp.where(e[0] == 1, 1 - which, which)
            specs.append(
                pl.BlockSpec((size, DEEP), lambda k, e, used=used, skip=skip: (0, (k + skip) * used(e)))
            )
    whole = pl.BlockSpec((rows, ka), lambda k, e: (0, 0))
    arrays = [a for a, _ in flat] + [basis] + before
    return pl.pallas_call(
        lambda *refs: rotate_kernel([len(block) for block in blocks], *refs),
        out_shape=jax.ShapeDtypeStruct((rows, ka), F32),
        grid_spec=pltpu.PrefetchScalarGridSpec(
            num_scalar_prefetch=1,
            grid=(steps,),
            in_specs=specs
            + [pl.BlockSpec((DEEP, ka), lambda k, e: (first + k, 0))]
            + [pl.BlockSpec(a.shape, lambda k, e: (0, 0)) for a in before],
            out_specs=whole,
            scratch_shapes=[pltpu.VMEM((rows, DEEP), BF16)],
        ),
        compiler_params=pltpu.CompilerParams(vmem_limit_bytes=VMEM),
        cost_estimate=pl.CostEstimate(
            flops=rows * ka, bytes_accessed=4 * rows * ka, transcendentals=0
        ),
        name="rotate",
    )(end, *arrays)


def swap_narrow(a):
    return lax.ppermute(a, "narrow", [(0, 1), (1, 0)])


def general(inputs, deltas, basis_in, basis_out):
    partial_in = dot(lax.all_gather(inputs, "wide", axis=0, tiled=True), basis_in)
    rotated_out = lax.psum(dot(deltas, basis_out), "wide").astype(BF16)
    order, zero = jnp.arange(EX, dtype=jnp.int32), jnp.zeros((1,), jnp.int32)
    return fit(order, zero, [(partial_in, swap_narrow(partial_in))], [[rotated_out]], zero)


def pairs(step, where=lambda z: True):
    out = []
    for z in range(LINE):
        for x in range(PAIR):
            if where(z):
                tz, tx = step(z, x)
                out.append((z * PAIR + x, tz * PAIR + tx))
    return out


def corner(z):
    return z in (0, LINE - 1)


def middle(z):
    return not corner(z)


ENDS = pairs(lambda z, x: (z ^ 1, x))
TO_ENDS = pairs(lambda z, x: (z ^ 1, x), middle)
FROM_ENDS = pairs(lambda z, x: (z ^ 1, x), corner)
MIDDLE = pairs(lambda z, x: (3 - z, x), middle)
ACROSS = pairs(lambda z, x: (z, 1 - x))
ACROSS_ENDS = pairs(lambda z, x: (z, 1 - x), corner)
ACROSS_MIDDLE = pairs(lambda z, x: (z, 1 - x), middle)


def send(a, perm):
    return lax.ppermute(a, "wide", perm)


def scheduled(inputs, deltas, basis_in, basis_out):
    w = lax.axis_index("wide")
    z, x = w // PAIR, w % PAIR
    at_end = (z == 0) | (z == LINE - 1)
    end = at_end.astype(jnp.int32).reshape(1)
    half = (z >= 2).astype(jnp.int32)
    steps = inputs.shape[1] // DEEP
    cuts = [0, 5 * steps // 14, 9 * steps // 14, 12 * steps // 14, steps]
    part = basis_out.shape[1] // 4
    got = {"own": inputs}

    def fence(*names):
        got.update(zip(names, lax.optimization_barrier(tuple(got[n] for n in names))))

    def pick(a, b):
        return jnp.where(at_end, got[a], got[b])

    def columns(a, h):
        return lax.dynamic_slice_in_dim(a, h * 2 * part, 2 * part, 1)

    def turn(before, blocks, first, count):
        return rotate(before, end, [[(got[n], first) for n in block] for block in blocks], basis_in, first, count)

    flip = jnp.where(z >= 2, 3, 0)
    line = lambda a, b: jnp.where(at_end, a, b) ^ flip
    mine, other = (lambda a, b: line(a, b) * PAIR + x), (lambda a, b: line(a, b) * PAIR + 1 - x)
    order = [mine(0, 1), mine(1, 0), other(0, 1), mine(2, 2), other(1, 2), mine(3, 3), other(2, 3), other(3, 0)]
    got["order"] = jnp.stack(order).astype(jnp.int32)
    got["places"] = jnp.stack([half, 1 - half])

    got["x1"] = send(got["own"], ACROSS)
    got["a1"] = send(got["own"], ENDS)
    got["m1"] = send(got["own"], MIDDLE)
    got["out"] = dot(deltas, jnp.concatenate([columns(basis_out, 1 - half), columns(basis_out, half)], axis=1))
    got["r1"] = send(got["out"].astype(BF16), FROM_ENDS)
    fence("x1", "a1", "m1", "out", "order", "places")
    some = steps // 2
    got["x2"] = send(got["a1"], ACROSS_ENDS)
    got["x2", "m"] = send(got["m1"], ACROSS_MIDDLE)
    got["a2"] = send(got["m1"], TO_ENDS)
    got["m2"] = send(got["a1"], MIDDLE)
    blocks = [["own"], ["a1"], ["x1"]]
    got["A"] = turn([], blocks, 0, some)
    cut = 2 * part
    fence("r1", "out", "A")
    got["give"] = (got["out"][:, :cut] + got["r1"][:, :cut].astype(F32)).astype(BF16)
    fence("x1", "x2", "a2", "m2", "out", "r1", "give", "A")
    got["x3"] = send(got["a2"], ACROSS_ENDS)
    got["m3"] = send(got["give"], MIDDLE)
    got["a3"] = send(got["m2"], TO_ENDS)
    got["e"] = send(got["x1"], FROM_ENDS)
    fence(("x2", "m"), "m2", "out", "r1")
    got["x3m", 0] = send(got["m2"][:, : cuts[1] * DEEP], ACROSS_MIDDLE)
    got["keep"] = got["out"][:, cut:] + got["r1"][:, cut:].astype(F32)
    fence("keep", ("x2", "m"))
    more = [["a2", "m1"], ["x2", ("x2", "m")]]
    got["B"] = turn([], more, 0, some)
    fence("m3", ("x3m", 0), "keep", "m2", "B")
    got["keep"] += got["m3"].astype(F32)
    got["x5"] = send(got["keep"].astype(BF16), ACROSS_MIDDLE)
    got["x3m", 1] = send(got["m2"][:, cuts[1] * DEEP :], ACROSS_MIDDLE)
    got["A"] = turn([got["A"], got["B"]], blocks + more, some, steps - some)
    fence("x3", "A")
    fence("a3", "A")

    def x4(piece):
        got["x4", piece] = send(got["a3"][:, cuts[piece] * DEEP : cuts[piece + 1] * DEEP], ACROSS_ENDS)

    def last(piece):
        first, until, side = cuts[piece], cuts[piece + 1], int(piece > 0)
        blocks = [
            [(got["a3"], first), (got["m2"], first)],
            [(got["x3"], first), (got["x3m", side], first - side * cuts[1])],
            [(got["x4", piece], 0), (got["e"], first)],
        ]
        got["D"] = rotate([got["D"]] if piece else [], end, blocks, basis_in, first, until - first)

    x4(0)
    fence("x5", "e", "keep", "A")
    got["sum"] = (got["keep"] + got["x5"].astype(F32)).astype(BF16)
    got["m4"] = send(got["sum"], MIDDLE)
    got["n1"] = send(got["sum"], TO_ENDS)
    fence(("x4", 0), "a3", "A", "sum")
    x4(1)
    last(0)
    fence(("x4", 1), ("x3m", 1), "m4", "n1", "sum", "a3", "A", "D")
    x4(2)
    got["n2"] = send(got["m4"], TO_ENDS)
    got["A2"] = swap_narrow(got["A"])
    got["R"] = pick("n1", "sum")
    last(1)
    fence(("x4", 2), "A", "A2", "R", "D", "a3")
    x4(3)
    last(2)
    fence(("x4", 3), "A", "A2", "R", "D")
    last(3)
    fence("n2", "m4", "R", "A", "A2", "D")
    got["D2"] = swap_narrow(got["D"])
    got["A"] = (got["A"] + got["A2"]).astype(BF16)

    pieces, places = [[got["R"]], [got["n2"], got["m4"]]], got["places"]
    return fit(got["order"], end, [[got["A"]], [got["D"], got["D2"]]], pieces, places)


def solution(mesh):
    return jax.shard_map(
        scheduled if mesh.shape["wide"] == LINE * PAIR else general,
        mesh=mesh,
        in_specs=(
            P(("grp", "wide"), "narrow"),
            P("grp", "wide"),
            P(("grp", "narrow"), "wide"),
            P(("grp", "wide"), "narrow"),
        ),
        out_specs=P(("grp", "wide"), "narrow"),
        check_vma=False,
    )
```

```python
import jax
import jax.numpy as jnp
from jax import lax
from jax.experimental import pallas as pl
from jax.experimental.pallas import tpu as pltpu
from jax.sharding import PartitionSpec as P

EX = 2
LINE, PAIR = 4, 2
DEEP = 2048
VMEM = 32 << 20
BF16, F32 = jnp.bfloat16, jnp.float32


def dot(a, b):
    return jnp.dot(a, b, preferred_element_type=F32)


def fit_kernel(counts, choices, order_ref, end_ref, place_ref, *refs):
    sum_refs, refs = refs[: sum(counts)], refs[sum(counts) :]
    piece_refs, (fit_ref, out_ref, turned_ref, rot_ref) = refs[:-4], refs[-4:]
    rows, ks = out_ref.shape
    size, seq = rows // order_ref.shape[0], rows // EX

    @pl.when(pl.program_id(0) == 0)
    def _():
        at = 0
        for piece, choice in enumerate(choices):
            width = piece_refs[at].shape[1]
            there = pl.ds(pl.multiple_of(place_ref[piece] * width, width), width)
            if choice == 1:
                out_ref[:, there] = piece_refs[at][...]
            else:
                out_ref[:, there] = jnp.where(end_ref[0] == 1, piece_refs[at][...], piece_refs[at + 1][...])
            at += choice

    slot, first = 0, 0
    for count in counts:
        halves = sum_refs[first : first + count]
        first += count
        for at in range(0, halves[0].shape[0], size):
            here = pl.ds(at, size)
            there = pl.ds(pl.multiple_of(order_ref[slot] * size, size), size)
            rot_ref[there, :] = sum(ref[here, :] for ref in halves).astype(BF16)
            slot += 1
    turned_ref[...] = rot_ref[...].T
    step = min(256, ks)
    for at in range(0, ks, step):
        total = None
        for e in range(EX):
            here = pl.ds(e * seq, seq)
            grad = dot(turned_ref[:, here], out_ref[here, pl.ds(at, step)])
            total = grad * grad if total is None else total + grad * grad
        fit_ref[:, pl.ds(at, step)] = total * (1.0 / EX)


def fit(order, end, sums, pieces, places):
    rows = sum(halves[0].shape[0] for halves in sums)
    ka = sums[0][0].shape[1]
    ks = sum(piece[0].shape[1] for piece in pieces)
    tile = 256 if ka % 256 == 0 else ka
    flat = [a for halves in sums for a in halves]
    outs = [a for piece in pieces for a in piece]
    return pl.pallas_call(
        lambda *refs: fit_kernel([len(halves) for halves in sums], [len(piece) for piece in pieces], *refs),
        out_shape=jax.ShapeDtypeStruct((ka, ks), F32),
        grid_spec=pltpu.PrefetchScalarGridSpec(
            num_scalar_prefetch=3,
            grid=(ka // tile,),
            in_specs=[pl.BlockSpec((a.shape[0], tile), lambda i, *_: (0, i)) for a in flat]
            + [pl.BlockSpec(a.shape, lambda i, *_: (0, 0)) for a in outs],
            out_specs=pl.BlockSpec((tile, ks), lambda i, *_: (i, 0)),
            scratch_shapes=[
                pltpu.VMEM((rows, ks), BF16),
                pltpu.VMEM((tile, rows), BF16),
                pltpu.VMEM((rows, tile), BF16),
            ],
        ),
        compiler_params=pltpu.CompilerParams(vmem_limit_bytes=32 << 20),
        cost_estimate=pl.CostEstimate(
            flops=2 * rows * ka * ks, bytes_accessed=8 * rows * ka + 2 * rows * ks + 4 * ka * ks, transcendentals=0
        ),
        name="fit",
    )(order, end, places, *flat, *outs)


def rotate_kernel(choices, end_ref, *refs):
    blocks = refs[: sum(choices)]
    basis_ref, *before, sum_ref, rows_ref = refs[sum(choices) :]
    size = blocks[0].shape[0]
    at = 0
    for i, choice in enumerate(choices):
        here = pl.ds(i * size, size)
        if choice == 1:
            rows_ref[here, :] = blocks[at][...]
        else:
            rows_ref[here, :] = jnp.where(end_ref[0] == 1, blocks[at][...], blocks[at + 1][...])
        at += choice

    @pl.when(pl.program_id(0) == 0)
    def _():
        if not before:
            sum_ref[...] = jnp.zeros_like(sum_ref)
        at = 0
        for ref in before:
            sum_ref[pl.ds(at, ref.shape[0]), :] = ref[...]
            at += ref.shape[0]

    sum_ref[...] += dot(rows_ref[...], basis_ref[...])


def rotate(before, end, blocks, basis, first, steps):
    flat = [pair for block in blocks for pair in block]
    size, ka = flat[0][0].shape[0], basis.shape[1]
    rows = size * len(blocks)
    specs = []
    for block in blocks:
        for which, (_, skip) in enumerate(block):
            used = lambda e, which=which, n=len(block): 1 if n == 1 else jnp.where(e[0] == 1, 1 - which, which)
            specs.append(
                pl.BlockSpec((size, DEEP), lambda k, e, used=used, skip=skip: (0, (k + skip) * used(e)))
            )
    whole = pl.BlockSpec((rows, ka), lambda k, e: (0, 0))
    arrays = [a for a, _ in flat] + [basis] + before
    return pl.pallas_call(
        lambda *refs: rotate_kernel([len(block) for block in blocks], *refs),
        out_shape=jax.ShapeDtypeStruct((rows, ka), F32),
        grid_spec=pltpu.PrefetchScalarGridSpec(
            num_scalar_prefetch=1,
            grid=(steps,),
            in_specs=specs
            + [pl.BlockSpec((DEEP, ka), lambda k, e: (first + k, 0))]
            + [pl.BlockSpec(a.shape, lambda k, e: (0, 0)) for a in before],
            out_specs=whole,
            scratch_shapes=[pltpu.VMEM((rows, DEEP), BF16)],
        ),
        compiler_params=pltpu.CompilerParams(vmem_limit_bytes=VMEM),
        cost_estimate=pl.CostEstimate(
            flops=rows * ka, bytes_accessed=4 * rows * ka, transcendentals=0
        ),
        name="rotate",
    )(end, *arrays)


def swap_narrow(a):
    return lax.ppermute(a, "narrow", [(0, 1), (1, 0)])


def general(inputs, deltas, basis_in, basis_out):
    partial_in = dot(lax.all_gather(inputs, "wide", axis=0, tiled=True), basis_in)
    rotated_out = lax.psum(dot(deltas, basis_out), "wide").astype(BF16)
    order, zero = jnp.arange(EX, dtype=jnp.int32), jnp.zeros((1,), jnp.int32)
    return fit(order, zero, [(partial_in, swap_narrow(partial_in))], [[rotated_out]], zero)


def pairs(step, where=lambda z: True):
    out = []
    for z in range(LINE):
        for x in range(PAIR):
            if where(z):
                tz, tx = step(z, x)
                out.append((z * PAIR + x, tz * PAIR + tx))
    return out


def corner(z):
    return z in (0, LINE - 1)


def middle(z):
    return not corner(z)


ENDS = pairs(lambda z, x: (z ^ 1, x))
TO_ENDS = pairs(lambda z, x: (z ^ 1, x), middle)
FROM_ENDS = pairs(lambda z, x: (z ^ 1, x), corner)
MIDDLE = pairs(lambda z, x: (3 - z, x), middle)
ACROSS = pairs(lambda z, x: (z, 1 - x))
ACROSS_ENDS = pairs(lambda z, x: (z, 1 - x), corner)
ACROSS_MIDDLE = pairs(lambda z, x: (z, 1 - x), middle)


def send(a, perm):
    return lax.ppermute(a, "wide", perm)


def scheduled(inputs, deltas, basis_in, basis_out):
    w = lax.axis_index("wide")
    z, x = w // PAIR, w % PAIR
    at_end = (z == 0) | (z == LINE - 1)
    end = at_end.astype(jnp.int32).reshape(1)
    half = (z >= 2).astype(jnp.int32)
    steps = inputs.shape[1] // DEEP
    cuts = [0, 5 * steps // 14, 9 * steps // 14, 12 * steps // 14, steps]
    part = basis_out.shape[1] // 4
    got = {"own": inputs}

    def fence(*names):
        got.update(zip(names, lax.optimization_barrier(tuple(got[n] for n in names))))

    def pick(a, b):
        return jnp.where(at_end, got[a], got[b])

    def columns(a, h):
        return lax.dynamic_slice_in_dim(a, h * 2 * part, 2 * part, 1)

    def turn(before, blocks, first, count):
        return rotate(before, end, [[(got[n], first) for n in block] for block in blocks], basis_in, first, count)

    flip = jnp.where(z >= 2, 3, 0)
    line = lambda a, b: jnp.where(at_end, a, b) ^ flip
    mine, other = (lambda a, b: line(a, b) * PAIR + x), (lambda a, b: line(a, b) * PAIR + 1 - x)
    order = [mine(0, 1), mine(1, 0), other(0, 1), mine(2, 2), other(1, 2), mine(3, 3), other(2, 3), other(3, 0)]
    got["order"] = jnp.stack(order).astype(jnp.int32)
    got["places"] = jnp.stack([half, 1 - half])

    got["x1"] = send(got["own"], ACROSS)
    got["a1"] = send(got["own"], ENDS)
    got["m1"] = send(got["own"], MIDDLE)
    got["out"] = dot(deltas, jnp.concatenate([columns(basis_out, 1 - half), columns(basis_out, half)], axis=1))
    got["r1"] = send(got["out"].astype(BF16), FROM_ENDS)
    fence("x1", "a1", "m1", "out", "order", "places")
    some = steps // 2
    got["x2"] = send(got["a1"], ACROSS_ENDS)
    got["x2", "m"] = send(got["m1"], ACROSS_MIDDLE)
    got["a2"] = send(got["m1"], TO_ENDS)
    got["m2"] = send(got["a1"], MIDDLE)
    blocks = [["own"], ["a1"], ["x1"]]
    got["A"] = turn([], blocks, 0, some)
    cut = 2 * part
    fence("r1", "out", "A")
    got["give"] = (got["out"][:, :cut] + got["r1"][:, :cut].astype(F32)).astype(BF16)
    fence("x1", "x2", "a2", "m2", "out", "r1", "give", "A")
    got["x3"] = send(got["a2"], ACROSS_ENDS)
    got["m3"] = send(got["give"], MIDDLE)
    got["a3"] = send(got["m2"], TO_ENDS)
    got["e"] = send(got["x1"], FROM_ENDS)
    fence(("x2", "m"), "m2", "out", "r1")
    got["x3m", 0] = send(got["m2"][:, : cuts[1] * DEEP], ACROSS_MIDDLE)
    got["keep"] = got["out"][:, cut:] + got["r1"][:, cut:].astype(F32)
    fence("keep", ("x2", "m"))
    more = [["a2", "m1"], ["x2", ("x2", "m")]]
    got["B"] = turn([], more, 0, some)
    fence("m3", ("x3m", 0), "keep", "m2", "B")
    got["keep"] += got["m3"].astype(F32)
    got["x5"] = send(got["keep"].astype(BF16), ACROSS_MIDDLE)
    got["x3m", 1] = send(got["m2"][:, cuts[1] * DEEP :], ACROSS_MIDDLE)
    got["A"] = turn([got["A"], got["B"]], blocks + more, some, steps - some)
    fence("x3", "A")
    fence("a3", "A")

    def x4(piece):
        got["x4", piece] = send(got["a3"][:, cuts[piece] * DEEP : cuts[piece + 1] * DEEP], ACROSS_ENDS)

    def last(piece):
        first, until, side = cuts[piece], cuts[piece + 1], int(piece > 0)
        blocks = [
            [(got["a3"], first), (got["m2"], first)],
            [(got["x3"], first), (got["x3m", side], first - side * cuts[1])],
            [(got["x4", piece], 0), (got["e"], first)],
        ]
        got["D"] = rotate([got["D"]] if piece else [], end, blocks, basis_in, first, until - first)

    x4(0)
    fence("x5", "e", "keep", "A")
    got["sum"] = (got["keep"] + got["x5"].astype(F32)).astype(BF16)
    got["m4"] = send(got["sum"], MIDDLE)
    got["n1"] = send(got["sum"], TO_ENDS)
    fence(("x4", 0), "a3", "A", "sum")
    x4(1)
    last(0)
    fence(("x4", 1), ("x3m", 1), "m4", "n1", "sum", "a3", "A", "D")
    x4(2)
    got["n2"] = send(got["m4"], TO_ENDS)
    got["A2"] = swap_narrow(got["A"])
    got["R"] = pick("n1", "sum")
    last(1)
    fence(("x4", 2), "A", "A2", "R", "D", "a3")
    x4(3)
    last(2)
    fence(("x4", 3), "A", "A2", "R", "D")
    last(3)
    fence("n2", "m4", "R", "A", "A2", "D")
    got["D2"] = swap_narrow(got["D"])
    got["A"] = (got["A"] + got["A2"]).astype(BF16)

    pieces, places = [[got["R"]], [got["n2"], got["m4"]]], got["places"]
    return fit(got["order"], end, [[got["A"]], [got["D"], got["D2"]]], pieces, places)


def solution(mesh):
    return jax.shard_map(
        scheduled if mesh.shape["wide"] == LINE * PAIR else general,
        mesh=mesh,
        in_specs=(
            P(("grp", "wide"), "narrow"),
            P("grp", "wide"),
            P(("grp", "narrow"), "wide"),
            P(("grp", "wide"), "narrow"),
        ),
        out_specs=P(("grp", "wide"), "narrow"),
        check_vma=False,
    )
```
